32 devices in a mesh: grp: 2 (over y), row: 8 (over z, core), col: 2 (over x).
Axes of the slice: x: 2, y: 2, z: 4, core: 2. Of those that a mesh axis runs over, the one named last changes fastest.
Arguments:
- sketch_base: int32 [2], P('grp'), parts along dimension 0, may hold values from 0 to 999999
- states: bfloat16 [4096, 8192], P(('grp', 'row'), 'col'), parts along dimension 0
Outputs:
- loadings: float32 [8192, 128], P(('col', 'row'), 'grp'), parts along dimension 1
- sketch_factor: float32 [128, 64], P('grp'), parts along dimension 0
The draws below stay inside these ranges and needn't reach their ends.
There are 2 independent parts, one for each index of `grp`. The reference program is written for one: setup_inputs(seed, part) draws one part's arguments, and reference() takes and returns one part's arrays. A program takes and returns all parts, laid end to end along the dimension named above; each array names one. Nothing has to cross between parts.
All inputs are finite; a program needn't handle non-finite values.
Results may differ from the reference program's by a relative error of at most 0.011.
Values may be sent and summed in bfloat16 or wider, within the bound.
No kernel may reach another device: no remote copies, remote signals or barrier semaphores. Data moves between devices by JAX's collectives and lax.ppermute only.
A program may use at most 64 MiB of HBM per device.

```python
import math
import jax
import jax.numpy as jnp
from jax import lax

D = 8192
RANK = 64
POWER = 4
ROWS_DEV = 256
ROWS = 2048
N_ROW = 8


def draw_states(key, part):
    key = jax.random.fold_in(key, 11)
    key_body = jax.random.fold_in(key, 0)
    key_rows = jax.random.fold_in(key, 1)
    key_cols = jax.random.fold_in(key, 2)
    key_left = jax.random.fold_in(key, 4)
    key_right = jax.random.fold_in(key, 5)
    key_spots = jax.random.fold_in(key, 6)
    count = 3 * RANK // 2
    levels = jnp.exp(-jnp.log(32.0) * jnp.arange(count, dtype=jnp.float32) / (RANK - 1))
    left = jax.random.normal(key_left, (ROWS, count), jnp.float32)
    right = jax.random.normal(key_right, (count, D), jnp.float32)
    spots = jax.random.randint(key_spots, (8,), 0, D)
    outlier = jnp.any(jnp.arange(D, dtype=jnp.int32)[None, :] == spots[:, None], axis=0)
    massive = jnp.where(outlier, 32.0, 1.0).astype(jnp.float32)[None, :]
    row_scale = jnp.exp(jax.random.uniform(key_rows, (ROWS, 1), jnp.float32, jnp.log(0.3), jnp.log(3.0)))
    position = jnp.arange(ROWS, dtype=jnp.float32)[:, None] / (ROWS - 1)
    body_draw = jax.random.normal(key_body, (ROWS, D), jnp.float32)
    col_scale = jnp.exp(jax.random.uniform(key_cols, (1, D), jnp.float32, jnp.log(0.5), jnp.log(2.0)))
    signal_gain = 0.8
    trend = jnp.exp(jnp.log(4.0) * (position - 0.5))
    signal = jnp.dot(left * (signal_gain * levels)[None, :], right, precision=lax.Precision.HIGHEST)
    values = 0.25 * ((body_draw + signal) * row_scale * col_scale * massive) * trend
    return values.astype(jnp.bfloat16)


def setup_inputs(seed: int = 0, part: int = 0) -> dict:
    arg_keys = jax.random.split(jax.random.key(seed), 3)
    part_keys = jax.random.split(jax.random.fold_in(arg_keys[2], part), 3)
    sketch_base = jax.random.randint(part_keys[0], (1,), 0, 1000000).astype(jnp.int32)
    states = draw_states(jax.random.fold_in(jax.random.fold_in(arg_keys[2], part), 71), part)
    return dict(sketch_base=sketch_base, states=states)


shift_ratio = 0.005

def scramble(value):
    value = value ^ jnp.right_shift(value, 16) & 65535
    value = value * 73244475
    value = value ^ jnp.right_shift(value, 16) & 65535
    value = value * 73244475
    value = value ^ jnp.right_shift(value, 16) & 65535
    return value

def sketch_table(base_value, feature_index, rank):
    counter = feature_index[:, None] * rank + jnp.arange(rank, dtype=jnp.int32)[None, :]
    offset = scramble(base_value)
    total = jnp.zeros(counter.shape, jnp.float32)
    for j in range(4):
        hashed = scramble(counter * 4 + j + offset)
        total = total + (hashed & 16777215).astype(jnp.float32) * (1.0 / 16777216.0)
    return ((total - 2.0) * 1.7320508).astype(jnp.bfloat16)

def gram(basis):
    return jnp.dot(basis.T, basis, precision=lax.Precision.HIGHEST)

def shifted(whole_gram):
    identity = jnp.eye(whole_gram.shape[0], dtype=whole_gram.dtype)
    return whole_gram + shift_ratio * jnp.trace(whole_gram) * identity

def orthonormal(sketch):
    lower = jnp.linalg.cholesky(shifted(gram(sketch)))
    first = jax.scipy.linalg.solve_triangular(lower, sketch.T, lower=True).T
    lower_two = jnp.linalg.cholesky(gram(first))
    return (jax.scipy.linalg.solve_triangular(lower_two, first.T, lower=True).T, lower)

def forward(states, right):
    blocks = states.reshape(N_ROW, ROWS_DEV, D)
    right_wide = right.astype(jnp.float32)

    def one(block):
        return jnp.dot(block.astype(jnp.float32), right_wide, precision=lax.Precision.HIGHEST)
    return lax.map(one, blocks).reshape(ROWS, right.shape[1])

def backward(states, basis):
    blocks = states.reshape(N_ROW, ROWS_DEV, D)
    pieces = basis.astype(jnp.bfloat16).astype(jnp.float32).reshape(N_ROW, ROWS_DEV, basis.shape[1])

    def step(total, item):
        block, piece = item
        return (total + jnp.dot(block.astype(jnp.float32).T, piece, precision=lax.Precision.HIGHEST), None)
    total, _ = lax.scan(step, jnp.zeros((D, basis.shape[1]), jnp.float32), (blocks, pieces))
    return total

def reference(sketch_base, states):
    omega = sketch_table(sketch_base[0], jnp.arange(D, dtype=jnp.int32), RANK)
    basis, lower = orthonormal(forward(states, omega))
    factor = lower * (1.0 / math.sqrt(ROWS * D))
    for step in range(POWER):
        weights = backward(states, basis).astype(jnp.bfloat16)
        basis, unused = orthonormal(forward(states, weights))
    return (backward(states, basis), factor)
```

```python
import functools
import math

import jax
import jax.numpy as jnp
from jax import lax
from jax.experimental import pallas as pl
from jax.experimental.pallas import tpu as pltpu
from jax.sharding import PartitionSpec as P

RANK = 64
POWER = 4
LANES = 128
SUB = 8


shift_ratio = 0.005


def scramble(value):
    value = value ^ jnp.right_shift(value, 16) & 65535
    value = value * 73244475
    value = value ^ jnp.right_shift(value, 16) & 65535
    value = value * 73244475
    value = value ^ jnp.right_shift(value, 16) & 65535
    return value


def sketch_table(base_value, feature_index, rank):
    counter = feature_index[:, None] * rank + jnp.arange(rank, dtype=jnp.int32)[None, :]
    offset = scramble(base_value)
    total = jnp.zeros(counter.shape, jnp.float32)
    for j in range(4):
        hashed = scramble(counter * 4 + j + offset)
        total = total + (hashed & 16777215).astype(jnp.float32) * (1.0 / 16777216.0)
    return ((total - 2.0) * 1.7320508).astype(jnp.bfloat16)


def three_terms(value):
    high = value.astype(jnp.bfloat16)
    rest = value - high.astype(jnp.float32)
    middle = rest.astype(jnp.bfloat16)
    low = (rest - middle.astype(jnp.float32)).astype(jnp.bfloat16)
    return high, middle, low


def dot_nn(left, right):
    return lax.dot_general(
        left, right, (((1,), (0,)), ((), ())), preferred_element_type=jnp.float32
    )


def dot_nt(left, right):
    return lax.dot_general(
        left, right, (((1,), (1,)), ((), ())), preferred_element_type=jnp.float32
    )


def small_times_wide(small, wide):
    sh, sm, sl = three_terms(small)
    wh, wm, wl = three_terms(wide)
    first = dot_nn(sl, wh) + dot_nn(sm, wm) + dot_nn(sh, wl)
    second = dot_nn(sm, wh) + dot_nn(sh, wm)
    return (first + second) + dot_nn(sh, wh)


def gram_of(wide):
    wh, wm, wl = three_terms(wide)
    hm = dot_nt(wh, wm)
    hl = dot_nt(wh, wl)
    return dot_nt(wh, wh) + ((hm + hm.T) + ((hl + hl.T) + dot_nt(wm, wm)))


def eliminate(matrix):
    size = matrix.shape[0]
    blocks = size // SUB
    row_index = lax.broadcasted_iota(jnp.int32, (SUB, size), 0)
    col_index = lax.broadcasted_iota(jnp.int32, (SUB, size), 1)
    work = [matrix[SUB * i : SUB * (i + 1), :] for i in range(blocks)]
    inverse = [
        jnp.where(col_index == row_index + SUB * i, 1.0, 0.0).astype(jnp.float32)
        for i in range(blocks)
    ]
    upper_rows, inverse_rows = [], []
    for b in range(blocks):
        columns = [
            {
                i: jnp.broadcast_to(work[i][:, SUB * b + j : SUB * b + j + 1], (SUB, size))
                for i in range(b, blocks)
            }
            for j in range(SUB)
        ]
        pivots = jnp.zeros((SUB, size), jnp.float32)
        for k in range(SUB):
            pivot = jnp.broadcast_to(columns[k][b][k : k + 1, :], (SUB, size))
            reciprocal = 1.0 / pivot
            pivots = jnp.where(row_index == k, pivot, pivots)
            work_row = jnp.broadcast_to(work[b][k : k + 1, :], (SUB, size))
            inverse_row = jnp.broadcast_to(inverse[b][k : k + 1, :], (SUB, size))
            later = [
                jnp.broadcast_to(columns[j][b][k : k + 1, :], (SUB, size))
                for j in range(k + 1, SUB)
            ]
            for i in range(b, blocks):
                factor = columns[k][i] * reciprocal
                if i == b:
                    factor = jnp.where(row_index > k, factor, 0.0)
                for j in range(k + 1, SUB):
                    columns[j][i] = columns[j][i] - factor * later[j - k - 1]
                work[i] = work[i] - factor * work_row
                inverse[i] = inverse[i] - factor * inverse_row
        root = lax.rsqrt(pivots)
        upper = work[b] * root
        upper_rows.append(jnp.where(col_index >= row_index + SUB * b, upper, 0.0))
        inverse_rows.append(inverse[b] * root)
    return jnp.concatenate(upper_rows, axis=0), jnp.concatenate(inverse_rows, axis=0)


def shifted(whole_gram):
    size = whole_gram.shape[0]
    diagonal = lax.broadcasted_iota(jnp.int32, (size, size), 0) == lax.broadcasted_iota(
        jnp.int32, (size, size), 1
    )
    on_diagonal = jnp.where(diagonal, whole_gram, 0.0)
    trace = jnp.sum(jnp.sum(on_diagonal, axis=1, keepdims=True), axis=0, keepdims=True)
    return jnp.where(diagonal, whole_gram + shift_ratio * trace, whole_gram)


def both_passes(wide):
    upper, inverse_one = eliminate(shifted(gram_of(wide)))
    first = small_times_wide(inverse_one, wide)
    unused, inverse_two = eliminate(gram_of(first))
    return upper, inverse_one, first, inverse_two


def wide_of(z_ref):
    return jnp.concatenate([z_ref[i] for i in range(z_ref.shape[0])], axis=1)


def narrow_basis(z_ref):
    upper, inverse_one, first, inverse_two = both_passes(wide_of(z_ref))
    return small_times_wide(inverse_two, first).astype(jnp.bfloat16), upper


def power_body(basis, a_ref, p_ref):
    weights = dot_nn(basis, a_ref[...]).astype(jnp.bfloat16)
    forth = dot_nt(weights, a_ref[...])
    width = p_ref.shape[2]
    for i in range(p_ref.shape[0]):
        p_ref[i] = forth[:, width * i : width * (i + 1)]


def orth_kernel(z_ref, basis_ref, upper_ref):
    basis_ref[...], upper_ref[...] = narrow_basis(z_ref)


def power_kernel(basis_ref, a_ref, p_ref):
    power_body(basis_ref[...], a_ref, p_ref)


def orth_power_kernel(z_ref, a_ref, p_ref):
    basis, unused = narrow_basis(z_ref)
    power_body(basis, a_ref, p_ref)


def last_kernel(z_ref, a_ref, out_ref):
    basis, unused = narrow_basis(z_ref)
    out_ref[...] = dot_nn(basis, a_ref[...]).T


def call(kernel, out_shapes, flops, *operands):
    moved = sum(x.size * x.dtype.itemsize for x in operands)
    return pl.pallas_call(
        kernel,
        out_shape=out_shapes,
        in_specs=[pl.BlockSpec(memory_space=pltpu.VMEM)] * len(operands),
        out_specs=jax.tree.map(lambda _: pl.BlockSpec(memory_space=pltpu.VMEM), out_shapes),
        compiler_params=pltpu.CompilerParams(vmem_limit_bytes=40 * 1024 * 1024),
        cost_estimate=pl.CostEstimate(flops=flops, bytes_accessed=moved, transcendentals=0),
    )(*operands)


def from_xor(value, axis, offset):
    size = lax.axis_size(axis)
    return lax.ppermute(value, axis, [(i, i ^ offset) for i in range(size)])


def sum_scatter(parts, n_z, n_col):
    half = parts.shape[0] // 2
    total = parts[:half] + from_xor(parts[half:], "row", 1)
    step = half // n_col
    pieces = [from_xor(total[step * o : step * (o + 1)], "col", o) for o in range(1, n_col)]
    total = functools.reduce(jnp.add, pieces, total[:step])
    pieces = [from_xor(total[o], "row", 2 * o) for o in range(1, n_z)]
    return functools.reduce(jnp.add, pieces, total[0])


def gather_all(own, n_z, n_col):
    chunks = jnp.stack([own] + [from_xor(own, "row", 2 * o) for o in range(1, n_z)])
    chunks = jnp.concatenate([chunks] + [from_xor(chunks, "col", o) for o in range(1, n_col)])
    return jnp.concatenate([chunks, from_xor(chunks, "row", 1)])


def per_device_transposed(sketch_base, states):
    n_row, n_col = lax.axis_size("row"), lax.axis_size("col")
    n_z = n_row // 2
    row, col = lax.axis_index("row"), lax.axis_index("col")
    rows_local, width_local = states.shape
    rows_total, width_total = rows_local * n_row, width_local * n_col
    chunk = rows_local // n_col
    cols = width_local // n_row
    n_chunks = n_row * n_col

    order = [col ^ o for o in range(n_col)]
    relative = jnp.concatenate(
        [lax.dynamic_slice_in_dim(states, o * chunk, chunk, 0) for o in order]
    )

    def block(offset):
        return lax.dynamic_slice_in_dim(relative, (row ^ offset) * cols, cols, 1)

    received = {0: block(0)}
    for offset in sorted(range(1, n_row), reverse=True):
        received[offset] = from_xor(block(offset), "row", offset)

    feature_index = col * width_local + jnp.arange(width_local, dtype=jnp.int32)
    omega = sketch_table(sketch_base[0], feature_index, RANK)
    partial = lax.dot_general(
        omega, relative, (((0,), (1,)), ((), ())), preferred_element_type=jnp.float32
    )
    own = partial[:, :chunk]
    for o in range(1, n_col):
        own = own + from_xor(partial[:, o * chunk : (o + 1) * chunk], "col", o)
    z = gather_all(own, n_z, n_col)

    a = jnp.concatenate(
        [
            received[2 * zo + core][co * chunk : (co + 1) * chunk]
            for core in range(2)
            for co in range(n_col)
            for zo in range(n_z)
        ]
    )

    f32 = jnp.float32
    square = jax.ShapeDtypeStruct((RANK, RANK), f32)
    wide = jax.ShapeDtypeStruct((RANK, rows_total), jnp.bfloat16)
    chunks = jax.ShapeDtypeStruct((n_chunks, RANK, chunk), f32)
    orth_flops = 8 * 64 * 64 * rows_total * 6
    power_flops = 4 * 64 * rows_total * cols

    basis, upper = call(orth_kernel, (wide, square), orth_flops, z)
    factor = upper.T * (1.0 / math.sqrt(rows_total * width_total))
    parts = call(power_kernel, chunks, power_flops, basis, a)
    for step in range(POWER - 1):
        z = gather_all(sum_scatter(parts, n_z, n_col), n_z, n_col)
        parts = call(orth_power_kernel, chunks, orth_flops + power_flops, z, a)
    z = gather_all(sum_scatter(parts, n_z, n_col), n_z, n_col)
    loadings = call(
        last_kernel, jax.ShapeDtypeStruct((cols, RANK), f32), orth_flops + power_flops, z, a
    )
    return loadings, factor


def local_gram(basis):
    return jnp.dot(basis.T, basis, precision=lax.Precision.HIGHEST)


def orthonormal_block(sketch):
    whole_gram = lax.psum(local_gram(sketch), "row")
    identity = jnp.eye(RANK, dtype=jnp.float32)
    lower = jnp.linalg.cholesky(whole_gram + shift_ratio * jnp.trace(whole_gram) * identity)
    first = jax.scipy.linalg.solve_triangular(lower, sketch.T, lower=True).T
    lower_two = jnp.linalg.cholesky(lax.psum(local_gram(first), "row"))
    return jax.scipy.linalg.solve_triangular(lower_two, first.T, lower=True).T, lower


def per_device_slabs(sketch_base, states):
    width_local = states.shape[1]
    rows_total = states.shape[0] * lax.axis_size("row")
    width_total = width_local * lax.axis_size("col")
    feature_index = lax.axis_index("col") * width_local + jnp.arange(width_local, dtype=jnp.int32)
    omega = sketch_table(sketch_base[0], feature_index, RANK)

    def row_basis(right):
        partial_sketch = jnp.dot(states, right, preferred_element_type=jnp.float32)
        basis_new, lower = orthonormal_block(lax.psum(partial_sketch, "col"))
        return basis_new.astype(jnp.bfloat16), lower

    def back(basis):
        return lax.dot_general(
            states, basis, (((0,), (0,)), ((), ())), preferred_element_type=jnp.float32
        )

    basis, first_lower = row_basis(omega)
    factor = first_lower * (1.0 / math.sqrt(rows_total * width_total))
    for step in range(POWER):
        basis, unused = row_basis(lax.psum(back(basis), "row").astype(jnp.bfloat16))
    return lax.psum_scatter(back(basis), "row", scatter_dimension=0, tiled=True), factor


def per_device(sketch_base, states):
    n_row, n_col = lax.axis_size("row"), lax.axis_size("col")
    rows_local, width_local = states.shape
    powers = n_row & (n_row - 1) == 0 and n_col & (n_col - 1) == 0 and n_row > 1
    tiled = rows_local % (n_col * LANES) == 0 and width_local % (n_row * LANES) == 0
    if powers and tiled:
        return per_device_transposed(sketch_base, states)
    return per_device_slabs(sketch_base, states)


def solution(mesh):
    placed = (P("grp"), P(("grp", "row"), "col"))
    return jax.shard_map(
        per_device,
        mesh=mesh,
        in_specs=placed,
        out_specs=(P(("col", "row"), "grp"), P("grp", None)),
        check_vma=False,
    )
```

```python
import functools
import math

import jax
import jax.numpy as jnp
from jax import lax
from jax.experimental import pallas as pl
from jax.experimental.pallas import tpu as pltpu
from jax.sharding import PartitionSpec as P

RANK = 64
POWER = 4
LANES = 128
SUB = 8


shift_ratio = 0.005


def scramble(value):
    value = value ^ jnp.right_shift(value, 16) & 65535
    value = value * 73244475
    value = value ^ jnp.right_shift(value, 16) & 65535
    value = value * 73244475
    value = value ^ jnp.right_shift(value, 16) & 65535
    return value


def sketch_table(base_value, feature_index, rank):
    counter = feature_index[:, None] * rank + jnp.arange(rank, dtype=jnp.int32)[None, :]
    offset = scramble(base_value)
    total = jnp.zeros(counter.shape, jnp.float32)
    for j in range(4):
        hashed = scramble(counter * 4 + j + offset)
        total = total + (hashed & 16777215).astype(jnp.float32) * (1.0 / 16777216.0)
    return ((total - 2.0) * 1.7320508).astype(jnp.bfloat16)


def three_terms(value):
    high = value.astype(jnp.bfloat16)
    rest = value - high.astype(jnp.float32)
    middle = rest.astype(jnp.bfloat16)
    low = (rest - middle.astype(jnp.float32)).astype(jnp.bfloat16)
    return high, middle, low


def dot_nn(left, right):
    return lax.dot_general(
        left, right, (((1,), (0,)), ((), ())), preferred_element_type=jnp.float32
    )


def dot_nt(left, right):
    return lax.dot_general(
        left, right, (((1,), (1,)), ((), ())), preferred_element_type=jnp.float32
    )


def small_times_wide(small, wide):
    sh, sm, sl = three_terms(small)
    wh, wm, wl = three_terms(wide)
    first = dot_nn(sl, wh) + dot_nn(sm, wm) + dot_nn(sh, wl)
    second = dot_nn(sm, wh) + dot_nn(sh, wm)
    return (first + second) + dot_nn(sh, wh)


def gram_of(wide):
    wh, wm, wl = three_terms(wide)
    hm = dot_nt(wh, wm)
    hl = dot_nt(wh, wl)
    return dot_nt(wh, wh) + ((hm + hm.T) + ((hl + hl.T) + dot_nt(wm, wm)))


def eliminate(matrix):
    size = matrix.shape[0]
    blocks = size // SUB
    row_index = lax.broadcasted_iota(jnp.int32, (SUB, size), 0)
    col_index = lax.broadcasted_iota(jnp.int32, (SUB, size), 1)
    work = [matrix[SUB * i : SUB * (i + 1), :] for i in range(blocks)]
    inverse = [
        jnp.where(col_index == row_index + SUB * i, 1.0, 0.0).astype(jnp.float32)
        for i in range(blocks)
    ]
    upper_rows, inverse_rows = [], []
    for b in range(blocks):
        columns = [
            {
                i: jnp.broadcast_to(work[i][:, SUB * b + j : SUB * b + j + 1], (SUB, size))
                for i in range(b, blocks)
            }
            for j in range(SUB)
        ]
        pivots = jnp.zeros((SUB, size), jnp.float32)
        for k in range(SUB):
            pivot = jnp.broadcast_to(columns[k][b][k : k + 1, :], (SUB, size))
            reciprocal = 1.0 / pivot
            pivots = jnp.where(row_index == k, pivot, pivots)
            work_row = jnp.broadcast_to(work[b][k : k + 1, :], (SUB, size))
            inverse_row = jnp.broadcast_to(inverse[b][k : k + 1, :], (SUB, size))
            later = [
                jnp.broadcast_to(columns[j][b][k : k + 1, :], (SUB, size))
                for j in range(k + 1, SUB)
            ]
            for i in range(b, blocks):
                factor = columns[k][i] * reciprocal
                if i == b:
                    factor = jnp.where(row_index > k, factor, 0.0)
                for j in range(k + 1, SUB):
                    columns[j][i] = columns[j][i] - factor * later[j - k - 1]
                work[i] = work[i] - factor * work_row
                inverse[i] = inverse[i] - factor * inverse_row
        root = lax.rsqrt(pivots)
        upper = work[b] * root
        upper_rows.append(jnp.where(col_index >= row_index + SUB * b, upper, 0.0))
        inverse_rows.append(inverse[b] * root)
    return jnp.concatenate(upper_rows, axis=0), jnp.concatenate(inverse_rows, axis=0)


def shifted(whole_gram):
    size = whole_gram.shape[0]
    diagonal = lax.broadcasted_iota(jnp.int32, (size, size), 0) == lax.broadcasted_iota(
        jnp.int32, (size, size), 1
    )
    on_diagonal = jnp.where(diagonal, whole_gram, 0.0)
    trace = jnp.sum(jnp.sum(on_diagonal, axis=1, keepdims=True), axis=0, keepdims=True)
    return jnp.where(diagonal, whole_gram + shift_ratio * trace, whole_gram)


def both_passes(wide):
    upper, inverse_one = eliminate(shifted(gram_of(wide)))
    first = small_times_wide(inverse_one, wide)
    unused, inverse_two = eliminate(gram_of(first))
    return upper, inverse_one, first, inverse_two


def wide_of(z_ref, at_ref):
    halves, n_z, n_col = z_ref.shape[:3]
    return jnp.concatenate(
        [
            z_ref[h, at_ref[0] ^ zo, c]
            for h in range(halves)
            for zo in range(n_z)
            for c in range(n_col)
        ],
        axis=1,
    )


def narrow_basis(z_ref, at_ref):
    upper, inverse_one, first, inverse_two = both_passes(wide_of(z_ref, at_ref))
    return small_times_wide(inverse_two, first).astype(jnp.bfloat16), upper


def power_body(basis, a_ref, at_ref, p_ref):
    weights = dot_nn(basis, a_ref[...]).astype(jnp.bfloat16)
    forth = dot_nt(weights, a_ref[...])
    halves, n_z, n_col, unused, width = p_ref.shape
    for h in range(halves):
        for zo in range(n_z):
            for c in range(n_col):
                i = (h * n_z + zo) * n_col + c
                p_ref[h, at_ref[0] ^ zo, c] = forth[:, width * i : width * (i + 1)]


def orth_kernel(at_ref, z_ref, basis_ref, upper_ref):
    basis_ref[...], upper_ref[...] = narrow_basis(z_ref, at_ref)


def power_kernel(at_ref, basis_ref, a_ref, p_ref):
    power_body(basis_ref[...], a_ref, at_ref, p_ref)


def orth_power_kernel(at_ref, z_ref, a_ref, p_ref):
    basis, unused = narrow_basis(z_ref, at_ref)
    power_body(basis, a_ref, at_ref, p_ref)


def last_kernel(at_ref, z_ref, a_ref, out_ref):
    basis, unused = narrow_basis(z_ref, at_ref)
    out_ref[...] = dot_nn(basis, a_ref[...]).T


def call(kernel, out_shapes, flops, at, *operands):
    moved = sum(x.size * x.dtype.itemsize for x in operands)
    return pl.pallas_call(
        kernel,
        out_shape=out_shapes,
        in_specs=[pl.BlockSpec(memory_space=pltpu.SMEM)]
        + [pl.BlockSpec(memory_space=pltpu.VMEM)] * len(operands),
        out_specs=jax.tree.map(lambda _: pl.BlockSpec(memory_space=pltpu.VMEM), out_shapes),
        compiler_params=pltpu.CompilerParams(vmem_limit_bytes=40 * 1024 * 1024),
        cost_estimate=pl.CostEstimate(flops=flops, bytes_accessed=moved, transcendentals=0),
    )(at, *operands)


def swap_cores(value):
    return lax.ppermute(value, "core", [(0, 1), (1, 0)])


def sum_scatter(parts):
    total = parts[0] + swap_cores(parts[1])
    total = total.reshape((-1,) + total.shape[2:])
    return jnp.sum(lax.all_to_all(total, ("z", "col"), 0, 0, tiled=True), axis=0)


def gather_all(own):
    n_z, n_col = lax.axis_size("z"), lax.axis_size("col")
    copies = jnp.broadcast_to(own[None], (n_z * n_col,) + own.shape)
    chunks = lax.all_to_all(copies, ("z", "col"), 0, 0, tiled=True)
    chunks = chunks.reshape((n_z, n_col) + own.shape)
    return jnp.stack([chunks, swap_cores(chunks)])


def per_device_transposed(sketch_base, states):
    n_z, n_core, n_col = lax.axis_size("z"), lax.axis_size("core"), lax.axis_size("col")
    n_row = n_z * n_core
    z_at, core, col = lax.axis_index("z"), lax.axis_index("core"), lax.axis_index("col")
    row = z_at * n_core + core
    rows_local, width_local = states.shape
    rows_total, width_total = rows_local * n_row, width_local * n_col
    chunk = rows_local // n_col
    cols = width_local // n_row

    def block(offset):
        return lax.dynamic_slice_in_dim(states, (row ^ offset) * cols, cols, 1)

    def to_row(value, offset):
        pairs = [(i, i ^ offset) for i in range(n_row)]
        return lax.ppermute(value, ("z", "core"), pairs)

    received = {0: block(0)}
    for offset in sorted(range(1, n_row), reverse=True):
        received[offset] = to_row(block(offset), offset)

    feature_index = col * width_local + jnp.arange(width_local, dtype=jnp.int32)
    omega = sketch_table(sketch_base[0], feature_index, RANK)
    partial = lax.dot_general(
        omega, states, (((0,), (1,)), ((), ())), preferred_element_type=jnp.float32
    )
    partial = partial.reshape(RANK, n_col, chunk).transpose(1, 0, 2)
    own = jnp.sum(lax.all_to_all(partial, "col", 0, 0, tiled=True), axis=0)
    z = gather_all(own)

    a = jnp.concatenate([received[2 * zo + other] for other in range(2) for zo in range(n_z)])
    at = z_at[None].astype(jnp.int32)

    f32 = jnp.float32
    square = jax.ShapeDtypeStruct((RANK, RANK), f32)
    wide = jax.ShapeDtypeStruct((RANK, rows_total), jnp.bfloat16)
    chunks = jax.ShapeDtypeStruct((2, n_z, n_col, RANK, chunk), f32)
    orth_flops = 8 * 64 * 64 * rows_total * 6
    power_flops = 4 * 64 * rows_total * cols

    basis, upper = call(orth_kernel, (wide, square), orth_flops, at, z)
    factor = upper.T * (1.0 / math.sqrt(rows_total * width_total))
    parts = call(power_kernel, chunks, power_flops, at, basis, a)
    for step in range(POWER - 1):
        z = gather_all(sum_scatter(parts))
        parts = call(orth_power_kernel, chunks, orth_flops + power_flops, at, z, a)
    z = gather_all(sum_scatter(parts))
    loadings = call(
        last_kernel, jax.ShapeDtypeStruct((cols, RANK), f32), orth_flops + power_flops, at, z, a
    )
    return loadings, factor


def local_gram(basis):
    return jnp.dot(basis.T, basis, precision=lax.Precision.HIGHEST)


def orthonormal_block(sketch):
    whole_gram = lax.psum(local_gram(sketch), "row")
    identity = jnp.eye(RANK, dtype=jnp.float32)
    lower = jnp.linalg.cholesky(whole_gram + shift_ratio * jnp.trace(whole_gram) * identity)
    first = jax.scipy.linalg.solve_triangular(lower, sketch.T, lower=True).T
    lower_two = jnp.linalg.cholesky(lax.psum(local_gram(first), "row"))
    return jax.scipy.linalg.solve_triangular(lower_two, first.T, lower=True).T, lower


def per_device_slabs(sketch_base, states):
    width_local = states.shape[1]
    rows_total = states.shape[0] * lax.axis_size("row")
    width_total = width_local * lax.axis_size("col")
    feature_index = lax.axis_index("col") * width_local + jnp.arange(width_local, dtype=jnp.int32)
    omega = sketch_table(sketch_base[0], feature_index, RANK)

    def row_basis(right):
        partial_sketch = jnp.dot(states, right, preferred_element_type=jnp.float32)
        basis_new, lower = orthonormal_block(lax.psum(partial_sketch, "col"))
        return basis_new.astype(jnp.bfloat16), lower

    def back(basis):
        return lax.dot_general(
            states, basis, (((0,), (0,)), ((), ())), preferred_element_type=jnp.float32
        )

    basis, first_lower = row_basis(omega)
    factor = first_lower * (1.0 / math.sqrt(rows_total * width_total))
    for step in range(POWER):
        basis, unused = row_basis(lax.psum(back(basis), "row").astype(jnp.bfloat16))
    return lax.psum_scatter(back(basis), "row", scatter_dimension=0, tiled=True), factor


def solution(mesh):
    n_grp, n_row, n_col = (mesh.shape[name] for name in ("grp", "row", "col"))
    fits = n_row % 2 == 0 and n_row & (n_row - 1) == 0

    def run(sketch_base, states):
        rows_local = states.shape[0] // (n_grp * n_row)
        width_local = states.shape[1] // n_col
        tiled = rows_local % (n_col * LANES) == 0 and width_local % (n_row * LANES) == 0
        if fits and tiled:
            split = mesh.devices.reshape(n_grp, n_row // 2, 2, n_col)
            inner = jax.sharding.Mesh(split, ("grp", "z", "core", "col"))
            row, step = ("z", "core"), per_device_transposed
        else:
            inner, row, step = mesh, ("row",), per_device_slabs
        return jax.shard_map(
            step,
            mesh=inner,
            in_specs=(P("grp"), P(("grp",) + row, "col")),
            out_specs=(P(("col",) + row, "grp"), P("grp", None)),
            check_vma=False,
        )(sketch_base, states)

    return run
```

```python
import functools
import math

import jax
import jax.numpy as jnp
from jax import lax
from jax.experimental import pallas as pl
from jax.experimental.pallas import tpu as pltpu
from jax.sharding import PartitionSpec as P

RANK = 64
POWER = 4
LANES = 128
SUB = 8


shift_ratio = 0.005


def scramble(value):
    value = value ^ jnp.right_shift(value, 16) & 65535
    value = value * 73244475
    value = value ^ jnp.right_shift(value, 16) & 65535
    value = value * 73244475
    value = value ^ jnp.right_shift(value, 16) & 65535
    return value


def sketch_table(base_value, feature_index, rank):
    counter = feature_index[:, None] * rank + jnp.arange(rank, dtype=jnp.int32)[None, :]
    offset = scramble(base_value)
    total = jnp.zeros(counter.shape, jnp.float32)
    for j in range(4):
        hashed = scramble(counter * 4 + j + offset)
        total = total + (hashed & 16777215).astype(jnp.float32) * (1.0 / 16777216.0)
    return ((total - 2.0) * 1.7320508).astype(jnp.bfloat16)


def three_terms(value):
    high = value.astype(jnp.bfloat16)
    rest = value - high.astype(jnp.float32)
    middle = rest.astype(jnp.bfloat16)
    low = (rest - middle.astype(jnp.float32)).astype(jnp.bfloat16)
    return high, middle, low


def dot_nn(left, right):
    return lax.dot_general(
        left, right, (((1,), (0,)), ((), ())), preferred_element_type=jnp.float32
    )


def dot_nt(left, right):
    return lax.dot_general(
        left, right, (((1,), (1,)), ((), ())), preferred_element_type=jnp.float32
    )


def small_times_wide(small, wide):
    sh, sm, sl = three_terms(small)
    wh, wm, wl = three_terms(wide)
    first = dot_nn(sl, wh) + dot_nn(sm, wm) + dot_nn(sh, wl)
    second = dot_nn(sm, wh) + dot_nn(sh, wm)
    return (first + second) + dot_nn(sh, wh)


def gram_of(wide):
    wh, wm, wl = three_terms(wide)
    hm = dot_nt(wh, wm)
    hl = dot_nt(wh, wl)
    return dot_nt(wh, wh) + ((hm + hm.T) + ((hl + hl.T) + dot_nt(wm, wm)))


def eliminate(matrix):
    size = matrix.shape[0]
    blocks = size // SUB
    row_index = lax.broadcasted_iota(jnp.int32, (SUB, size), 0)
    col_index = lax.broadcasted_iota(jnp.int32, (SUB, size), 1)
    work = [matrix[SUB * i : SUB * (i + 1), :] for i in range(blocks)]
    inverse = [
        jnp.where(col_index == row_index + SUB * i, 1.0, 0.0).astype(jnp.float32)
        for i in range(blocks)
    ]
    upper_rows, inverse_rows = [], []
    for b in range(blocks):
        columns = [
            {
                i: jnp.broadcast_to(work[i][:, SUB * b + j : SUB * b + j + 1], (SUB, size))
                for i in range(b, blocks)
            }
            for j in range(SUB)
        ]
        pivots = jnp.zeros((SUB, size), jnp.float32)
        for k in range(SUB):
            pivot = jnp.broadcast_to(columns[k][b][k : k + 1, :], (SUB, size))
            reciprocal = 1.0 / pivot
            pivots = jnp.where(row_index == k, pivot, pivots)
            work_row = jnp.broadcast_to(work[b][k : k + 1, :], (SUB, size))
            inverse_row = jnp.broadcast_to(inverse[b][k : k + 1, :], (SUB, size))
            later = [
                jnp.broadcast_to(columns[j][b][k : k + 1, :], (SUB, size))
                for j in range(k + 1, SUB)
            ]
            for i in range(b, blocks):
                factor = columns[k][i] * reciprocal
                if i == b:
                    factor = jnp.where(row_index > k, factor, 0.0)
                for j in range(k + 1, SUB):
                    columns[j][i] = columns[j][i] - factor * later[j - k - 1]
                work[i] = work[i] - factor * work_row
                inverse[i] = inverse[i] - factor * inverse_row
        root = lax.rsqrt(pivots)
        upper = work[b] * root
        upper_rows.append(jnp.where(col_index >= row_index + SUB * b, upper, 0.0))
        inverse_rows.append(inverse[b] * root)
    return jnp.concatenate(upper_rows, axis=0), jnp.concatenate(inverse_rows, axis=0)


def shifted(whole_gram):
    size = whole_gram.shape[0]
    diagonal = lax.broadcasted_iota(jnp.int32, (size, size), 0) == lax.broadcasted_iota(
        jnp.int32, (size, size), 1
    )
    on_diagonal = jnp.where(diagonal, whole_gram, 0.0)
    trace = jnp.sum(jnp.sum(on_diagonal, axis=1, keepdims=True), axis=0, keepdims=True)
    return jnp.where(diagonal, whole_gram + shift_ratio * trace, whole_gram)


def both_passes(wide):
    upper, inverse_one = eliminate(shifted(gram_of(wide)))
    first = small_times_wide(inverse_one, wide)
    unused, inverse_two = eliminate(gram_of(first))
    return upper, inverse_one, first, inverse_two


def wide_of(z_ref, at_ref):
    chunks = [z_ref[at_ref[i]].astype(jnp.float32) for i in range(z_ref.shape[0])]
    return jnp.concatenate(chunks, axis=1)


def narrow_basis(z_ref, at_ref):
    upper, inverse_one, first, inverse_two = both_passes(wide_of(z_ref, at_ref))
    return small_times_wide(inverse_two, first).astype(jnp.bfloat16), upper


def power_body(basis, a_ref, at_ref, keep_ref, send_ref, all_ref):
    weights = dot_nn(basis, a_ref[...]).astype(jnp.bfloat16)
    forth = dot_nt(weights, a_ref[...])
    half, unused, width = keep_ref.shape
    for i in range(2 * half):
        all_ref[at_ref[i]] = forth[:, width * i : width * (i + 1)]
    keep_ref[...] = all_ref[:half]
    send_ref[...] = all_ref[half:].astype(send_ref.dtype)


def orth_kernel(at_ref, z_ref, basis_ref, upper_ref):
    basis_ref[...], upper_ref[...] = narrow_basis(z_ref, at_ref)


def power_kernel(at_ref, basis_ref, a_ref, keep_ref, send_ref, all_ref):
    power_body(basis_ref[...], a_ref, at_ref, keep_ref, send_ref, all_ref)


def orth_power_kernel(at_ref, z_ref, a_ref, keep_ref, send_ref, all_ref):
    basis, unused = narrow_basis(z_ref, at_ref)
    power_body(basis, a_ref, at_ref, keep_ref, send_ref, all_ref)


def last_kernel(at_ref, z_ref, a_ref, out_ref):
    basis, unused = narrow_basis(z_ref, at_ref)
    out_ref[...] = dot_nn(basis, a_ref[...])


def call(kernel, out_shapes, flops, at, *operands, scratch=()):
    moved = sum(x.size * x.dtype.itemsize for x in operands)
    return pl.pallas_call(
        kernel,
        out_shape=out_shapes,
        scratch_shapes=scratch,
        in_specs=[pl.BlockSpec(memory_space=pltpu.SMEM)]
        + [pl.BlockSpec(memory_space=pltpu.VMEM)] * len(operands),
        out_specs=jax.tree.map(lambda _: pl.BlockSpec(memory_space=pltpu.VMEM), out_shapes),
        compiler_params=pltpu.CompilerParams(vmem_limit_bytes=40 * 1024 * 1024),
        cost_estimate=pl.CostEstimate(flops=flops, bytes_accessed=moved, transcendentals=0),
    )(at, *operands)


def bits(size):
    return [1 << k for k in range(size.bit_length() - 1)]


def from_xor(value, axis, offset):
    size = lax.axis_size(axis)
    return lax.ppermute(value, axis, [(i, i ^ offset) for i in range(size)])


def stages():
    steps = [("col", bit) for bit in bits(lax.axis_size("col"))]
    steps += [("z", bit) for bit in bits(lax.axis_size("z"))]
    return [(axis, bit, (axis, bit) != steps[-1]) for axis, bit in steps]


def sum_parts(keep, send, dtype):
    total = keep + from_xor(send, "core", 1).astype(jnp.float32)
    for axis, bit, halved in stages():
        if halved:
            half = total.shape[0] // 2
            other = from_xor(total[half:].astype(dtype), axis, bit)
            total = total[:half] + other.astype(jnp.float32)
        else:
            mine = total.astype(dtype)
            other = from_xor(mine, axis, bit)
            total = mine.astype(jnp.float32) + other.astype(jnp.float32)
    return total.astype(dtype)


def gather_parts(own):
    for axis, bit, halved in reversed(stages()):
        if halved:
            own = jnp.concatenate([own, from_xor(own, axis, bit)])
    return jnp.concatenate([own, from_xor(own, "core", 1)])


def chunk_places(digits, n_col, n_z):
    here = {name: lax.axis_index(name) for name in ("z", "core", "col")}
    index = jnp.arange(n_z * 2 * n_col, dtype=jnp.int32)
    coordinate = {"z": index // (2 * n_col), "core": index // n_col % 2, "col": index % n_col}
    place = jnp.zeros_like(index)
    for axis, bit, relative in digits:
        value = coordinate[axis] ^ here[axis] if relative else coordinate[axis]
        place = place * 2 + (value // bit) % 2
    return place.astype(jnp.int32)


def per_device_transposed(sketch_base, states):
    n_z, n_core, n_col = lax.axis_size("z"), lax.axis_size("core"), lax.axis_size("col")
    n_row = n_z * n_core
    rows_local, width_local = states.shape
    rows_total, width_total = rows_local * n_row, width_local * n_col
    chunk = rows_local // n_col
    cols = width_local // n_row
    n_chunks = n_row * n_col

    by_target = states.reshape(rows_local, n_row, cols).transpose(1, 0, 2)
    a = lax.all_to_all(by_target, ("z", "core"), 0, 0, tiled=True).reshape(rows_total, cols)

    col = lax.axis_index("col")
    feature_index = col * width_local + jnp.arange(width_local, dtype=jnp.int32)
    omega = sketch_table(sketch_base[0], feature_index, RANK)
    z = lax.dot_general(
        omega, states, (((0,), (1,)), ((), ())), preferred_element_type=jnp.float32
    )
    for bit in bits(n_col):
        z = z + from_xor(z, "col", bit)
    z = z.reshape(RANK, n_col, chunk).transpose(1, 0, 2)
    z_bits = bits(n_z)[::-1]
    for bit in z_bits:
        z = jnp.concatenate([z, from_xor(z, "z", bit)])
    z = jnp.concatenate([z, from_xor(z, "core", 1)])
    digits = [("core", 1, True)] + [("z", bit, True) for bit in z_bits[::-1]]
    at_first = chunk_places(digits + [("col", bit, False) for bit in bits(n_col)[::-1]], n_col, n_z)
    at = chunk_places([("core", 1, True)] + stages(), n_col, n_z)

    f32 = jnp.float32
    square = jax.ShapeDtypeStruct((RANK, RANK), f32)
    wide = jax.ShapeDtypeStruct((RANK, rows_total), jnp.bfloat16)
    orth_flops = 8 * 64 * 64 * rows_total * 6
    power_flops = 4 * 64 * rows_total * cols

    def sent_as(dtype):
        shape = (n_chunks // 2, RANK, chunk)
        return jax.ShapeDtypeStruct(shape, f32), jax.ShapeDtypeStruct(shape, dtype)

    basis, upper = call(orth_kernel, (wide, square), orth_flops, at_first, z)
    factor = upper.T * (1.0 / math.sqrt(rows_total * width_total))
    dtype = f32
    scratch = (pltpu.VMEM((n_chunks, RANK, chunk), f32),)
    parts = call(power_kernel, sent_as(dtype), power_flops, at, basis, a, scratch=scratch)
    for step in range(POWER - 1):
        z = gather_parts(sum_parts(*parts, dtype))
        dtype = jnp.bfloat16
        flops = orth_flops + power_flops
        parts = call(orth_power_kernel, sent_as(dtype), flops, at, z, a, scratch=scratch)
    z = gather_parts(sum_parts(*parts, dtype))
    loadings = jax.ShapeDtypeStruct((RANK, cols), f32)
    return call(last_kernel, loadings, orth_flops + power_flops, at, z, a).T, factor


def local_gram(basis):
    return jnp.dot(basis.T, basis, precision=lax.Precision.HIGHEST)


def orthonormal_block(sketch):
    whole_gram = lax.psum(local_gram(sketch), "row")
    identity = jnp.eye(RANK, dtype=jnp.float32)
    lower = jnp.linalg.cholesky(whole_gram + shift_ratio * jnp.trace(whole_gram) * identity)
    first = jax.scipy.linalg.solve_triangular(lower, sketch.T, lower=True).T
    lower_two = jnp.linalg.cholesky(lax.psum(local_gram(first), "row"))
    return jax.scipy.linalg.solve_triangular(lower_two, first.T, lower=True).T, lower


def per_device_slabs(sketch_base, states):
    width_local = states.shape[1]
    rows_total = states.shape[0] * lax.axis_size("row")
    width_total = width_local * lax.axis_size("col")
    feature_index = lax.axis_index("col") * width_local + jnp.arange(width_local, dtype=jnp.int32)
    omega = sketch_table(sketch_base[0], feature_index, RANK)

    def row_basis(right):
        partial_sketch = jnp.dot(states, right, preferred_element_type=jnp.float32)
        basis_new, lower = orthonormal_block(lax.psum(partial_sketch, "col"))
        return basis_new.astype(jnp.bfloat16), lower

    def back(basis):
        return lax.dot_general(
            states, basis, (((0,), (0,)), ((), ())), preferred_element_type=jnp.float32
        )

    basis, first_lower = row_basis(omega)
    factor = first_lower * (1.0 / math.sqrt(rows_total * width_total))
    for step in range(POWER):
        basis, unused = row_basis(lax.psum(back(basis), "row").astype(jnp.bfloat16))
    return lax.psum_scatter(back(basis), "row", scatter_dimension=0, tiled=True), factor


def solution(mesh):
    n_grp, n_row, n_col = (mesh.shape[name] for name in ("grp", "row", "col"))
    fits = n_row % 2 == 0 and n_row & (n_row - 1) == 0

    def run(sketch_base, states):
        rows_local = states.shape[0] // (n_grp * n_row)
        width_local = states.shape[1] // n_col
        tiled = rows_local % (n_col * LANES) == 0 and width_local % (n_row * LANES) == 0
        if fits and tiled:
            split = mesh.devices.reshape(n_grp, n_row // 2, 2, n_col)
            inner = jax.sharding.Mesh(split, ("grp", "z", "core", "col"))
            row, step = ("z", "core"), per_device_transposed
        else:
            inner, row, step = mesh, ("row",), per_device_slabs
        return jax.shard_map(
            step,
            mesh=inner,
            in_specs=(P("grp"), P(("grp",) + row, "col")),
            out_specs=(P(("col",) + row, "grp"), P("grp", None)),
            check_vma=False,
        )(sketch_base, states)

    return run
```

```python
import functools
import math

import jax
import jax.numpy as jnp
from jax import lax
from jax.experimental import pallas as pl
from jax.experimental.pallas import tpu as pltpu
from jax.sharding import PartitionSpec as P

RANK = 64
POWER = 4
LANES = 128
SUB = 8


shift_ratio = 0.005


def scramble(value):
    value = value ^ jnp.right_shift(value, 16) & 65535
    value = value * 73244475
    value = value ^ jnp.right_shift(value, 16) & 65535
    value = value * 73244475
    value = value ^ jnp.right_shift(value, 16) & 65535
    return value


def sketch_table(base_value, feature_index, rank):
    counter = feature_index[:, None] * rank + jnp.arange(rank, dtype=jnp.int32)[None, :]
    offset = scramble(base_value)
    total = jnp.zeros(counter.shape, jnp.float32)
    for j in range(4):
        hashed = scramble(counter * 4 + j + offset)
        total = total + (hashed & 16777215).astype(jnp.float32) * (1.0 / 16777216.0)
    return ((total - 2.0) * 1.7320508).astype(jnp.bfloat16)


def terms_of(value):
    if value.dtype == jnp.bfloat16:
        return [value]
    high = value.astype(jnp.bfloat16)
    rest = value - high.astype(jnp.float32)
    middle = rest.astype(jnp.bfloat16)
    low = (rest - middle.astype(jnp.float32)).astype(jnp.bfloat16)
    return [high, middle, low]


def dot_nn(left, right):
    return lax.dot_general(
        left, right, (((1,), (0,)), ((), ())), preferred_element_type=jnp.float32
    )


def dot_nt(left, right):
    return lax.dot_general(
        left, right, (((1,), (1,)), ((), ())), preferred_element_type=jnp.float32
    )


def small_times_wide(small, wide):
    left, right = terms_of(small), terms_of(wide)
    pairs = [(i, d - i) for d in (2, 1, 0) for i in range(d + 1)]
    pairs = [(i, j) for i, j in pairs if i < len(left) and j < len(right)]
    return dot_nn(
        jnp.concatenate([left[i] for i, unused in pairs], axis=1),
        jnp.concatenate([right[j] for unused, j in pairs], axis=0),
    )


def gram_of(wide):
    terms = terms_of(wide)
    if len(terms) == 1:
        return dot_nt(terms[0], terms[0])
    rank = wide.shape[0]
    stacked = jnp.concatenate(terms, axis=0)
    both = dot_nt(stacked, stacked)
    cross = both[rank : 2 * rank, :rank] + both[2 * rank :, :rank]
    return both[:rank, :rank] + ((cross + cross.T) + both[rank : 2 * rank, rank : 2 * rank])


def eliminate(matrix):
    size = matrix.shape[0]
    blocks = size // SUB
    row_index = lax.broadcasted_iota(jnp.int32, (SUB, 2 * size), 0)
    square_row = lax.broadcasted_iota(jnp.int32, (SUB, size), 0)
    square_col = lax.broadcasted_iota(jnp.int32, (SUB, size), 1)
    work = []
    for i in range(blocks):
        unit = jnp.where(square_col == square_row + SUB * i, 1.0, 0.0).astype(jnp.float32)
        work.append(jnp.concatenate([matrix[SUB * i : SUB * (i + 1), :], unit], axis=1))
    rows = []
    for b in range(blocks):
        columns = [
            {
                i: jnp.broadcast_to(work[i][:, SUB * b + j : SUB * b + j + 1], (SUB, 2 * size))
                for i in range(b, blocks)
            }
            for j in range(SUB)
        ]
        pivots = jnp.zeros((SUB, 2 * size), jnp.float32)
        for k in range(SUB):
            pivot = jnp.broadcast_to(columns[k][b][k : k + 1, :], (SUB, 2 * size))
            reciprocal = 1.0 / pivot
            pivots = jnp.where(row_index == k, pivot, pivots)
            work_row = jnp.broadcast_to(work[b][k : k + 1, :], (SUB, 2 * size))
            later = [
                jnp.broadcast_to(columns[j][b][k : k + 1, :], (SUB, 2 * size))
                for j in range(k + 1, SUB)
            ]
            for i in range(b, blocks):
                factor = columns[k][i] * reciprocal
                if i == b:
                    factor = jnp.where(row_index > k, factor, 0.0)
                for j in range(k + 1, SUB):
                    columns[j][i] = columns[j][i] - factor * later[j - k - 1]
                work[i] = work[i] - factor * work_row
        rows.append(work[b] * lax.rsqrt(pivots))
    both = jnp.concatenate(rows, axis=0)
    keep = lax.broadcasted_iota(jnp.int32, (size, size), 1) >= lax.broadcasted_iota(
        jnp.int32, (size, size), 0
    )
    return jnp.where(keep, both[:, :size], 0.0), both[:, size:]


def shifted(whole_gram):
    size = whole_gram.shape[0]
    diagonal = lax.broadcasted_iota(jnp.int32, (size, size), 0) == lax.broadcasted_iota(
        jnp.int32, (size, size), 1
    )
    on_diagonal = jnp.where(diagonal, whole_gram, 0.0)
    trace = jnp.sum(jnp.sum(on_diagonal, axis=1, keepdims=True), axis=0, keepdims=True)
    return jnp.where(diagonal, whole_gram + shift_ratio * trace, whole_gram)


def wide_of(at_ref, z_refs):
    half = z_refs[0].shape[0]
    n_col = at_ref.shape[0] // half
    chunks = [z_refs[i // n_col % 2][at_ref[i]] for i in range(at_ref.shape[0])]
    return jnp.concatenate(chunks, axis=1)


def narrow_basis(at_ref, z_refs):
    wide = wide_of(at_ref, z_refs)
    upper, inverse_one = eliminate(shifted(gram_of(wide)))
    first = small_times_wide(inverse_one, wide)
    unused, inverse_two = eliminate(gram_of(first))
    return small_times_wide(inverse_two, first).astype(jnp.bfloat16), upper


def times_slab(basis, a_refs):
    rows = a_refs[0].shape[0]
    pieces = [
        dot_nn(basis[:, rows * s : rows * (s + 1)], a_ref[...]) for s, a_ref in enumerate(a_refs)
    ]
    return functools.reduce(jnp.add, pieces)


def power_body(basis, a_refs, at_ref, part_refs):
    weights = times_slab(basis, a_refs).astype(jnp.bfloat16)
    width = part_refs[0].shape[2]
    n_col = at_ref.shape[0] // len(a_refs)
    for s, a_ref in enumerate(a_refs):
        forth = dot_nt(weights, a_ref[...])
        target = part_refs[s % 2]
        for c in range(n_col):
            block = forth[:, width * c : width * (c + 1)]
            target[at_ref[s * n_col + c]] = block.astype(target.dtype)


def orth_kernel(at_ref, z_ref, other_ref, basis_ref, upper_ref):
    basis_ref[...], upper_ref[...] = narrow_basis(at_ref, (z_ref, other_ref))


def power_kernel(at_ref, basis_ref, *refs):
    power_body(basis_ref[...], refs[:-2], at_ref, refs[-2:])


def orth_power_kernel(at_ref, z_ref, other_ref, *refs):
    basis, unused = narrow_basis(at_ref, (z_ref, other_ref))
    power_body(basis, refs[:-2], at_ref, refs[-2:])


def last_kernel(at_ref, z_ref, other_ref, *refs):
    basis, unused = narrow_basis(at_ref, (z_ref, other_ref))
    refs[-1][...] = times_slab(basis, refs[:-1])


def call(kernel, out_shapes, flops, at, *operands):
    moved = sum(x.size * x.dtype.itemsize for x in operands)
    return pl.pallas_call(
        kernel,
        out_shape=out_shapes,
        in_specs=[pl.BlockSpec(memory_space=pltpu.SMEM)]
        + [pl.BlockSpec(memory_space=pltpu.VMEM)] * len(operands),
        out_specs=jax.tree.map(lambda _: pl.BlockSpec(memory_space=pltpu.VMEM), out_shapes),
        compiler_params=pltpu.CompilerParams(vmem_limit_bytes=40 * 1024 * 1024),
        cost_estimate=pl.CostEstimate(flops=flops, bytes_accessed=moved, transcendentals=0),
    )(at, *operands)


def bits(size):
    return [1 << k for k in range(size.bit_length() - 1)]


def from_xor(value, axis, offset):
    size = math.prod(lax.axis_size(name) for name in axis)
    return lax.ppermute(value, axis, [(i, i ^ offset) for i in range(size)])


def sum_parts(keep, send, dtype):
    total = keep + from_xor(send, ("core",), 1).astype(jnp.float32)
    for bit in bits(lax.axis_size("col")):
        half = total.shape[0] // 2
        other = from_xor(total[half:].astype(dtype), ("col",), bit)
        total = total[:half] + other.astype(jnp.float32)
    for bit in bits(lax.axis_size("z")):
        mine = total.astype(dtype)
        total = mine.astype(jnp.float32) + from_xor(mine, ("z",), bit).astype(jnp.float32)
    return total.astype(dtype)


def gather_parts(own):
    for bit in bits(lax.axis_size("col"))[::-1]:
        own = jnp.concatenate([own, from_xor(own, ("col",), bit)])
    return own, from_xor(own, ("core",), 1)


def chunk_places(digits):
    n_z, n_col = lax.axis_size("z"), lax.axis_size("col")
    index = jnp.arange(n_z * 2 * n_col, dtype=jnp.int32)
    z_at, col_at = lax.axis_index("z"), lax.axis_index("col")
    column = index % n_col
    relative = {"z": index // (2 * n_col), "col": column ^ col_at}
    absolute = {"z": relative["z"] ^ z_at, "col": column}
    place = jnp.zeros_like(index)
    for axis, bit, is_relative in digits:
        place = place * 2 + ((relative if is_relative else absolute)[axis] // bit) % 2
    return place.astype(jnp.int32)


def per_device_transposed(sketch_base, states):
    n_z, n_core, n_col = lax.axis_size("z"), lax.axis_size("core"), lax.axis_size("col")
    n_row = n_z * n_core
    rows_local, width_local = states.shape
    rows_total, width_total = rows_local * n_row, width_local * n_col
    chunk = rows_local // n_col
    cols = width_local // n_row
    half = n_z * n_col
    row = lax.axis_index("z") * n_core + lax.axis_index("core")
    pieces = [None] * n_row

    def block(slab, offset):
        return lax.dynamic_slice_in_dim(slab, (row ^ offset) * cols, cols, 1)

    def move(slab, offsets):
        for offset in offsets:
            pieces[offset] = block(slab, offset)
            if offset:
                pieces[offset] = from_xor(pieces[offset], ("z", "core"), offset)

    far = list(range(n_row // 2, n_row))
    near = list(range(n_row // 2 - 1, -1, -1))
    move(states, far[:1])

    col = lax.axis_index("col")
    feature_index = col * width_local + jnp.arange(width_local, dtype=jnp.int32)
    omega = sketch_table(sketch_base[0], feature_index, RANK)
    z = lax.dot_general(
        omega, states, (((0,), (1,)), ((), ())), preferred_element_type=jnp.float32
    )
    for bit in bits(n_col):
        z = z + from_xor(z, ("col",), bit)
    z = z.reshape(RANK, n_col, chunk).transpose(1, 0, 2)
    z_bits = bits(n_z)[::-1]
    for k, bit in enumerate(z_bits):
        z = jnp.concatenate([z, from_xor(z, ("z",), bit)])
        slab, z = lax.optimization_barrier((states, z))
        if k == 0:
            move(slab, far[1:2])
    move(slab, far[2:] + near)
    z = z, from_xor(z, ("core",), 1)
    absolute_col = [("col", bit, False) for bit in bits(n_col)[::-1]]
    at_first = chunk_places([("z", bit, True) for bit in z_bits[::-1]] + absolute_col)
    relative_col = [("col", bit, True) for bit in bits(n_col)]
    at = chunk_places(relative_col + [("z", bit, False) for bit in z_bits])

    f32 = jnp.float32
    square = jax.ShapeDtypeStruct((RANK, RANK), f32)
    wide = jax.ShapeDtypeStruct((RANK, rows_total), jnp.bfloat16)
    orth_flops = 8 * 64 * 64 * rows_total * 6
    power_flops = 4 * 64 * rows_total * cols

    def sent_as(dtype):
        shape = (half, RANK, chunk)
        return jax.ShapeDtypeStruct(shape, f32), jax.ShapeDtypeStruct(shape, dtype)

    basis, upper = call(orth_kernel, (wide, square), orth_flops, at_first, *z)
    factor = upper.T * (1.0 / math.sqrt(rows_total * width_total))
    dtype = f32
    parts = call(power_kernel, sent_as(dtype), power_flops, at, basis, *pieces)
    for step in range(POWER - 1):
        z = gather_parts(sum_parts(*parts, dtype))
        dtype = jnp.bfloat16
        flops = orth_flops + power_flops
        parts = call(orth_power_kernel, sent_as(dtype), flops, at, *z, *pieces)
    z = gather_parts(sum_parts(*parts, dtype))
    loadings = jax.ShapeDtypeStruct((RANK, cols), f32)
    return call(last_kernel, loadings, orth_flops + power_flops, at, *z, *pieces).T, factor


def local_gram(basis):
    return jnp.dot(basis.T, basis, precision=lax.Precision.HIGHEST)


def orthonormal_block(sketch):
    whole_gram = lax.psum(local_gram(sketch), "row")
    identity = jnp.eye(RANK, dtype=jnp.float32)
    lower = jnp.linalg.cholesky(whole_gram + shift_ratio * jnp.trace(whole_gram) * identity)
    first = jax.scipy.linalg.solve_triangular(lower, sketch.T, lower=True).T
    lower_two = jnp.linalg.cholesky(lax.psum(local_gram(first), "row"))
    return jax.scipy.linalg.solve_triangular(lower_two, first.T, lower=True).T, lower


def per_device_slabs(sketch_base, states):
    width_local = states.shape[1]
    rows_total = states.shape[0] * lax.axis_size("row")
    width_total = width_local * lax.axis_size("col")
    feature_index = lax.axis_index("col") * width_local + jnp.arange(width_local, dtype=jnp.int32)
    omega = sketch_table(sketch_base[0], feature_index, RANK)

    def row_basis(right):
        partial_sketch = jnp.dot(states, right, preferred_element_type=jnp.float32)
        basis_new, lower = orthonormal_block(lax.psum(partial_sketch, "col"))
        return basis_new.astype(jnp.bfloat16), lower

    def back(basis):
        return lax.dot_general(
            states, basis, (((0,), (0,)), ((), ())), preferred_element_type=jnp.float32
        )

    basis, first_lower = row_basis(omega)
    factor = first_lower * (1.0 / math.sqrt(rows_total * width_total))
    for step in range(POWER):
        basis, unused = row_basis(lax.psum(back(basis), "row").astype(jnp.bfloat16))
    return lax.psum_scatter(back(basis), "row", scatter_dimension=0, tiled=True), factor


def solution(mesh):
    n_grp, n_row, n_col = (mesh.shape[name] for name in ("grp", "row", "col"))
    fits = n_row % 2 == 0 and n_row & (n_row - 1) == 0

    def run(sketch_base, states):
        rows_local = states.shape[0] // (n_grp * n_row)
        width_local = states.shape[1] // n_col
        tiled = rows_local % (n_col * LANES) == 0 and width_local % (n_row * LANES) == 0
        if fits and tiled:
            split = mesh.devices.reshape(n_grp, n_row // 2, 2, n_col)
            inner = jax.sharding.Mesh(split, ("grp", "z", "core", "col"))
            row, step = ("z", "core"), per_device_transposed
        else:
            inner, row, step = mesh, ("row",), per_device_slabs
        return jax.shard_map(
            step,
            mesh=inner,
            in_specs=(P("grp"), P(("grp",) + row, "col")),
            out_specs=(P(("col",) + row, "grp"), P("grp", None)),
            check_vma=False,
        )(sketch_base, states)

    return run
```

```python
import functools
import math

import jax
import jax.numpy as jnp
from jax import lax
from jax.experimental import pallas as pl
from jax.experimental.pallas import tpu as pltpu
from jax.sharding import PartitionSpec as P

RANK = 64
POWER = 4
LANES = 128
SUB = 8


shift_ratio = 0.005


def scramble(value):
    value = value ^ jnp.right_shift(value, 16) & 65535
    value = value * 73244475
    value = value ^ jnp.right_shift(value, 16) & 65535
    value = value * 73244475
    value = value ^ jnp.right_shift(value, 16) & 65535
    return value


def sketch_table(base_value, feature_index, rank):
    counter = feature_index[:, None] * rank + jnp.arange(rank, dtype=jnp.int32)[None, :]
    offset = scramble(base_value)
    total = jnp.zeros(counter.shape, jnp.float32)
    for j in range(4):
        hashed = scramble(counter * 4 + j + offset)
        total = total + (hashed & 16777215).astype(jnp.float32) * (1.0 / 16777216.0)
    return ((total - 2.0) * 1.7320508).astype(jnp.bfloat16)


def terms_of(value):
    if value.dtype == jnp.bfloat16:
        return [value]
    high = value.astype(jnp.bfloat16)
    rest = value - high.astype(jnp.float32)
    middle = rest.astype(jnp.bfloat16)
    low = (rest - middle.astype(jnp.float32)).astype(jnp.bfloat16)
    return [high, middle, low]


def dot_nn(left, right):
    return lax.dot_general(
        left, right, (((1,), (0,)), ((), ())), preferred_element_type=jnp.float32
    )


def dot_nt(left, right):
    return lax.dot_general(
        left, right, (((1,), (1,)), ((), ())), preferred_element_type=jnp.float32
    )


def small_times_wide(small, wide):
    left, right = terms_of(small), terms_of(wide)
    pairs = [(i, d - i) for d in (2, 1, 0) for i in range(d + 1)]
    pairs = [(i, j) for i, j in pairs if i < len(left) and j < len(right)]
    return dot_nn(
        jnp.concatenate([left[i] for i, unused in pairs], axis=1),
        jnp.concatenate([right[j] for unused, j in pairs], axis=0),
    )


def gram_of(wide):
    terms = terms_of(wide)
    if len(terms) == 1:
        return dot_nt(terms[0], terms[0])
    rank = wide.shape[0]
    stacked = jnp.concatenate(terms, axis=0)
    both = dot_nt(stacked, stacked)
    cross = both[rank : 2 * rank, :rank] + both[2 * rank :, :rank]
    return both[:rank, :rank] + ((cross + cross.T) + both[rank : 2 * rank, rank : 2 * rank])


def eliminate(matrix):
    size = matrix.shape[0]
    blocks = size // SUB
    row_index = lax.broadcasted_iota(jnp.int32, (SUB, 2 * size), 0)
    square_row = lax.broadcasted_iota(jnp.int32, (SUB, size), 0)
    square_col = lax.broadcasted_iota(jnp.int32, (SUB, size), 1)
    work = []
    for i in range(blocks):
        unit = jnp.where(square_col == square_row + SUB * i, 1.0, 0.0).astype(jnp.float32)
        work.append(jnp.concatenate([matrix[SUB * i : SUB * (i + 1), :], unit], axis=1))

    def everywhere(row):
        return jnp.broadcast_to(row, (SUB, 2 * size))

    rows = []
    for b in range(blocks):
        columns = {
            i: [everywhere(work[i][:, SUB * b + j : SUB * b + j + 1]) for j in range(SUB)]
            for i in range(b, blocks)
        }
        entry = [
            [everywhere(columns[b][j][i : i + 1, :]) if i <= j else None for j in range(SUB)]
            for i in range(SUB)
        ]
        row = [everywhere(work[b][k : k + 1, :]) for k in range(SUB)]
        reciprocal = []
        for k in range(SUB):
            reciprocal.append(1.0 / entry[k][k])
            for i in range(k + 1, SUB):
                factor = entry[k][i] * reciprocal[k]
                for j in range(i, SUB):
                    entry[i][j] = entry[i][j] - factor * entry[k][j]
                row[i] = row[i] - factor * row[k]
        for i in range(b + 1, blocks):
            for k in range(SUB):
                factor = columns[i][k] * reciprocal[k]
                for j in range(k + 1, SUB):
                    columns[i][j] = columns[i][j] - factor * entry[k][j]
                work[i] = work[i] - factor * row[k]
        scaled = row[0] * lax.rsqrt(entry[0][0])
        for k in range(1, SUB):
            scaled = jnp.where(row_index == k, row[k] * lax.rsqrt(entry[k][k]), scaled)
        rows.append(scaled)
    both = jnp.concatenate(rows, axis=0)
    keep = lax.broadcasted_iota(jnp.int32, (size, size), 1) >= lax.broadcasted_iota(
        jnp.int32, (size, size), 0
    )
    return jnp.where(keep, both[:, :size], 0.0), both[:, size:]


def shifted(whole_gram, trace):
    size = whole_gram.shape[0]
    diagonal = lax.broadcasted_iota(jnp.int32, (size, size), 0) == lax.broadcasted_iota(
        jnp.int32, (size, size), 1
    )
    return jnp.where(diagonal, whole_gram + shift_ratio * trace, whole_gram)


def sum_of_squares(wide):
    wide = wide.astype(jnp.float32)
    by_row = jnp.sum(wide * wide, axis=0, keepdims=True)
    return jnp.sum(by_row, axis=1, keepdims=True)


def wide_of(at_ref, z_refs):
    half = z_refs[0].shape[0]
    n_col = at_ref.shape[0] // half
    chunks = [z_refs[i // n_col % 2][at_ref[i]] for i in range(at_ref.shape[0])]
    return jnp.concatenate(chunks, axis=1)


def narrow_basis(at_ref, z_refs):
    wide = wide_of(at_ref, z_refs)
    upper, inverse_one = eliminate(shifted(gram_of(wide), sum_of_squares(wide)))
    first = small_times_wide(inverse_one, wide)
    unused, inverse_two = eliminate(gram_of(first))
    return small_times_wide(inverse_two, first).astype(jnp.bfloat16), upper


def times_slab(basis, a_refs):
    rows = a_refs[0].shape[0]
    pieces = [
        dot_nn(basis[:, rows * s : rows * (s + 1)], a_ref[...]) for s, a_ref in enumerate(a_refs)
    ]
    return functools.reduce(jnp.add, pieces)


def power_body(basis, a_refs, at_ref, part_refs):
    weights = times_slab(basis, a_refs).astype(jnp.bfloat16)
    width = part_refs[0].shape[2]
    n_col = at_ref.shape[0] // len(a_refs)
    for s, a_ref in enumerate(a_refs):
        forth = dot_nt(weights, a_ref[...])
        target = part_refs[s % 2]
        for c in range(n_col):
            block = forth[:, width * c : width * (c + 1)]
            target[at_ref[s * n_col + c]] = block.astype(target.dtype)


def orth_kernel(at_ref, z_ref, other_ref, basis_ref, upper_ref):
    basis_ref[...], upper_ref[...] = narrow_basis(at_ref, (z_ref, other_ref))


def power_kernel(at_ref, basis_ref, *refs):
    power_body(basis_ref[...], refs[:-2], at_ref, refs[-2:])


def orth_power_kernel(at_ref, z_ref, other_ref, *refs):
    basis, unused = narrow_basis(at_ref, (z_ref, other_ref))
    power_body(basis, refs[:-2], at_ref, refs[-2:])


def last_kernel(at_ref, z_ref, other_ref, *refs):
    basis, unused = narrow_basis(at_ref, (z_ref, other_ref))
    refs[-1][...] = times_slab(basis, refs[:-1])


def call(kernel, out_shapes, flops, at, *operands):
    moved = sum(x.size * x.dtype.itemsize for x in operands)
    return pl.pallas_call(
        kernel,
        out_shape=out_shapes,
        in_specs=[pl.BlockSpec(memory_space=pltpu.SMEM)]
        + [pl.BlockSpec(memory_space=pltpu.VMEM)] * len(operands),
        out_specs=jax.tree.map(lambda _: pl.BlockSpec(memory_space=pltpu.VMEM), out_shapes),
        compiler_params=pltpu.CompilerParams(vmem_limit_bytes=40 * 1024 * 1024),
        cost_estimate=pl.CostEstimate(flops=flops, bytes_accessed=moved, transcendentals=0),
    )(at, *operands)


def bits(size):
    return [1 << k for k in range(size.bit_length() - 1)]


def from_xor(value, axis, offset):
    size = math.prod(lax.axis_size(name) for name in axis)
    return lax.ppermute(value, axis, [(i, i ^ offset) for i in range(size)])


def sum_parts(keep, send, dtype):
    total = keep + from_xor(send, ("core",), 1).astype(jnp.float32)
    for bit in bits(lax.axis_size("col")):
        half = total.shape[0] // 2
        other = from_xor(total[half:].astype(dtype), ("col",), bit)
        total = total[:half] + other.astype(jnp.float32)
    for bit in bits(lax.axis_size("z")):
        mine = total.astype(dtype)
        total = mine.astype(jnp.float32) + from_xor(mine, ("z",), bit).astype(jnp.float32)
    return total.astype(dtype)


def gather_parts(own):
    for bit in bits(lax.axis_size("col"))[::-1]:
        own = jnp.concatenate([own, from_xor(own, ("col",), bit)])
    return own, from_xor(own, ("core",), 1)


def chunk_places(digits):
    n_z, n_col = lax.axis_size("z"), lax.axis_size("col")
    index = jnp.arange(n_z * 2 * n_col, dtype=jnp.int32)
    z_at, col_at = lax.axis_index("z"), lax.axis_index("col")
    column = index % n_col
    relative = {"z": index // (2 * n_col), "col": column ^ col_at}
    absolute = {"z": relative["z"] ^ z_at, "col": column}
    place = jnp.zeros_like(index)
    for axis, bit, is_relative in digits:
        place = place * 2 + ((relative if is_relative else absolute)[axis] // bit) % 2
    return place.astype(jnp.int32)


def per_device_transposed(sketch_base, states):
    n_z, n_core, n_col = lax.axis_size("z"), lax.axis_size("core"), lax.axis_size("col")
    n_row = n_z * n_core
    rows_local, width_local = states.shape
    rows_total, width_total = rows_local * n_row, width_local * n_col
    chunk = rows_local // n_col
    cols = width_local // n_row
    half = n_z * n_col
    row = lax.axis_index("z") * n_core + lax.axis_index("core")
    pieces = [None] * n_row

    def block(slab, offset):
        return lax.dynamic_slice_in_dim(slab, (row ^ offset) * cols, cols, 1)

    def move(slab, offsets):
        for offset in offsets:
            pieces[offset] = block(slab, offset)
            if offset:
                pieces[offset] = from_xor(pieces[offset], ("z", "core"), offset)

    far = list(range(n_row // 2, n_row))
    near = list(range(n_row // 2 - 1, -1, -1))
    pieces[far[0]] = block(states, far[0])
    slab, pieces[far[0]] = lax.optimization_barrier((states, pieces[far[0]]))
    pieces[far[0]] = from_xor(pieces[far[0]], ("z", "core"), far[0])

    col = lax.axis_index("col")
    feature_index = col * width_local + jnp.arange(width_local, dtype=jnp.int32)
    omega = sketch_table(sketch_base[0], feature_index, RANK)
    z = lax.dot_general(omega, slab, (((0,), (1,)), ((), ())), preferred_element_type=jnp.float32)
    for bit in bits(n_col):
        z = z + from_xor(z, ("col",), bit)
    z = z.reshape(RANK, n_col, chunk).transpose(1, 0, 2)
    z, pieces[far[0]], slab = lax.optimization_barrier((z, pieces[far[0]], slab))
    move(slab, far[1:2])
    z_bits = bits(n_z)[::-1]
    for k, bit in enumerate(z_bits):
        z = jnp.concatenate([z, from_xor(z, ("z",), bit)])
        z, slab = lax.optimization_barrier((z, slab))
        move(slab, far[2:3] if k == 0 else [])
    move(slab, far[3:])
    z = z, from_xor(z, ("core",), 1)
    absolute_col = [("col", bit, False) for bit in bits(n_col)[::-1]]
    at_first = chunk_places([("z", bit, True) for bit in z_bits[::-1]] + absolute_col)
    relative_col = [("col", bit, True) for bit in bits(n_col)]
    at = chunk_places(relative_col + [("z", bit, False) for bit in z_bits])

    f32 = jnp.float32
    square = jax.ShapeDtypeStruct((RANK, RANK), f32)
    wide = jax.ShapeDtypeStruct((RANK, rows_total), jnp.bfloat16)
    orth_flops = 8 * 64 * 64 * rows_total * 6
    power_flops = 4 * 64 * rows_total * cols

    def sent_as(dtype):
        shape = (half, RANK, chunk)
        return jax.ShapeDtypeStruct(shape, f32), jax.ShapeDtypeStruct(shape, dtype)

    basis, upper = call(orth_kernel, (wide, square), orth_flops, at_first, *z)
    basis, slab = lax.optimization_barrier((basis, slab))
    move(slab, near)
    factor = upper.T * (1.0 / math.sqrt(rows_total * width_total))
    dtype = f32
    parts = call(power_kernel, sent_as(dtype), power_flops, at, basis, *pieces)
    for step in range(POWER - 1):
        z = gather_parts(sum_parts(*parts, dtype))
        dtype = jnp.bfloat16
        flops = orth_flops + power_flops
        parts = call(orth_power_kernel, sent_as(dtype), flops, at, *z, *pieces)
    z = gather_parts(sum_parts(*parts, dtype))
    loadings = jax.ShapeDtypeStruct((RANK, cols), f32)
    return call(last_kernel, loadings, orth_flops + power_flops, at, *z, *pieces).T, factor


def local_gram(basis):
    return jnp.dot(basis.T, basis, precision=lax.Precision.HIGHEST)


def orthonormal_block(sketch):
    whole_gram = lax.psum(local_gram(sketch), "row")
    identity = jnp.eye(RANK, dtype=jnp.float32)
    lower = jnp.linalg.cholesky(whole_gram + shift_ratio * jnp.trace(whole_gram) * identity)
    first = jax.scipy.linalg.solve_triangular(lower, sketch.T, lower=True).T
    lower_two = jnp.linalg.cholesky(lax.psum(local_gram(first), "row"))
    return jax.scipy.linalg.solve_triangular(lower_two, first.T, lower=True).T, lower


def per_device_slabs(sketch_base, states):
    width_local = states.shape[1]
    rows_total = states.shape[0] * lax.axis_size("row")
    width_total = width_local * lax.axis_size("col")
    feature_index = lax.axis_index("col") * width_local + jnp.arange(width_local, dtype=jnp.int32)
    omega = sketch_table(sketch_base[0], feature_index, RANK)

    def row_basis(right):
        partial_sketch = jnp.dot(states, right, preferred_element_type=jnp.float32)
        basis_new, lower = orthonormal_block(lax.psum(partial_sketch, "col"))
        return basis_new.astype(jnp.bfloat16), lower

    def back(basis):
        return lax.dot_general(
            states, basis, (((0,), (0,)), ((), ())), preferred_element_type=jnp.float32
        )

    basis, first_lower = row_basis(omega)
    factor = first_lower * (1.0 / math.sqrt(rows_total * width_total))
    for step in range(POWER):
        basis, unused = row_basis(lax.psum(back(basis), "row").astype(jnp.bfloat16))
    return lax.psum_scatter(back(basis), "row", scatter_dimension=0, tiled=True), factor


def solution(mesh):
    n_grp, n_row, n_col = (mesh.shape[name] for name in ("grp", "row", "col"))
    fits = n_row % 2 == 0 and n_row & (n_row - 1) == 0

    def run(sketch_base, states):
        rows_local = states.shape[0] // (n_grp * n_row)
        width_local = states.shape[1] // n_col
        tiled = rows_local % (n_col * LANES) == 0 and width_local % (n_row * LANES) == 0
        if fits and tiled:
            split = mesh.devices.reshape(n_grp, n_row // 2, 2, n_col)
            inner = jax.sharding.Mesh(split, ("grp", "z", "core", "col"))
            row, step = ("z", "core"), per_device_transposed
        else:
            inner, row, step = mesh, ("row",), per_device_slabs
        return jax.shard_map(
            step,
            mesh=inner,
            in_specs=(P("grp"), P(("grp",) + row, "col")),
            out_specs=(P(("col",) + row, "grp"), P("grp", None)),
            check_vma=False,
        )(sketch_base, states)

    return run
```

```python
import functools
import math

import jax
import jax.numpy as jnp
from jax import lax
from jax.experimental import pallas as pl
from jax.experimental.pallas import tpu as pltpu
from jax.sharding import PartitionSpec as P

RANK = 64
POWER = 4
LANES = 128
SUB = 8
SKETCH_FLOPS = 30_000_000_000


shift_ratio = 0.005


def scramble(value):
    value = value ^ jnp.right_shift(value, 16) & 65535
    value = value * 73244475
    value = value ^ jnp.right_shift(value, 16) & 65535
    value = value * 73244475
    value = value ^ jnp.right_shift(value, 16) & 65535
    return value


def sketch_table(base_value, feature_index, rank):
    counter = feature_index[:, None] * rank + jnp.arange(rank, dtype=jnp.int32)[None, :]
    offset = scramble(base_value)
    total = jnp.zeros(counter.shape, jnp.float32)
    for j in range(4):
        hashed = scramble(counter * 4 + j + offset)
        total = total + (hashed & 16777215).astype(jnp.float32) * (1.0 / 16777216.0)
    return ((total - 2.0) * 1.7320508).astype(jnp.bfloat16)


def sketch_kernel(at_ref, states_ref, out_ref):
    rank = out_ref.shape[0]
    width = states_ref.shape[1]
    step = math.gcd(width, 512)
    out_ref[...] = jnp.zeros_like(out_ref)

    def body(i, carry):
        start = pl.multiple_of(i * step, step)
        feature = lax.broadcasted_iota(jnp.int32, (rank, step), 1) + (at_ref[1] + start)
        column = lax.broadcasted_iota(jnp.int32, (rank, step), 0)
        counter = (feature * rank + column) * 4 + at_ref[0]
        total = jnp.zeros((rank, step), jnp.float32)
        for j in range(4):
            hashed = scramble(counter + j)
            total = total + (hashed & 16777215).astype(jnp.float32) * (1.0 / 16777216.0)
        omega = ((total - 2.0) * 1.7320508).astype(jnp.bfloat16)
        out_ref[...] += dot_nt(omega, states_ref[:, pl.ds(start, step)])
        return carry

    lax.fori_loop(0, width // step, body, 0)


def terms_of(value):
    if value.dtype == jnp.bfloat16:
        return [value]
    high = value.astype(jnp.bfloat16)
    rest = value - high.astype(jnp.float32)
    middle = rest.astype(jnp.bfloat16)
    low = (rest - middle.astype(jnp.float32)).astype(jnp.bfloat16)
    return [high, middle, low]


def dot_nn(left, right):
    return lax.dot_general(
        left, right, (((1,), (0,)), ((), ())), preferred_element_type=jnp.float32
    )


def dot_nt(left, right):
    return lax.dot_general(
        left, right, (((1,), (1,)), ((), ())), preferred_element_type=jnp.float32
    )


def small_times_wide(small, wide):
    left, right = terms_of(small), terms_of(wide)
    pairs = [(i, d - i) for d in (2, 1, 0) for i in range(d + 1)]
    pairs = [(i, j) for i, j in pairs if i < len(left) and j < len(right)]
    return dot_nn(
        jnp.concatenate([left[i] for i, unused in pairs], axis=1),
        jnp.concatenate([right[j] for unused, j in pairs], axis=0),
    )


def gram_of(wide):
    terms = terms_of(wide)
    if len(terms) == 1:
        return dot_nt(terms[0], terms[0])
    rank = wide.shape[0]
    stacked = jnp.concatenate(terms, axis=0)
    both = dot_nt(stacked, stacked)
    cross = both[rank : 2 * rank, :rank] + both[2 * rank :, :rank]
    return both[:rank, :rank] + ((cross + cross.T) + both[rank : 2 * rank, rank : 2 * rank])


def eliminate(matrix):
    size = matrix.shape[0]
    blocks = size // SUB
    row_index = lax.broadcasted_iota(jnp.int32, (SUB, 2 * size), 0)
    square_row = lax.broadcasted_iota(jnp.int32, (SUB, size), 0)
    square_col = lax.broadcasted_iota(jnp.int32, (SUB, size), 1)
    work = []
    for i in range(blocks):
        unit = jnp.where(square_col == square_row + SUB * i, 1.0, 0.0).astype(jnp.float32)
        work.append(jnp.concatenate([matrix[SUB * i : SUB * (i + 1), :], unit], axis=1))
    rows = []
    for b in range(blocks):
        columns = [
            {
                i: jnp.broadcast_to(work[i][:, SUB * b + j : SUB * b + j + 1], (SUB, 2 * size))
                for i in range(b, blocks)
            }
            for j in range(SUB)
        ]
        pivots = jnp.zeros((SUB, 2 * size), jnp.float32)
        for k in range(SUB):
            pivot = jnp.broadcast_to(columns[k][b][k : k + 1, :], (SUB, 2 * size))
            reciprocal = 1.0 / pivot
            pivots = jnp.where(row_index == k, pivot, pivots)
            work_row = jnp.broadcast_to(work[b][k : k + 1, :], (SUB, 2 * size))
            later = [
                jnp.broadcast_to(columns[j][b][k : k + 1, :], (SUB, 2 * size))
                for j in range(k + 1, SUB)
            ]
            for i in range(b, blocks):
                factor = columns[k][i] * reciprocal
                if i == b:
                    factor = jnp.where(row_index > k, factor, 0.0)
                for j in range(k + 1, SUB):
                    columns[j][i] = columns[j][i] - factor * later[j - k - 1]
                work[i] = work[i] - factor * work_row
        rows.append(work[b] * lax.rsqrt(pivots))
    both = jnp.concatenate(rows, axis=0)
    keep = lax.broadcasted_iota(jnp.int32, (size, size), 1) >= lax.broadcasted_iota(
        jnp.int32, (size, size), 0
    )
    return jnp.where(keep, both[:, :size], 0.0), both[:, size:]


def shifted(whole_gram):
    size = whole_gram.shape[0]
    diagonal = lax.broadcasted_iota(jnp.int32, (size, size), 0) == lax.broadcasted_iota(
        jnp.int32, (size, size), 1
    )
    on_diagonal = jnp.where(diagonal, whole_gram, 0.0)
    trace = jnp.sum(jnp.sum(on_diagonal, axis=1, keepdims=True), axis=0, keepdims=True)
    return jnp.where(diagonal, whole_gram + shift_ratio * trace, whole_gram)


def wide_of(at_ref, z_refs):
    half = z_refs[0].shape[0]
    n_col = at_ref.shape[0] // half
    chunks = [z_refs[i // n_col % 2][at_ref[i]] for i in range(at_ref.shape[0])]
    return jnp.concatenate(chunks, axis=1)


def narrow_basis(at_ref, z_refs):
    wide = wide_of(at_ref, z_refs)
    upper, inverse_one = eliminate(shifted(gram_of(wide)))
    first = small_times_wide(inverse_one, wide)
    unused, inverse_two = eliminate(gram_of(first))
    return small_times_wide(inverse_two, first).astype(jnp.bfloat16), upper


def times_slab(basis, a_refs):
    rows = a_refs[0].shape[0]
    pieces = [
        dot_nn(basis[:, rows * s : rows * (s + 1)], a_ref[...]) for s, a_ref in enumerate(a_refs)
    ]
    return functools.reduce(jnp.add, pieces)


def power_body(basis, a_refs, at_ref, part_refs):
    weights = times_slab(basis, a_refs).astype(jnp.bfloat16)
    width = part_refs[0].shape[2]
    n_col = at_ref.shape[0] // len(a_refs)
    for s, a_ref in enumerate(a_refs):
        forth = dot_nt(weights, a_ref[...])
        target = part_refs[s % 2]
        for c in range(n_col):
            block = forth[:, width * c : width * (c + 1)]
            target[at_ref[s * n_col + c]] = block.astype(target.dtype)


def orth_kernel(at_ref, z_ref, other_ref, basis_ref, upper_ref):
    basis_ref[...], upper_ref[...] = narrow_basis(at_ref, (z_ref, other_ref))


def power_kernel(at_ref, basis_ref, *refs):
    power_body(basis_ref[...], refs[:-2], at_ref, refs[-2:])


def orth_power_kernel(at_ref, z_ref, other_ref, *refs):
    basis, unused = narrow_basis(at_ref, (z_ref, other_ref))
    power_body(basis, refs[:-2], at_ref, refs[-2:])


def last_kernel(at_ref, z_ref, other_ref, *refs):
    basis, unused = narrow_basis(at_ref, (z_ref, other_ref))
    refs[-1][...] = times_slab(basis, refs[:-1])


def call(kernel, out_shapes, flops, at, *operands):
    moved = sum(x.size * x.dtype.itemsize for x in operands)
    return pl.pallas_call(
        kernel,
        out_shape=out_shapes,
        in_specs=[pl.BlockSpec(memory_space=pltpu.SMEM)]
        + [pl.BlockSpec(memory_space=pltpu.VMEM)] * len(operands),
        out_specs=jax.tree.map(lambda _: pl.BlockSpec(memory_space=pltpu.VMEM), out_shapes),
        compiler_params=pltpu.CompilerParams(vmem_limit_bytes=40 * 1024 * 1024),
        cost_estimate=pl.CostEstimate(flops=flops, bytes_accessed=moved, transcendentals=0),
    )(at, *operands)


def bits(size):
    return [1 << k for k in range(size.bit_length() - 1)]


def from_xor(value, axis, offset):
    size = math.prod(lax.axis_size(name) for name in axis)
    return lax.ppermute(value, axis, [(i, i ^ offset) for i in range(size)])


def sum_parts(keep, send, dtype):
    total = keep + from_xor(send, ("core",), 1).astype(jnp.float32)
    for bit in bits(lax.axis_size("col")):
        half = total.shape[0] // 2
        other = from_xor(total[half:].astype(dtype), ("col",), bit)
        total = total[:half] + other.astype(jnp.float32)
    for bit in bits(lax.axis_size("z")):
        mine = total.astype(dtype)
        total = mine.astype(jnp.float32) + from_xor(mine, ("z",), bit).astype(jnp.float32)
    return total.astype(dtype)


def gather_parts(own):
    for bit in bits(lax.axis_size("col"))[::-1]:
        own = jnp.concatenate([own, from_xor(own, ("col",), bit)])
    return own, from_xor(own, ("core",), 1)


def chunk_places(digits):
    n_z, n_col = lax.axis_size("z"), lax.axis_size("col")
    index = jnp.arange(n_z * 2 * n_col, dtype=jnp.int32)
    z_at, col_at = lax.axis_index("z"), lax.axis_index("col")
    column = index % n_col
    relative = {"z": index // (2 * n_col), "col": column ^ col_at}
    absolute = {"z": relative["z"] ^ z_at, "col": column}
    place = jnp.zeros_like(index)
    for axis, bit, is_relative in digits:
        place = place * 2 + ((relative if is_relative else absolute)[axis] // bit) % 2
    return place.astype(jnp.int32)


def per_device_transposed(sketch_base, states):
    n_z, n_core, n_col = lax.axis_size("z"), lax.axis_size("core"), lax.axis_size("col")
    n_row = n_z * n_core
    rows_local, width_local = states.shape
    rows_total, width_total = rows_local * n_row, width_local * n_col
    chunk = rows_local // n_col
    cols = width_local // n_row
    half = n_z * n_col
    row = lax.axis_index("z") * n_core + lax.axis_index("core")
    pieces = [None] * n_row

    def block(slab, offset):
        return lax.dynamic_slice_in_dim(slab, (row ^ offset) * cols, cols, 1)

    def move(slab, offsets):
        for offset in offsets:
            pieces[offset] = block(slab, offset)
            if offset:
                pieces[offset] = from_xor(pieces[offset], ("z", "core"), offset)

    far = list(range(n_row // 2, n_row))
    near = list(range(n_row // 2 - 1, -1, -1))
    rounds = [far[:1] + near[1:], far[1:2] + near[:1]]
    rounds += [[offset] for offset in far[2:]]

    def after_round(value):
        if not rounds:
            return value
        offsets = rounds.pop(0)
        move(slab[0], offsets)
        moved = [pieces[offset] for offset in offsets]
        value, slab[0], moved = lax.optimization_barrier((value, slab[0], moved))
        for offset, piece in zip(offsets, moved):
            pieces[offset] = piece
        return value

    slab = [states]

    f32 = jnp.float32
    at_sketch = jnp.stack([scramble(sketch_base[0]), lax.axis_index("col") * width_local])
    z = call(
        sketch_kernel,
        jax.ShapeDtypeStruct((RANK, rows_local), f32),
        SKETCH_FLOPS,
        at_sketch.astype(jnp.int32),
        states,
    )
    z = after_round(z)
    for bit in bits(n_col):
        z = z + from_xor(z, ("col",), bit)
    z = z.reshape(RANK, n_col, chunk).transpose(1, 0, 2)
    z_bits = bits(n_z)[::-1]
    for bit in z_bits:
        z = after_round(z)
        z = jnp.concatenate([z, from_xor(z, ("z",), bit)])
    for offsets in rounds:
        move(slab[0], offsets)
    z = z, from_xor(z, ("core",), 1)
    absolute_col = [("col", bit, False) for bit in bits(n_col)[::-1]]
    at_first = chunk_places([("z", bit, True) for bit in z_bits[::-1]] + absolute_col)
    relative_col = [("col", bit, True) for bit in bits(n_col)]
    at = chunk_places(relative_col + [("z", bit, False) for bit in z_bits])

    square = jax.ShapeDtypeStruct((RANK, RANK), f32)
    wide = jax.ShapeDtypeStruct((RANK, rows_total), jnp.bfloat16)
    orth_flops = 8 * 64 * 64 * rows_total * 6
    power_flops = 4 * 64 * rows_total * cols

    def sent_as(dtype):
        shape = (half, RANK, chunk)
        return jax.ShapeDtypeStruct(shape, f32), jax.ShapeDtypeStruct(shape, dtype)

    basis, upper = call(orth_kernel, (wide, square), 1, at_first, *z)
    factor = upper.T * (1.0 / math.sqrt(rows_total * width_total))
    dtype = f32
    parts = call(power_kernel, sent_as(dtype), power_flops, at, basis, *pieces)
    for step in range(POWER - 1):
        z = gather_parts(sum_parts(*parts, dtype))
        dtype = jnp.bfloat16
        flops = orth_flops + power_flops
        parts = call(orth_power_kernel, sent_as(dtype), flops, at, *z, *pieces)
    z = gather_parts(sum_parts(*parts, dtype))
    loadings = jax.ShapeDtypeStruct((RANK, cols), f32)
    return call(last_kernel, loadings, orth_flops + power_flops, at, *z, *pieces).T, factor


def local_gram(basis):
    return jnp.dot(basis.T, basis, precision=lax.Precision.HIGHEST)


def orthonormal_block(sketch):
    whole_gram = lax.psum(local_gram(sketch), "row")
    identity = jnp.eye(RANK, dtype=jnp.float32)
    lower = jnp.linalg.cholesky(whole_gram + shift_ratio * jnp.trace(whole_gram) * identity)
    first = jax.scipy.linalg.solve_triangular(lower, sketch.T, lower=True).T
    lower_two = jnp.linalg.cholesky(lax.psum(local_gram(first), "row"))
    return jax.scipy.linalg.solve_triangular(lower_two, first.T, lower=True).T, lower


def per_device_slabs(sketch_base, states):
    width_local = states.shape[1]
    rows_total = states.shape[0] * lax.axis_size("row")
    width_total = width_local * lax.axis_size("col")
    feature_index = lax.axis_index("col") * width_local + jnp.arange(width_local, dtype=jnp.int32)
    omega = sketch_table(sketch_base[0], feature_index, RANK)

    def row_basis(right):
        partial_sketch = jnp.dot(states, right, preferred_element_type=jnp.float32)
        basis_new, lower = orthonormal_block(lax.psum(partial_sketch, "col"))
        return basis_new.astype(jnp.bfloat16), lower

    def back(basis):
        return lax.dot_general(
            states, basis, (((0,), (0,)), ((), ())), preferred_element_type=jnp.float32
        )

    basis, first_lower = row_basis(omega)
    factor = first_lower * (1.0 / math.sqrt(rows_total * width_total))
    for step in range(POWER):
        basis, unused = row_basis(lax.psum(back(basis), "row").astype(jnp.bfloat16))
    return lax.psum_scatter(back(basis), "row", scatter_dimension=0, tiled=True), factor


def solution(mesh):
    n_grp, n_row, n_col = (mesh.shape[name] for name in ("grp", "row", "col"))
    fits = n_row % 2 == 0 and n_row & (n_row - 1) == 0

    def run(sketch_base, states):
        rows_local = states.shape[0] // (n_grp * n_row)
        width_local = states.shape[1] // n_col
        tiled = rows_local % (n_col * LANES) == 0 and width_local % (n_row * LANES) == 0
        if fits and tiled:
            split = mesh.devices.reshape(n_grp, n_row // 2, 2, n_col)
            inner = jax.sharding.Mesh(split, ("grp", "z", "core", "col"))
            row, step = ("z", "core"), per_device_transposed
        else:
            inner, row, step = mesh, ("row",), per_device_slabs
        return jax.shard_map(
            step,
            mesh=inner,
            in_specs=(P("grp"), P(("grp",) + row, "col")),
            out_specs=(P(("col",) + row, "grp"), P("grp", None)),
            check_vma=False,
        )(sketch_base, states)

    return run
```

```python
import functools
import math

import jax
import jax.numpy as jnp
from jax import lax
from jax.experimental import pallas as pl
from jax.experimental.pallas import tpu as pltpu
from jax.sharding import PartitionSpec as P

RANK = 64
POWER = 4
LANES = 128
SUB = 8


shift_ratio = 0.005


def scramble(value):
    value = value ^ jnp.right_shift(value, 16) & 65535
    value = value * 73244475
    value = value ^ jnp.right_shift(value, 16) & 65535
    value = value * 73244475
    value = value ^ jnp.right_shift(value, 16) & 65535
    return value


def sketch_table(base_value, feature_index, rank):
    counter = feature_index[:, None] * rank + jnp.arange(rank, dtype=jnp.int32)[None, :]
    offset = scramble(base_value)
    total = jnp.zeros(counter.shape, jnp.float32)
    for j in range(4):
        hashed = scramble(counter * 4 + j + offset)
        total = total + (hashed & 16777215).astype(jnp.float32) * (1.0 / 16777216.0)
    return ((total - 2.0) * 1.7320508).astype(jnp.bfloat16)


def terms_of(value):
    if value.dtype == jnp.bfloat16:
        return [value]
    high = value.astype(jnp.bfloat16)
    rest = value - high.astype(jnp.float32)
    middle = rest.astype(jnp.bfloat16)
    low = (rest - middle.astype(jnp.float32)).astype(jnp.bfloat16)
    return [high, middle, low]


def dot_nn(left, right):
    return lax.dot_general(
        left, right, (((1,), (0,)), ((), ())), preferred_element_type=jnp.float32
    )


def dot_nt(left, right):
    return lax.dot_general(
        left, right, (((1,), (1,)), ((), ())), preferred_element_type=jnp.float32
    )


def small_times_wide(small, wide):
    left, right = terms_of(small), terms_of(wide)
    pairs = [(i, d - i) for d in (2, 1, 0) for i in range(d + 1)]
    pairs = [(i, j) for i, j in pairs if i < len(left) and j < len(right)]
    return dot_nn(
        jnp.concatenate([left[i] for i, unused in pairs], axis=1),
        jnp.concatenate([right[j] for unused, j in pairs], axis=0),
    )


def gram_of(wide):
    terms = terms_of(wide)
    if len(terms) == 1:
        return dot_nt(terms[0], terms[0])
    rank = wide.shape[0]
    stacked = jnp.concatenate(terms, axis=0)
    both = dot_nt(stacked, stacked)
    cross = both[rank : 2 * rank, :rank] + both[2 * rank :, :rank]
    return both[:rank, :rank] + ((cross + cross.T) + both[rank : 2 * rank, rank : 2 * rank])


def eliminate(matrix):
    size = matrix.shape[0]
    blocks = size // SUB
    row_index = lax.broadcasted_iota(jnp.int32, (SUB, 2 * size), 0)
    square_row = lax.broadcasted_iota(jnp.int32, (SUB, size), 0)
    square_col = lax.broadcasted_iota(jnp.int32, (SUB, size), 1)
    work = []
    for i in range(blocks):
        unit = jnp.where(square_col == square_row + SUB * i, 1.0, 0.0).astype(jnp.float32)
        work.append(jnp.concatenate([matrix[SUB * i : SUB * (i + 1), :], unit], axis=1))
    rows = []
    for b in range(blocks):
        columns = [
            {
                i: jnp.broadcast_to(work[i][:, SUB * b + j : SUB * b + j + 1], (SUB, 2 * size))
                for i in range(b, blocks)
            }
            for j in range(SUB)
        ]
        pivots = jnp.zeros((SUB, 2 * size), jnp.float32)
        for k in range(SUB):
            pivot = jnp.broadcast_to(columns[k][b][k : k + 1, :], (SUB, 2 * size))
            reciprocal = pl.reciprocal(pivot, approx=True)
            reciprocal = reciprocal * (2.0 - pivot * reciprocal)
            pivots = jnp.where(row_index == k, pivot, pivots)
            work_row = jnp.broadcast_to(work[b][k : k + 1, :], (SUB, 2 * size))
            later = [
                jnp.broadcast_to(columns[j][b][k : k + 1, :], (SUB, 2 * size))
                for j in range(k + 1, SUB)
            ]
            for i in range(b, blocks):
                factor = columns[k][i] * reciprocal
                if i == b:
                    factor = jnp.where(row_index > k, factor, 0.0)
                for j in range(k + 1, SUB):
                    columns[j][i] = columns[j][i] - factor * later[j - k - 1]
                work[i] = work[i] - factor * work_row
        rows.append(work[b] * lax.rsqrt(pivots))
    both = jnp.concatenate(rows, axis=0)
    keep = lax.broadcasted_iota(jnp.int32, (size, size), 1) >= lax.broadcasted_iota(
        jnp.int32, (size, size), 0
    )
    return jnp.where(keep, both[:, :size], 0.0), both[:, size:]


def shifted(whole_gram):
    size = whole_gram.shape[0]
    diagonal = lax.broadcasted_iota(jnp.int32, (size, size), 0) == lax.broadcasted_iota(
        jnp.int32, (size, size), 1
    )
    on_diagonal = jnp.where(diagonal, whole_gram, 0.0)
    trace = jnp.sum(jnp.sum(on_diagonal, axis=1, keepdims=True), axis=0, keepdims=True)
    return jnp.where(diagonal, whole_gram + shift_ratio * trace, whole_gram)


def wide_of(at_ref, z_refs):
    half = z_refs[0].shape[0]
    n_col = at_ref.shape[0] // half
    chunks = [z_refs[i // n_col % 2][at_ref[i]] for i in range(at_ref.shape[0])]
    return jnp.concatenate(chunks, axis=1)


def narrow_basis(at_ref, z_refs):
    wide = wide_of(at_ref, z_refs)
    upper, inverse_one = eliminate(shifted(gram_of(wide)))
    first = small_times_wide(inverse_one, wide)
    unused, inverse_two = eliminate(gram_of(first))
    return small_times_wide(inverse_two, first).astype(jnp.bfloat16), upper


def times_slab(basis, a_refs):
    rows = a_refs[0].shape[0]
    pieces = [
        dot_nn(basis[:, rows * s : rows * (s + 1)], a_ref[...]) for s, a_ref in enumerate(a_refs)
    ]
    return functools.reduce(jnp.add, pieces)


def power_body(basis, a_refs, at_ref, part_refs):
    weights = times_slab(basis, a_refs).astype(jnp.bfloat16)
    width = part_refs[0].shape[2]
    n_col = at_ref.shape[0] // len(a_refs)
    for s, a_ref in enumerate(a_refs):
        forth = dot_nt(weights, a_ref[...])
        target = part_refs[s % 2]
        for c in range(n_col):
            block = forth[:, width * c : width * (c + 1)]
            target[at_ref[s * n_col + c]] = block.astype(target.dtype)


def orth_kernel(at_ref, z_ref, other_ref, basis_ref, upper_ref):
    basis_ref[...], upper_ref[...] = narrow_basis(at_ref, (z_ref, other_ref))


def power_kernel(at_ref, basis_ref, *refs):
    power_body(basis_ref[...], refs[:-2], at_ref, refs[-2:])


def orth_power_kernel(at_ref, z_ref, other_ref, *refs):
    basis, unused = narrow_basis(at_ref, (z_ref, other_ref))
    power_body(basis, refs[:-2], at_ref, refs[-2:])


def last_kernel(at_ref, z_ref, other_ref, *refs):
    basis, unused = narrow_basis(at_ref, (z_ref, other_ref))
    refs[-1][...] = times_slab(basis, refs[:-1])


def call(kernel, out_shapes, flops, at, *operands):
    moved = sum(x.size * x.dtype.itemsize for x in operands)
    return pl.pallas_call(
        kernel,
        out_shape=out_shapes,
        in_specs=[pl.BlockSpec(memory_space=pltpu.SMEM)]
        + [pl.BlockSpec(memory_space=pltpu.VMEM)] * len(operands),
        out_specs=jax.tree.map(lambda _: pl.BlockSpec(memory_space=pltpu.VMEM), out_shapes),
        compiler_params=pltpu.CompilerParams(vmem_limit_bytes=40 * 1024 * 1024),
        cost_estimate=pl.CostEstimate(flops=flops, bytes_accessed=moved, transcendentals=0),
    )(at, *operands)


def bits(size):
    return [1 << k for k in range(size.bit_length() - 1)]


def from_xor(value, axis, offset):
    size = math.prod(lax.axis_size(name) for name in axis)
    return lax.ppermute(value, axis, [(i, i ^ offset) for i in range(size)])


def sum_parts(keep, send, dtype):
    total = keep + from_xor(send, ("core",), 1).astype(jnp.float32)
    for bit in bits(lax.axis_size("col")):
        half = total.shape[0] // 2
        other = from_xor(total[half:].astype(dtype), ("col",), bit)
        total = total[:half] + other.astype(jnp.float32)
    for bit in bits(lax.axis_size("z")):
        mine = total.astype(dtype)
        total = mine.astype(jnp.float32) + from_xor(mine, ("z",), bit).astype(jnp.float32)
    return total.astype(dtype)


def gather_parts(own):
    for bit in bits(lax.axis_size("col"))[::-1]:
        own = jnp.concatenate([own, from_xor(own, ("col",), bit)])
    return own, from_xor(own, ("core",), 1)


def chunk_places(digits):
    n_z, n_col = lax.axis_size("z"), lax.axis_size("col")
    index = jnp.arange(n_z * 2 * n_col, dtype=jnp.int32)
    z_at, col_at = lax.axis_index("z"), lax.axis_index("col")
    column = index % n_col
    relative = {"z": index // (2 * n_col), "col": column ^ col_at}
    absolute = {"z": relative["z"] ^ z_at, "col": column}
    place = jnp.zeros_like(index)
    for axis, bit, is_relative in digits:
        place = place * 2 + ((relative if is_relative else absolute)[axis] // bit) % 2
    return place.astype(jnp.int32)


def per_device_transposed(sketch_base, states):
    n_z, n_core, n_col = lax.axis_size("z"), lax.axis_size("core"), lax.axis_size("col")
    n_row = n_z * n_core
    rows_local, width_local = states.shape
    rows_total, width_total = rows_local * n_row, width_local * n_col
    chunk = rows_local // n_col
    cols = width_local // n_row
    half = n_z * n_col
    row = lax.axis_index("z") * n_core + lax.axis_index("core")
    pieces = [None] * n_row

    def block(slab, offset):
        return lax.dynamic_slice_in_dim(slab, (row ^ offset) * cols, cols, 1)

    def move(slab, offsets):
        for offset in offsets:
            pieces[offset] = block(slab, offset)
            if offset:
                pieces[offset] = from_xor(pieces[offset], ("z", "core"), offset)

    far = list(range(n_row // 2, n_row))
    near = list(range(n_row // 2 - 1, -1, -1))

    col = lax.axis_index("col")
    feature_index = col * width_local + jnp.arange(width_local, dtype=jnp.int32)
    omega = sketch_table(sketch_base[0], feature_index, RANK)
    z = lax.dot_general(
        omega, states, (((0,), (1,)), ((), ())), preferred_element_type=jnp.float32
    )
    for bit in bits(n_col):
        z = z + from_xor(z, ("col",), bit)
    z = z.reshape(RANK, n_col, chunk).transpose(1, 0, 2)
    z_bits = bits(n_z)[::-1]
    for k, bit in enumerate(z_bits):
        z = jnp.concatenate([z, from_xor(z, ("z",), bit)])
        if k == 0:
            z, slab = lax.optimization_barrier((z, states))
            move(slab, far + near)
    z = z, from_xor(z, ("core",), 1)
    held = far[:1] + near[:1]
    z, moved = lax.optimization_barrier((z, [pieces[offset] for offset in held]))
    for offset, piece in zip(held, moved):
        pieces[offset] = piece
    absolute_col = [("col", bit, False) for bit in bits(n_col)[::-1]]
    at_first = chunk_places([("z", bit, True) for bit in z_bits[::-1]] + absolute_col)
    relative_col = [("col", bit, True) for bit in bits(n_col)]
    at = chunk_places(relative_col + [("z", bit, False) for bit in z_bits])

    f32 = jnp.float32
    square = jax.ShapeDtypeStruct((RANK, RANK), f32)
    wide = jax.ShapeDtypeStruct((RANK, rows_total), jnp.bfloat16)
    orth_flops = 8 * 64 * 64 * rows_total * 6
    power_flops = 4 * 64 * rows_total * cols

    def sent_as(dtype):
        shape = (half, RANK, chunk)
        return jax.ShapeDtypeStruct(shape, f32), jax.ShapeDtypeStruct(shape, dtype)

    basis, upper = call(orth_kernel, (wide, square), orth_flops, at_first, *z)
    factor = upper.T * (1.0 / math.sqrt(rows_total * width_total))
    dtype = f32
    parts = call(power_kernel, sent_as(dtype), power_flops, at, basis, *pieces)
    for step in range(POWER - 1):
        z = gather_parts(sum_parts(*parts, dtype))
        dtype = jnp.bfloat16
        flops = orth_flops + power_flops
        parts = call(orth_power_kernel, sent_as(dtype), flops, at, *z, *pieces)
    z = gather_parts(sum_parts(*parts, dtype))
    loadings = jax.ShapeDtypeStruct((RANK, cols), f32)
    return call(last_kernel, loadings, orth_flops + power_flops, at, *z, *pieces).T, factor


def local_gram(basis):
    return jnp.dot(basis.T, basis, precision=lax.Precision.HIGHEST)


def orthonormal_block(sketch):
    whole_gram = lax.psum(local_gram(sketch), "row")
    identity = jnp.eye(RANK, dtype=jnp.float32)
    lower = jnp.linalg.cholesky(whole_gram + shift_ratio * jnp.trace(whole_gram) * identity)
    first = jax.scipy.linalg.solve_triangular(lower, sketch.T, lower=True).T
    lower_two = jnp.linalg.cholesky(lax.psum(local_gram(first), "row"))
    return jax.scipy.linalg.solve_triangular(lower_two, first.T, lower=True).T, lower


def per_device_slabs(sketch_base, states):
    width_local = states.shape[1]
    rows_total = states.shape[0] * lax.axis_size("row")
    width_total = width_local * lax.axis_size("col")
    feature_index = lax.axis_index("col") * width_local + jnp.arange(width_local, dtype=jnp.int32)
    omega = sketch_table(sketch_base[0], feature_index, RANK)

    def row_basis(right):
        partial_sketch = jnp.dot(states, right, preferred_element_type=jnp.float32)
        basis_new, lower = orthonormal_block(lax.psum(partial_sketch, "col"))
        return basis_new.astype(jnp.bfloat16), lower

    def back(basis):
        return lax.dot_general(
            states, basis, (((0,), (0,)), ((), ())), preferred_element_type=jnp.float32
        )

    basis, first_lower = row_basis(omega)
    factor = first_lower * (1.0 / math.sqrt(rows_total * width_total))
    for step in range(POWER):
        basis, unused = row_basis(lax.psum(back(basis), "row").astype(jnp.bfloat16))
    return lax.psum_scatter(back(basis), "row", scatter_dimension=0, tiled=True), factor


def solution(mesh):
    n_grp, n_row, n_col = (mesh.shape[name] for name in ("grp", "row", "col"))
    fits = n_row % 2 == 0 and n_row & (n_row - 1) == 0

    def run(sketch_base, states):
        rows_local = states.shape[0] // (n_grp * n_row)
        width_local = states.shape[1] // n_col
        tiled = rows_local % (n_col * LANES) == 0 and width_local % (n_row * LANES) == 0
        if fits and tiled:
            split = mesh.devices.reshape(n_grp, n_row // 2, 2, n_col)
            inner = jax.sharding.Mesh(split, ("grp", "z", "core", "col"))
            row, step = ("z", "core"), per_device_transposed
        else:
            inner, row, step = mesh, ("row",), per_device_slabs
        return jax.shard_map(
            step,
            mesh=inner,
            in_specs=(P("grp"), P(("grp",) + row, "col")),
            out_specs=(P(("col",) + row, "grp"), P("grp", None)),
            check_vma=False,
        )(sketch_base, states)

    return run
```

```python
import functools
import math

import jax
import jax.numpy as jnp
from jax import lax
from jax.experimental import pallas as pl
from jax.experimental.pallas import tpu as pltpu
from jax.sharding import PartitionSpec as P

RANK = 64
POWER = 4
LANES = 128
SUB = 8


shift_ratio = 0.005


def scramble(value):
    value = value ^ jnp.right_shift(value, 16) & 65535
    value = value * 73244475
    value = value ^ jnp.right_shift(value, 16) & 65535
    value = value * 73244475
    value = value ^ jnp.right_shift(value, 16) & 65535
    return value


def sketch_table(base_value, feature_index, rank):
    counter = feature_index[:, None] * rank + jnp.arange(rank, dtype=jnp.int32)[None, :]
    offset = scramble(base_value)
    total = jnp.zeros(counter.shape, jnp.float32)
    for j in range(4):
        hashed = scramble(counter * 4 + j + offset)
        total = total + (hashed & 16777215).astype(jnp.float32) * (1.0 / 16777216.0)
    return ((total - 2.0) * 1.7320508).astype(jnp.bfloat16)


def terms_of(value):
    if value.dtype == jnp.bfloat16:
        return [value]
    high = value.astype(jnp.bfloat16)
    rest = value - high.astype(jnp.float32)
    middle = rest.astype(jnp.bfloat16)
    low = (rest - middle.astype(jnp.float32)).astype(jnp.bfloat16)
    return [high, middle, low]


def dot_nn(left, right):
    return lax.dot_general(
        left, right, (((1,), (0,)), ((), ())), preferred_element_type=jnp.float32
    )


def dot_nt(left, right):
    return lax.dot_general(
        left, right, (((1,), (1,)), ((), ())), preferred_element_type=jnp.float32
    )


def small_times_wide(small, wide):
    left, right = terms_of(small), terms_of(wide)
    pairs = [(i, d - i) for d in (2, 1, 0) for i in range(d + 1)]
    pairs = [(i, j) for i, j in pairs if i < len(left) and j < len(right)]
    return dot_nn(
        jnp.concatenate([left[i] for i, unused in pairs], axis=1),
        jnp.concatenate([right[j] for unused, j in pairs], axis=0),
    )


def gram_of(wide):
    terms = terms_of(wide)
    if len(terms) == 1:
        return dot_nt(terms[0], terms[0])
    rank = wide.shape[0]
    stacked = jnp.concatenate(terms, axis=0)
    both = dot_nt(stacked, stacked)
    cross = both[rank : 2 * rank, :rank] + both[2 * rank :, :rank]
    return both[:rank, :rank] + ((cross + cross.T) + both[rank : 2 * rank, rank : 2 * rank])


def eliminate(matrix):
    size = matrix.shape[0]
    blocks = size // SUB
    row_index = lax.broadcasted_iota(jnp.int32, (SUB, 2 * size), 0)
    square_row = lax.broadcasted_iota(jnp.int32, (SUB, size), 0)
    square_col = lax.broadcasted_iota(jnp.int32, (SUB, size), 1)
    work = []
    for i in range(blocks):
        unit = jnp.where(square_col == square_row + SUB * i, 1.0, 0.0).astype(jnp.float32)
        work.append(jnp.concatenate([matrix[SUB * i : SUB * (i + 1), :], unit], axis=1))
    rows = []
    for b in range(blocks):
        columns = [
            {
                i: jnp.broadcast_to(work[i][:, SUB * b + j : SUB * b + j + 1], (SUB, 2 * size))
                for i in range(b, blocks)
            }
            for j in range(SUB)
        ]
        pivots = jnp.zeros((SUB, 2 * size), jnp.float32)
        for k in range(SUB):
            pivot = jnp.broadcast_to(columns[k][b][k : k + 1, :], (SUB, 2 * size))
            reciprocal = 1.0 / pivot
            pivots = jnp.where(row_index == k, pivot, pivots)
            work_row = jnp.broadcast_to(work[b][k : k + 1, :], (SUB, 2 * size))
            later = [
                jnp.broadcast_to(columns[j][b][k : k + 1, :], (SUB, 2 * size))
                for j in range(k + 1, SUB)
            ]
            for i in range(b, blocks):
                factor = columns[k][i] * reciprocal
                if i == b:
                    factor = jnp.where(row_index > k, factor, 0.0)
                for j in range(k + 1, SUB):
                    columns[j][i] = columns[j][i] - factor * later[j - k - 1]
                work[i] = work[i] - factor * work_row
        rows.append(work[b] * lax.rsqrt(pivots))
    both = jnp.concatenate(rows, axis=0)
    keep = lax.broadcasted_iota(jnp.int32, (size, size), 1) >= lax.broadcasted_iota(
        jnp.int32, (size, size), 0
    )
    return jnp.where(keep, both[:, :size], 0.0), both[:, size:]


def shifted(whole_gram):
    size = whole_gram.shape[0]
    diagonal = lax.broadcasted_iota(jnp.int32, (size, size), 0) == lax.broadcasted_iota(
        jnp.int32, (size, size), 1
    )
    on_diagonal = jnp.where(diagonal, whole_gram, 0.0)
    trace = jnp.sum(jnp.sum(on_diagonal, axis=1, keepdims=True), axis=0, keepdims=True)
    return jnp.where(diagonal, whole_gram + shift_ratio * trace, whole_gram)


def wide_of(at_ref, z_refs):
    half = z_refs[0].shape[0]
    n_col = at_ref.shape[0] // half
    chunks = [z_refs[i // n_col % 2][at_ref[i]] for i in range(at_ref.shape[0])]
    return jnp.concatenate(chunks, axis=1)


def narrow_basis(at_ref, z_refs):
    wide = wide_of(at_ref, z_refs)
    upper, inverse_one = eliminate(shifted(gram_of(wide)))
    first = small_times_wide(inverse_one, wide)
    unused, inverse_two = eliminate(gram_of(first))
    return small_times_wide(inverse_two, first).astype(jnp.bfloat16), upper


def power_body(basis, a, at_ref, part_refs):
    weights = dot_nn(basis, a).astype(jnp.bfloat16)
    forth = dot_nt(weights, a)
    half, unused, width = part_refs[0].shape
    n_col = at_ref.shape[0] // half
    for i in range(2 * half):
        target = part_refs[i // n_col % 2]
        target[at_ref[i]] = forth[:, width * i : width * (i + 1)].astype(target.dtype)


def orth_kernel(at_ref, z_ref, other_ref, basis_ref, upper_ref):
    basis_ref[...], upper_ref[...] = narrow_basis(at_ref, (z_ref, other_ref))


def power_kernel(at_ref, basis_ref, *refs):
    piece_refs, a_ref, part_refs = refs[:-3], refs[-3], refs[-2:]
    rows = piece_refs[0].shape[0]
    for s, piece_ref in enumerate(piece_refs):
        a_ref[rows * s : rows * (s + 1), :] = piece_ref[...]
    power_body(basis_ref[...], a_ref[...], at_ref, part_refs)


def orth_power_kernel(at_ref, z_ref, other_ref, a_ref, *part_refs):
    basis, unused = narrow_basis(at_ref, (z_ref, other_ref))
    power_body(basis, a_ref[...], at_ref, part_refs)


def last_kernel(at_ref, z_ref, other_ref, a_ref, out_ref):
    basis, unused = narrow_basis(at_ref, (z_ref, other_ref))
    out_ref[...] = dot_nn(basis, a_ref[...])


def call(kernel, out_shapes, flops, at, *operands):
    moved = sum(x.size * x.dtype.itemsize for x in operands)
    return pl.pallas_call(
        kernel,
        out_shape=out_shapes,
        in_specs=[pl.BlockSpec(memory_space=pltpu.SMEM)]
        + [pl.BlockSpec(memory_space=pltpu.VMEM)] * len(operands),
        out_specs=jax.tree.map(lambda _: pl.BlockSpec(memory_space=pltpu.VMEM), out_shapes),
        compiler_params=pltpu.CompilerParams(vmem_limit_bytes=40 * 1024 * 1024),
        cost_estimate=pl.CostEstimate(flops=flops, bytes_accessed=moved, transcendentals=0),
    )(at, *operands)


def bits(size):
    return [1 << k for k in range(size.bit_length() - 1)]


def from_xor(value, axis, offset):
    size = math.prod(lax.axis_size(name) for name in axis)
    return lax.ppermute(value, axis, [(i, i ^ offset) for i in range(size)])


def sum_parts(keep, send, dtype):
    total = keep + from_xor(send, ("core",), 1).astype(jnp.float32)
    for bit in bits(lax.axis_size("col")):
        half = total.shape[0] // 2
        other = from_xor(total[half:].astype(dtype), ("col",), bit)
        total = total[:half] + other.astype(jnp.float32)
    for bit in bits(lax.axis_size("z")):
        mine = total.astype(dtype)
        total = mine.astype(jnp.float32) + from_xor(mine, ("z",), bit).astype(jnp.float32)
    return total.astype(dtype)


def gather_parts(own):
    for bit in bits(lax.axis_size("col"))[::-1]:
        own = jnp.concatenate([own, from_xor(own, ("col",), bit)])
    return own, from_xor(own, ("core",), 1)


def chunk_places(digits):
    n_z, n_col = lax.axis_size("z"), lax.axis_size("col")
    index = jnp.arange(n_z * 2 * n_col, dtype=jnp.int32)
    z_at, col_at = lax.axis_index("z"), lax.axis_index("col")
    column = index % n_col
    relative = {"z": index // (2 * n_col), "col": column ^ col_at}
    absolute = {"z": relative["z"] ^ z_at, "col": column}
    place = jnp.zeros_like(index)
    for axis, bit, is_relative in digits:
        place = place * 2 + ((relative if is_relative else absolute)[axis] // bit) % 2
    return place.astype(jnp.int32)


def per_device_transposed(sketch_base, states):
    n_z, n_core, n_col = lax.axis_size("z"), lax.axis_size("core"), lax.axis_size("col")
    n_row = n_z * n_core
    rows_local, width_local = states.shape
    rows_total, width_total = rows_local * n_row, width_local * n_col
    chunk = rows_local // n_col
    cols = width_local // n_row
    half = n_z * n_col
    row = lax.axis_index("z") * n_core + lax.axis_index("core")
    pieces = [None] * n_row

    def block(slab, offset):
        return lax.dynamic_slice_in_dim(slab, (row ^ offset) * cols, cols, 1)

    def move(slab, offsets):
        for offset in offsets:
            pieces[offset] = block(slab, offset)
            if offset:
                pieces[offset] = from_xor(pieces[offset], ("z", "core"), offset)

    far = list(range(n_row // 2, n_row))
    near = list(range(2, n_row // 2))
    beside = [[1], near + far[:1]]

    def hold(value, offsets):
        move(states, offsets)
        value, moved = lax.optimization_barrier((value, [pieces[o] for o in offsets]))
        for o, piece in zip(offsets, moved):
            pieces[o] = piece
        return value

    col = lax.axis_index("col")
    feature_index = col * width_local + jnp.arange(width_local, dtype=jnp.int32)
    omega = sketch_table(sketch_base[0], feature_index, RANK)
    z = lax.dot_general(
        omega, states, (((0,), (1,)), ((), ())), preferred_element_type=jnp.float32
    )
    for bit in bits(n_col):
        z = z + from_xor(z, ("col",), bit)
    z = z.reshape(RANK, n_col, chunk).transpose(1, 0, 2)
    z_bits = bits(n_z)[::-1]
    for k, bit in enumerate(z_bits):
        z = hold(z, beside.pop(0)) if beside else z
        z = jnp.concatenate([z, from_xor(z, ("z",), bit)])
        if k == 0:
            z, slab = lax.optimization_barrier((z, states))
            move(slab, far[1:2])
    z, slab = lax.optimization_barrier((z, states))
    move(slab, far[2:] + [0] + [o for offsets in beside for o in offsets])
    z = z, from_xor(z, ("core",), 1)
    absolute_col = [("col", bit, False) for bit in bits(n_col)[::-1]]
    at_first = chunk_places([("z", bit, True) for bit in z_bits[::-1]] + absolute_col)
    relative_col = [("col", bit, True) for bit in bits(n_col)]
    at = chunk_places(relative_col + [("z", bit, False) for bit in z_bits])

    f32 = jnp.float32
    square = jax.ShapeDtypeStruct((RANK, RANK), f32)
    wide = jax.ShapeDtypeStruct((RANK, rows_total), jnp.bfloat16)
    orth_flops = 8 * 64 * 64 * rows_total * 6
    power_flops = 4 * 64 * rows_total * cols

    def sent_as(dtype):
        shape = (half, RANK, chunk)
        return jax.ShapeDtypeStruct(shape, f32), jax.ShapeDtypeStruct(shape, dtype)

    basis, upper = call(orth_kernel, (wide, square), orth_flops, at_first, *z)
    factor = upper.T * (1.0 / math.sqrt(rows_total * width_total))
    dtype = f32
    slab = jax.ShapeDtypeStruct((rows_total, cols), states.dtype)
    a, *parts = call(power_kernel, (slab,) + sent_as(dtype), power_flops, at, basis, *pieces)
    for step in range(POWER - 1):
        z = gather_parts(sum_parts(*parts, dtype))
        dtype = jnp.bfloat16
        flops = orth_flops + power_flops
        parts = call(orth_power_kernel, sent_as(dtype), flops, at, *z, a)
    z = gather_parts(sum_parts(*parts, dtype))
    loadings = jax.ShapeDtypeStruct((RANK, cols), f32)
    return call(last_kernel, loadings, orth_flops + power_flops, at, *z, a).T, factor


def local_gram(basis):
    return jnp.dot(basis.T, basis, precision=lax.Precision.HIGHEST)


def orthonormal_block(sketch):
    whole_gram = lax.psum(local_gram(sketch), "row")
    identity = jnp.eye(RANK, dtype=jnp.float32)
    lower = jnp.linalg.cholesky(whole_gram + shift_ratio * jnp.trace(whole_gram) * identity)
    first = jax.scipy.linalg.solve_triangular(lower, sketch.T, lower=True).T
    lower_two = jnp.linalg.cholesky(lax.psum(local_gram(first), "row"))
    return jax.scipy.linalg.solve_triangular(lower_two, first.T, lower=True).T, lower


def per_device_slabs(sketch_base, states):
    width_local = states.shape[1]
    rows_total = states.shape[0] * lax.axis_size("row")
    width_total = width_local * lax.axis_size("col")
    feature_index = lax.axis_index("col") * width_local + jnp.arange(width_local, dtype=jnp.int32)
    omega = sketch_table(sketch_base[0], feature_index, RANK)

    def row_basis(right):
        partial_sketch = jnp.dot(states, right, preferred_element_type=jnp.float32)
        basis_new, lower = orthonormal_block(lax.psum(partial_sketch, "col"))
        return basis_new.astype(jnp.bfloat16), lower

    def back(basis):
        return lax.dot_general(
            states, basis, (((0,), (0,)), ((), ())), preferred_element_type=jnp.float32
        )

    basis, first_lower = row_basis(omega)
    factor = first_lower * (1.0 / math.sqrt(rows_total * width_total))
    for step in range(POWER):
        basis, unused = row_basis(lax.psum(back(basis), "row").astype(jnp.bfloat16))
    return lax.psum_scatter(back(basis), "row", scatter_dimension=0, tiled=True), factor


def solution(mesh):
    n_grp, n_row, n_col = (mesh.shape[name] for name in ("grp", "row", "col"))
    fits = n_row % 2 == 0 and n_row & (n_row - 1) == 0

    def run(sketch_base, states):
        rows_local = states.shape[0] // (n_grp * n_row)
        width_local = states.shape[1] // n_col
        tiled = rows_local % (n_col * LANES) == 0 and width_local % (n_row * LANES) == 0
        if fits and tiled:
            split = mesh.devices.reshape(n_grp, n_row // 2, 2, n_col)
            inner = jax.sharding.Mesh(split, ("grp", "z", "core", "col"))
            row, step = ("z", "core"), per_device_transposed
        else:
            inner, row, step = mesh, ("row",), per_device_slabs
        return jax.shard_map(
            step,
            mesh=inner,
            in_specs=(P("grp"), P(("grp",) + row, "col")),
            out_specs=(P(("col",) + row, "grp"), P("grp", None)),
            check_vma=False,
        )(sketch_base, states)

    return run
```

```python
import functools
import math

import jax
import jax.numpy as jnp
from jax import lax
from jax.experimental import pallas as pl
from jax.experimental.pallas import tpu as pltpu
from jax.sharding import PartitionSpec as P

RANK = 64
POWER = 4
LANES = 128
SUB = 8


shift_ratio = 0.005


def scramble(value):
    value = value ^ jnp.right_shift(value, 16) & 65535
    value = value * 73244475
    value = value ^ jnp.right_shift(value, 16) & 65535
    value = value * 73244475
    value = value ^ jnp.right_shift(value, 16) & 65535
    return value


def sketch_table(base_value, feature_index, rank):
    counter = feature_index[:, None] * rank + jnp.arange(rank, dtype=jnp.int32)[None, :]
    offset = scramble(base_value)
    total = jnp.zeros(counter.shape, jnp.float32)
    for j in range(4):
        hashed = scramble(counter * 4 + j + offset)
        total = total + (hashed & 16777215).astype(jnp.float32) * (1.0 / 16777216.0)
    return ((total - 2.0) * 1.7320508).astype(jnp.bfloat16)


def terms_of(value):
    if value.dtype == jnp.bfloat16:
        return [value]
    high = value.astype(jnp.bfloat16)
    rest = value - high.astype(jnp.float32)
    middle = rest.astype(jnp.bfloat16)
    low = (rest - middle.astype(jnp.float32)).astype(jnp.bfloat16)
    return [high, middle, low]


def dot_nn(left, right):
    return lax.dot_general(
        left, right, (((1,), (0,)), ((), ())), preferred_element_type=jnp.float32
    )


def dot_nt(left, right):
    return lax.dot_general(
        left, right, (((1,), (1,)), ((), ())), preferred_element_type=jnp.float32
    )


def small_times_wide(small, wide):
    left, right = terms_of(small), terms_of(wide)
    pairs = [(i, d - i) for d in (2, 1, 0) for i in range(d + 1)]
    pairs = [(i, j) for i, j in pairs if i < len(left) and j < len(right)]
    return dot_nn(
        jnp.concatenate([left[i] for i, unused in pairs], axis=1),
        jnp.concatenate([right[j] for unused, j in pairs], axis=0),
    )


def gram_of(wide):
    terms = terms_of(wide)
    if len(terms) == 1:
        return dot_nt(terms[0], terms[0])
    rank = wide.shape[0]
    stacked = jnp.concatenate(terms, axis=0)
    both = dot_nt(stacked, stacked)
    cross = both[rank : 2 * rank, :rank] + both[2 * rank :, :rank]
    return both[:rank, :rank] + ((cross + cross.T) + both[rank : 2 * rank, rank : 2 * rank])


def eliminate(matrix):
    size = matrix.shape[0]
    blocks = size // SUB
    row_index = lax.broadcasted_iota(jnp.int32, (SUB, 2 * size), 0)
    square_row = lax.broadcasted_iota(jnp.int32, (SUB, size), 0)
    square_col = lax.broadcasted_iota(jnp.int32, (SUB, size), 1)
    work = []
    for i in range(blocks):
        unit = jnp.where(square_col == square_row + SUB * i, 1.0, 0.0).astype(jnp.float32)
        work.append(jnp.concatenate([matrix[SUB * i : SUB * (i + 1), :], unit], axis=1))
    rows = []
    for b in range(blocks):
        columns = [
            {
                i: jnp.broadcast_to(work[i][:, SUB * b + j : SUB * b + j + 1], (SUB, 2 * size))
                for i in range(b, blocks)
            }
            for j in range(SUB)
        ]
        pivots = jnp.zeros((SUB, 2 * size), jnp.float32)
        for k in range(SUB):
            pivot = jnp.broadcast_to(columns[k][b][k : k + 1, :], (SUB, 2 * size))
            reciprocal = 1.0 / pivot
            pivots = jnp.where(row_index == k, pivot, pivots)
            work_row = jnp.broadcast_to(work[b][k : k + 1, :], (SUB, 2 * size))
            later = [
                jnp.broadcast_to(columns[j][b][k : k + 1, :], (SUB, 2 * size))
                for j in range(k + 1, SUB)
            ]
            for i in range(b, blocks):
                factor = columns[k][i] * reciprocal
                if i == b:
                    factor = jnp.where(row_index > k, factor, 0.0)
                for j in range(k + 1, SUB):
                    columns[j][i] = columns[j][i] - factor * later[j - k - 1]
                work[i] = work[i] - factor * work_row
        rows.append(work[b] * lax.rsqrt(pivots))
    both = jnp.concatenate(rows, axis=0)
    keep = lax.broadcasted_iota(jnp.int32, (size, size), 1) >= lax.broadcasted_iota(
        jnp.int32, (size, size), 0
    )
    return jnp.where(keep, both[:, :size], 0.0), both[:, size:]


def shifted(whole_gram):
    size = whole_gram.shape[0]
    diagonal = lax.broadcasted_iota(jnp.int32, (size, size), 0) == lax.broadcasted_iota(
        jnp.int32, (size, size), 1
    )
    on_diagonal = jnp.where(diagonal, whole_gram, 0.0)
    trace = jnp.sum(jnp.sum(on_diagonal, axis=1, keepdims=True), axis=0, keepdims=True)
    return jnp.where(diagonal, whole_gram + shift_ratio * trace, whole_gram)


def wide_of(at_ref, z_refs):
    half = z_refs[0].shape[0]
    n_col = at_ref.shape[0] // half
    chunks = [z_refs[i // n_col % 2][at_ref[i]] for i in range(at_ref.shape[0])]
    return jnp.concatenate(chunks, axis=1)


def narrow_basis(at_ref, z_refs):
    wide = wide_of(at_ref, z_refs)
    upper, inverse_one = eliminate(shifted(gram_of(wide)))
    first = small_times_wide(inverse_one, wide)
    unused, inverse_two = eliminate(gram_of(first))
    return small_times_wide(inverse_two, first).astype(jnp.bfloat16), upper


def power_body(basis, a, at_ref, part_refs):
    weights = dot_nn(basis, a).astype(jnp.bfloat16)
    forth = dot_nt(weights, a)
    half, unused, width = part_refs[0].shape
    n_col = at_ref.shape[0] // half
    for i in range(2 * half):
        target = part_refs[i // n_col % 2]
        target[at_ref[i]] = forth[:, width * i : width * (i + 1)].astype(target.dtype)


def orth_kernel(at_ref, z_ref, other_ref, basis_ref, upper_ref):
    basis_ref[...], upper_ref[...] = narrow_basis(at_ref, (z_ref, other_ref))


def power_kernel(at_ref, basis_ref, *refs):
    piece_refs, a_ref, part_refs = refs[:-3], refs[-3], refs[-2:]
    rows = piece_refs[0].shape[0]
    for s, piece_ref in enumerate(piece_refs):
        a_ref[rows * s : rows * (s + 1), :] = piece_ref[...]
    power_body(basis_ref[...], a_ref[...], at_ref, part_refs)


def orth_power_kernel(at_ref, z_ref, other_ref, a_ref, *part_refs):
    basis, unused = narrow_basis(at_ref, (z_ref, other_ref))
    power_body(basis, a_ref[...], at_ref, part_refs)


def last_kernel(at_ref, z_ref, other_ref, a_ref, out_ref):
    basis, unused = narrow_basis(at_ref, (z_ref, other_ref))
    out_ref[...] = dot_nn(basis, a_ref[...])


def call(kernel, out_shapes, flops, at, *operands):
    moved = sum(x.size * x.dtype.itemsize for x in operands)
    return pl.pallas_call(
        kernel,
        out_shape=out_shapes,
        in_specs=[pl.BlockSpec(memory_space=pltpu.SMEM)]
        + [pl.BlockSpec(memory_space=pltpu.VMEM)] * len(operands),
        out_specs=jax.tree.map(lambda _: pl.BlockSpec(memory_space=pltpu.VMEM), out_shapes),
        compiler_params=pltpu.CompilerParams(vmem_limit_bytes=40 * 1024 * 1024),
        cost_estimate=pl.CostEstimate(flops=flops, bytes_accessed=moved, transcendentals=0),
    )(at, *operands)


def bits(size):
    return [1 << k for k in range(size.bit_length() - 1)]


def from_xor(value, axis, offset):
    size = math.prod(lax.axis_size(name) for name in axis)
    return lax.ppermute(value, axis, [(i, i ^ offset) for i in range(size)])


def sum_parts(keep, send, dtype):
    total = keep + from_xor(send, ("core",), 1).astype(jnp.float32)
    for bit in bits(lax.axis_size("col")):
        half = total.shape[0] // 2
        other = from_xor(total[half:].astype(dtype), ("col",), bit)
        total = total[:half] + other.astype(jnp.float32)
    for bit in bits(lax.axis_size("z")):
        mine = total.astype(dtype)
        total = mine.astype(jnp.float32) + from_xor(mine, ("z",), bit).astype(jnp.float32)
    return total.astype(dtype)


def gather_parts(own):
    for bit in bits(lax.axis_size("col"))[::-1]:
        own = jnp.concatenate([own, from_xor(own, ("col",), bit)])
    return own, from_xor(own, ("core",), 1)


def chunk_places(digits):
    n_z, n_col = lax.axis_size("z"), lax.axis_size("col")
    index = jnp.arange(n_z * 2 * n_col, dtype=jnp.int32)
    z_at, col_at = lax.axis_index("z"), lax.axis_index("col")
    column = index % n_col
    relative = {"z": index // (2 * n_col), "col": column ^ col_at}
    absolute = {"z": relative["z"] ^ z_at, "col": column}
    place = jnp.zeros_like(index)
    for axis, bit, is_relative in digits:
        place = place * 2 + ((relative if is_relative else absolute)[axis] // bit) % 2
    return place.astype(jnp.int32)


def per_device_transposed(sketch_base, states):
    n_z, n_core, n_col = lax.axis_size("z"), lax.axis_size("core"), lax.axis_size("col")
    n_row = n_z * n_core
    rows_local, width_local = states.shape
    rows_total, width_total = rows_local * n_row, width_local * n_col
    chunk = rows_local // n_col
    cols = width_local // n_row
    half = n_z * n_col
    row = lax.axis_index("z") * n_core + lax.axis_index("core")
    pieces = [None] * n_row

    def block(slab, offset):
        return lax.dynamic_slice_in_dim(slab, (row ^ offset) * cols, cols, 1)

    def move(slab, offsets):
        for offset in offsets:
            pieces[offset] = block(slab, offset)
            if offset:
                pieces[offset] = from_xor(pieces[offset], ("z", "core"), offset)

    far = list(range(n_row // 2, n_row))
    near = list(range(1, n_row // 2))

    def hold(value, offsets):
        value, moved = lax.optimization_barrier((value, [pieces[o] for o in offsets]))
        for o, piece in zip(offsets, moved):
            pieces[o] = piece
        return value

    col = lax.axis_index("col")
    feature_index = col * width_local + jnp.arange(width_local, dtype=jnp.int32)
    omega = sketch_table(sketch_base[0], feature_index, RANK)
    z = lax.dot_general(
        omega, states, (((0,), (1,)), ((), ())), preferred_element_type=jnp.float32
    )
    move(states, far[:2] + [0])
    for bit in bits(n_col):
        z = z + from_xor(z, ("col",), bit)
    z = z.reshape(RANK, n_col, chunk).transpose(1, 0, 2)
    z_bits = bits(n_z)[::-1]
    z = jnp.concatenate([z, from_xor(z, ("z",), z_bits[0])])
    z, slab = lax.optimization_barrier((z, states))
    move(slab, far[2:])
    z = hold(z, far[:1])
    for bit in z_bits[1:]:
        z = jnp.concatenate([z, from_xor(z, ("z",), bit)])
    move(slab, near)
    z = hold(z, far[1:2])
    z = z, from_xor(z, ("core",), 1)
    z = hold(z, far[2:3])
    absolute_col = [("col", bit, False) for bit in bits(n_col)[::-1]]
    at_first = chunk_places([("z", bit, True) for bit in z_bits[::-1]] + absolute_col)
    relative_col = [("col", bit, True) for bit in bits(n_col)]
    at = chunk_places(relative_col + [("z", bit, False) for bit in z_bits])

    f32 = jnp.float32
    square = jax.ShapeDtypeStruct((RANK, RANK), f32)
    wide = jax.ShapeDtypeStruct((RANK, rows_total), jnp.bfloat16)
    orth_flops = 8 * 64 * 64 * rows_total * 6
    power_flops = 4 * 64 * rows_total * cols

    def sent_as(dtype):
        shape = (half, RANK, chunk)
        return jax.ShapeDtypeStruct(shape, f32), jax.ShapeDtypeStruct(shape, dtype)

    basis, upper = call(orth_kernel, (wide, square), orth_flops, at_first, *z)
    factor = upper.T * (1.0 / math.sqrt(rows_total * width_total))
    dtype = f32
    slab = jax.ShapeDtypeStruct((rows_total, cols), states.dtype)
    a, *parts = call(power_kernel, (slab,) + sent_as(dtype), power_flops, at, basis, *pieces)
    for step in range(POWER - 1):
        z = gather_parts(sum_parts(*parts, dtype))
        dtype = jnp.bfloat16
        flops = orth_flops + power_flops
        parts = call(orth_power_kernel, sent_as(dtype), flops, at, *z, a)
    z = gather_parts(sum_parts(*parts, dtype))
    loadings = jax.ShapeDtypeStruct((RANK, cols), f32)
    return call(last_kernel, loadings, orth_flops + power_flops, at, *z, a).T, factor


def local_gram(basis):
    return jnp.dot(basis.T, basis, precision=lax.Precision.HIGHEST)


def orthonormal_block(sketch):
    whole_gram = lax.psum(local_gram(sketch), "row")
    identity = jnp.eye(RANK, dtype=jnp.float32)
    lower = jnp.linalg.cholesky(whole_gram + shift_ratio * jnp.trace(whole_gram) * identity)
    first = jax.scipy.linalg.solve_triangular(lower, sketch.T, lower=True).T
    lower_two = jnp.linalg.cholesky(lax.psum(local_gram(first), "row"))
    return jax.scipy.linalg.solve_triangular(lower_two, first.T, lower=True).T, lower


def per_device_slabs(sketch_base, states):
    width_local = states.shape[1]
    rows_total = states.shape[0] * lax.axis_size("row")
    width_total = width_local * lax.axis_size("col")
    feature_index = lax.axis_index("col") * width_local + jnp.arange(width_local, dtype=jnp.int32)
    omega = sketch_table(sketch_base[0], feature_index, RANK)

    def row_basis(right):
        partial_sketch = jnp.dot(states, right, preferred_element_type=jnp.float32)
        basis_new, lower = orthonormal_block(lax.psum(partial_sketch, "col"))
        return basis_new.astype(jnp.bfloat16), lower

    def back(basis):
        return lax.dot_general(
            states, basis, (((0,), (0,)), ((), ())), preferred_element_type=jnp.float32
        )

    basis, first_lower = row_basis(omega)
    factor = first_lower * (1.0 / math.sqrt(rows_total * width_total))
    for step in range(POWER):
        basis, unused = row_basis(lax.psum(back(basis), "row").astype(jnp.bfloat16))
    return lax.psum_scatter(back(basis), "row", scatter_dimension=0, tiled=True), factor


def solution(mesh):
    n_grp, n_row, n_col = (mesh.shape[name] for name in ("grp", "row", "col"))
    fits = n_row % 2 == 0 and n_row & (n_row - 1) == 0

    def run(sketch_base, states):
        rows_local = states.shape[0] // (n_grp * n_row)
        width_local = states.shape[1] // n_col
        tiled = rows_local % (n_col * LANES) == 0 and width_local % (n_row * LANES) == 0
        if fits and tiled:
            split = mesh.devices.reshape(n_grp, n_row // 2, 2, n_col)
            inner = jax.sharding.Mesh(split, ("grp", "z", "core", "col"))
            row, step = ("z", "core"), per_device_transposed
        else:
            inner, row, step = mesh, ("row",), per_device_slabs
        return jax.shard_map(
            step,
            mesh=inner,
            in_specs=(P("grp"), P(("grp",) + row, "col")),
            out_specs=(P(("col",) + row, "grp"), P("grp", None)),
            check_vma=False,
        )(sketch_base, states)

    return run
```

```python
import functools
import math

import jax
import jax.numpy as jnp
from jax import lax
from jax.experimental import pallas as pl
from jax.experimental.pallas import tpu as pltpu
from jax.sharding import PartitionSpec as P

RANK = 64
POWER = 4
LANES = 128
SUB = 8


shift_ratio = 0.005


def scramble(value):
    value = value ^ jnp.right_shift(value, 16) & 65535
    value = value * 73244475
    value = value ^ jnp.right_shift(value, 16) & 65535
    value = value * 73244475
    value = value ^ jnp.right_shift(value, 16) & 65535
    return value


def sketch_table(base_value, feature_index, rank):
    counter = feature_index[:, None] * rank + jnp.arange(rank, dtype=jnp.int32)[None, :]
    offset = scramble(base_value)
    total = jnp.zeros(counter.shape, jnp.float32)
    for j in range(4):
        hashed = scramble(counter * 4 + j + offset)
        total = total + (hashed & 16777215).astype(jnp.float32) * (1.0 / 16777216.0)
    return ((total - 2.0) * 1.7320508).astype(jnp.bfloat16)


def terms_of(value):
    if value.dtype == jnp.bfloat16:
        return [value]
    high = value.astype(jnp.bfloat16)
    rest = value - high.astype(jnp.float32)
    middle = rest.astype(jnp.bfloat16)
    low = (rest - middle.astype(jnp.float32)).astype(jnp.bfloat16)
    return [high, middle, low]


def dot_nn(left, right):
    return lax.dot_general(
        left, right, (((1,), (0,)), ((), ())), preferred_element_type=jnp.float32
    )


def dot_nt(left, right):
    return lax.dot_general(
        left, right, (((1,), (1,)), ((), ())), preferred_element_type=jnp.float32
    )


def small_times_wide(small, wide):
    left, right = terms_of(small), terms_of(wide)
    pairs = [(i, d - i) for d in (2, 1, 0) for i in range(d + 1)]
    pairs = [(i, j) for i, j in pairs if i < len(left) and j < len(right)]
    return dot_nn(
        jnp.concatenate([left[i] for i, unused in pairs], axis=1),
        jnp.concatenate([right[j] for unused, j in pairs], axis=0),
    )


def gram_of(wide):
    terms = terms_of(wide)
    if len(terms) == 1:
        return dot_nt(terms[0], terms[0])
    rank = wide.shape[0]
    stacked = jnp.concatenate(terms, axis=0)
    both = dot_nt(stacked, stacked)
    cross = both[rank : 2 * rank, :rank] + both[2 * rank :, :rank]
    return both[:rank, :rank] + ((cross + cross.T) + both[rank : 2 * rank, rank : 2 * rank])


def eliminate(matrix):
    size = matrix.shape[0]
    blocks = size // SUB
    row_index = lax.broadcasted_iota(jnp.int32, (SUB, 2 * size), 0)
    square_row = lax.broadcasted_iota(jnp.int32, (SUB, size), 0)
    square_col = lax.broadcasted_iota(jnp.int32, (SUB, size), 1)
    work = []
    for i in range(blocks):
        unit = jnp.where(square_col == square_row + SUB * i, 1.0, 0.0).astype(jnp.float32)
        work.append(jnp.concatenate([matrix[SUB * i : SUB * (i + 1), :], unit], axis=1))
    rows = []
    for b in range(blocks):
        columns = [
            {
                i: jnp.broadcast_to(work[i][:, SUB * b + j : SUB * b + j + 1], (SUB, 2 * size))
                for i in range(b, blocks)
            }
            for j in range(SUB)
        ]
        pivots = jnp.zeros((SUB, 2 * size), jnp.float32)
        for k in range(SUB):
            pivot = jnp.broadcast_to(columns[k][b][k : k + 1, :], (SUB, 2 * size))
            reciprocal = 1.0 / pivot
            pivots = jnp.where(row_index == k, pivot, pivots)
            work_row = jnp.broadcast_to(work[b][k : k + 1, :], (SUB, 2 * size))
            later = [
                jnp.broadcast_to(columns[j][b][k : k + 1, :], (SUB, 2 * size))
                for j in range(k + 1, SUB)
            ]
            for i in range(b, blocks):
                factor = columns[k][i] * reciprocal
                if i == b:
                    factor = jnp.where(row_index > k, factor, 0.0)
                for j in range(k + 1, SUB):
                    columns[j][i] = columns[j][i] - factor * later[j - k - 1]
                work[i] = work[i] - factor * work_row
        rows.append(work[b] * lax.rsqrt(pivots))
    both = jnp.concatenate(rows, axis=0)
    keep = lax.broadcasted_iota(jnp.int32, (size, size), 1) >= lax.broadcasted_iota(
        jnp.int32, (size, size), 0
    )
    return jnp.where(keep, both[:, :size], 0.0), both[:, size:]


def shifted(whole_gram):
    size = whole_gram.shape[0]
    diagonal = lax.broadcasted_iota(jnp.int32, (size, size), 0) == lax.broadcasted_iota(
        jnp.int32, (size, size), 1
    )
    on_diagonal = jnp.where(diagonal, whole_gram, 0.0)
    trace = jnp.sum(jnp.sum(on_diagonal, axis=1, keepdims=True), axis=0, keepdims=True)
    return jnp.where(diagonal, whole_gram + shift_ratio * trace, whole_gram)


def wide_of(at_ref, z_refs):
    chunks = [z_ref[at_ref[i]] for z_ref in z_refs for i in range(at_ref.shape[0])]
    return jnp.concatenate(chunks, axis=1)


def first_pass(at_ref, z_refs):
    wide = wide_of(at_ref, z_refs)
    upper, inverse_one = eliminate(shifted(gram_of(wide)))
    return small_times_wide(inverse_one, wide), upper


def back_product(at_ref, z_refs, a):
    first, unused = first_pass(at_ref, z_refs)
    rank = first.shape[0]
    back = dot_nn(jnp.concatenate(terms_of(first), axis=0), a)
    back = back[:rank] + (back[rank : 2 * rank] + back[2 * rank :])
    unused, inverse_two = eliminate(gram_of(first))
    return small_times_wide(inverse_two, back)


def forth_product(weights, a_ref, at_ref, part_ref):
    chunks, unused, width = part_ref.shape
    forth = dot_nt(weights.astype(jnp.bfloat16), a_ref[: chunks * width, :])
    for i in range(chunks):
        part_ref[at_ref[i]] = forth[:, width * i : width * (i + 1)]


def orth_kernel(at_ref, z_ref, other_ref, basis_ref, upper_ref):
    first, upper = first_pass(at_ref, (z_ref, other_ref))
    unused, inverse_two = eliminate(gram_of(first))
    basis_ref[...] = small_times_wide(inverse_two, first).astype(jnp.bfloat16)
    upper_ref[...] = upper


def power_kernel(at_ref, basis_ref, *refs):
    piece_refs, a_ref, part_ref = refs[:-2], refs[-2], refs[-1]
    rows = piece_refs[0].shape[0]
    for s, piece_ref in enumerate(piece_refs):
        a_ref[rows * s : rows * (s + 1), :] = piece_ref[...]
    forth_product(dot_nn(basis_ref[...], a_ref[...]), a_ref, at_ref, part_ref)


def orth_power_kernel(at_ref, z_ref, other_ref, a_ref, part_ref):
    weights = back_product(at_ref, (z_ref, other_ref), a_ref[...])
    forth_product(weights, a_ref, at_ref, part_ref)


def last_kernel(at_ref, core_ref, z_ref, other_ref, a_ref, out_ref):
    cols = out_ref.shape[1]
    start = pl.multiple_of(core_ref[0] * cols, cols)
    out_ref[...] = back_product(at_ref, (z_ref, other_ref), a_ref[:, pl.ds(start, cols)])


def call(kernel, out_shapes, flops, scalars, *operands):
    moved = sum(x.size * x.dtype.itemsize for x in operands)
    return pl.pallas_call(
        kernel,
        out_shape=out_shapes,
        in_specs=[pl.BlockSpec(memory_space=pltpu.SMEM)] * len(scalars)
        + [pl.BlockSpec(memory_space=pltpu.VMEM)] * len(operands),
        out_specs=jax.tree.map(lambda _: pl.BlockSpec(memory_space=pltpu.VMEM), out_shapes),
        compiler_params=pltpu.CompilerParams(vmem_limit_bytes=40 * 1024 * 1024),
        cost_estimate=pl.CostEstimate(flops=flops, bytes_accessed=moved, transcendentals=0),
    )(*scalars, *operands)


def bits(size):
    return [1 << k for k in range(size.bit_length() - 1)]


def from_xor(value, axis, offset):
    size = math.prod(lax.axis_size(name) for name in axis)
    return lax.ppermute(value, axis, [(i, i ^ offset) for i in range(size)])


def sum_parts(total, dtype):
    for bit in bits(lax.axis_size("col")):
        half = total.shape[0] // 2
        other = from_xor(total[half:].astype(dtype), ("col",), bit)
        total = total[:half] + other.astype(jnp.float32)
    for bit in bits(lax.axis_size("z")):
        mine = total.astype(dtype)
        total = mine.astype(jnp.float32) + from_xor(mine, ("z",), bit).astype(jnp.float32)
    return total.astype(dtype)


def gather_parts(own):
    for bit in bits(lax.axis_size("col"))[::-1]:
        own = jnp.concatenate([own, from_xor(own, ("col",), bit)])
    return own, from_xor(own, ("core",), 1)


def chunk_places(digits):
    n_z, n_col = lax.axis_size("z"), lax.axis_size("col")
    index = jnp.arange(n_z * n_col, dtype=jnp.int32)
    z_at, col_at = lax.axis_index("z"), lax.axis_index("col")
    column = index % n_col
    relative = {"z": index // n_col, "col": column ^ col_at}
    absolute = {"z": relative["z"] ^ z_at, "col": column}
    place = jnp.zeros_like(index)
    for axis, bit, is_relative in digits:
        place = place * 2 + ((relative if is_relative else absolute)[axis] // bit) % 2
    return place.astype(jnp.int32)


def per_device_transposed(sketch_base, states):
    n_z, n_core, n_col = lax.axis_size("z"), lax.axis_size("core"), lax.axis_size("col")
    n_row = n_z * n_core
    rows_local, width_local = states.shape
    rows_total, width_total = rows_local * n_row, width_local * n_col
    chunk = rows_local // n_col
    cols = width_local // n_z
    chunks = n_z * n_col
    z_at, col = lax.axis_index("z"), lax.axis_index("col")
    pieces = {}

    def move(slab, offset):
        block = lax.dynamic_slice_in_dim(slab, (z_at ^ offset) * cols, cols, 1)
        pieces[offset] = from_xor(block, ("z",), offset) if offset else block

    feature_index = col * width_local + jnp.arange(width_local, dtype=jnp.int32)
    omega = sketch_table(sketch_base[0], feature_index, RANK)
    z = lax.dot_general(
        omega, states, (((0,), (1,)), ((), ())), preferred_element_type=jnp.float32
    )
    z_bits = bits(n_z)[::-1]
    far = z_bits[0]
    move(states, 0)
    move(states, far)
    for bit in bits(n_col):
        z = z + from_xor(z, ("col",), bit)
    z = z.reshape(RANK, n_col, chunk).transpose(1, 0, 2)
    z = jnp.concatenate([z, from_xor(z, ("z",), far)])
    z, slab = lax.optimization_barrier((z, states))
    for offset in sorted(set(range(1, n_z)) - {far}, reverse=True):
        move(slab, offset)
    z, pieces[far] = lax.optimization_barrier((z, pieces[far]))
    for bit in z_bits[1:]:
        z = jnp.concatenate([z, from_xor(z, ("z",), bit)])
    z = z, from_xor(z, ("core",), 1)
    absolute_col = [("col", bit, False) for bit in bits(n_col)[::-1]]
    at_first = chunk_places([("z", bit, True) for bit in z_bits[::-1]] + absolute_col)
    relative_col = [("col", bit, True) for bit in bits(n_col)]
    at = chunk_places(relative_col + [("z", bit, False) for bit in z_bits])
    early = [0, far]
    late = [offset for offset in range(n_z) if offset not in early]
    others = {offset: from_xor(pieces[offset], ("core",), 1) for offset in early}

    f32 = jnp.float32
    square = jax.ShapeDtypeStruct((RANK, RANK), f32)
    wide = jax.ShapeDtypeStruct((RANK, rows_total), jnp.bfloat16)
    slab = jax.ShapeDtypeStruct((rows_total, cols), states.dtype)
    parts = jax.ShapeDtypeStruct((chunks, RANK, chunk), f32)
    loadings = jax.ShapeDtypeStruct((RANK, cols // n_core), f32)
    orth_flops = 8 * 64 * 64 * rows_total * 6
    flops = orth_flops + 4 * 64 * rows_total * cols

    basis, upper = call(orth_kernel, (wide, square), orth_flops, (at_first,), *z)
    basis, moved = lax.optimization_barrier((basis, [pieces[offset] for offset in late]))
    pieces.update(zip(late, moved))
    others.update((offset, from_xor(pieces[offset], ("core",), 1)) for offset in late)
    blocks = [half[offset] for half in (pieces, others) for offset in range(n_z)]
    factor = upper.T * (1.0 / math.sqrt(rows_total * width_total))
    a, total = call(power_kernel, (slab, parts), flops, (at,), basis, *blocks)
    z = gather_parts(sum_parts(total, f32))
    for step in range(POWER - 1):
        total = call(orth_power_kernel, parts, flops, (at,), *z, a)
        z = gather_parts(sum_parts(total, jnp.bfloat16))
    core = lax.axis_index("core")[None].astype(jnp.int32)
    return call(last_kernel, loadings, flops, (at, core), *z, a).T, factor


def local_gram(basis):
    return jnp.dot(basis.T, basis, precision=lax.Precision.HIGHEST)


def orthonormal_block(sketch):
    whole_gram = lax.psum(local_gram(sketch), "row")
    identity = jnp.eye(RANK, dtype=jnp.float32)
    lower = jnp.linalg.cholesky(whole_gram + shift_ratio * jnp.trace(whole_gram) * identity)
    first = jax.scipy.linalg.solve_triangular(lower, sketch.T, lower=True).T
    lower_two = jnp.linalg.cholesky(lax.psum(local_gram(first), "row"))
    return jax.scipy.linalg.solve_triangular(lower_two, first.T, lower=True).T, lower


def per_device_slabs(sketch_base, states):
    width_local = states.shape[1]
    rows_total = states.shape[0] * lax.axis_size("row")
    width_total = width_local * lax.axis_size("col")
    feature_index = lax.axis_index("col") * width_local + jnp.arange(width_local, dtype=jnp.int32)
    omega = sketch_table(sketch_base[0], feature_index, RANK)

    def row_basis(right):
        partial_sketch = jnp.dot(states, right, preferred_element_type=jnp.float32)
        basis_new, lower = orthonormal_block(lax.psum(partial_sketch, "col"))
        return basis_new.astype(jnp.bfloat16), lower

    def back(basis):
        return lax.dot_general(
            states, basis, (((0,), (0,)), ((), ())), preferred_element_type=jnp.float32
        )

    basis, first_lower = row_basis(omega)
    factor = first_lower * (1.0 / math.sqrt(rows_total * width_total))
    for step in range(POWER):
        basis, unused = row_basis(lax.psum(back(basis), "row").astype(jnp.bfloat16))
    return lax.psum_scatter(back(basis), "row", scatter_dimension=0, tiled=True), factor


def solution(mesh):
    n_grp, n_row, n_col = (mesh.shape[name] for name in ("grp", "row", "col"))
    fits = n_row % 2 == 0 and n_row & (n_row - 1) == 0

    def run(sketch_base, states):
        rows_local = states.shape[0] // (n_grp * n_row)
        width_local = states.shape[1] // n_col
        tiled = rows_local % (n_col * LANES) == 0 and width_local % (n_row * LANES) == 0
        if fits and tiled:
            split = mesh.devices.reshape(n_grp, n_row // 2, 2, n_col)
            inner = jax.sharding.Mesh(split, ("grp", "z", "core", "col"))
            row, step = ("z", "core"), per_device_transposed
        else:
            inner, row, step = mesh, ("row",), per_device_slabs
        return jax.shard_map(
            step,
            mesh=inner,
            in_specs=(P("grp"), P(("grp",) + row, "col")),
            out_specs=(P(("col",) + row, "grp"), P("grp", None)),
            check_vma=False,
        )(sketch_base, states)

    return run
```

```python
import functools
import math

import jax
import jax.numpy as jnp
from jax import lax
from jax.experimental import pallas as pl
from jax.experimental.pallas import tpu as pltpu
from jax.sharding import PartitionSpec as P

RANK = 64
POWER = 4
LANES = 128
SUB = 8
TILE = 256


shift_ratio = 0.005


def scramble(value):
    value = value ^ jnp.right_shift(value, 16) & 65535
    value = value * 73244475
    value = value ^ jnp.right_shift(value, 16) & 65535
    value = value * 73244475
    value = value ^ jnp.right_shift(value, 16) & 65535
    return value


def sketch_table(base_value, feature_index, rank):
    counter = feature_index[:, None] * rank + jnp.arange(rank, dtype=jnp.int32)[None, :]
    offset = scramble(base_value)
    total = jnp.zeros(counter.shape, jnp.float32)
    for j in range(4):
        hashed = scramble(counter * 4 + j + offset)
        total = total + (hashed & 16777215).astype(jnp.float32) * (1.0 / 16777216.0)
    return ((total - 2.0) * 1.7320508).astype(jnp.bfloat16)


def terms_of(value):
    if value.dtype == jnp.bfloat16:
        return [value]
    high = value.astype(jnp.bfloat16)
    rest = value - high.astype(jnp.float32)
    middle = rest.astype(jnp.bfloat16)
    low = (rest - middle.astype(jnp.float32)).astype(jnp.bfloat16)
    return [high, middle, low]


def dot_nn(left, right):
    return lax.dot_general(
        left, right, (((1,), (0,)), ((), ())), preferred_element_type=jnp.float32
    )


def dot_nt(left, right):
    return lax.dot_general(
        left, right, (((1,), (1,)), ((), ())), preferred_element_type=jnp.float32
    )


def small_times_wide(small, wide):
    left, right = terms_of(small), terms_of(wide)
    pairs = [(i, d - i) for d in (2, 1, 0) for i in range(d + 1)]
    pairs = [(i, j) for i, j in pairs if i < len(left) and j < len(right)]
    return dot_nn(
        jnp.concatenate([left[i] for i, unused in pairs], axis=1),
        jnp.concatenate([right[j] for unused, j in pairs], axis=0),
    )


def gram_of(wide):
    terms = terms_of(wide)
    if len(terms) == 1:
        return dot_nt(terms[0], terms[0])
    rank = wide.shape[0]
    stacked = jnp.concatenate(terms, axis=0)
    both = dot_nt(stacked, stacked)
    cross = both[rank : 2 * rank, :rank] + both[2 * rank :, :rank]
    return both[:rank, :rank] + ((cross + cross.T) + both[rank : 2 * rank, rank : 2 * rank])


def eliminate(matrix, beside=()):
    beside = list(beside)
    size = matrix.shape[0]
    blocks = size // SUB
    row_index = lax.broadcasted_iota(jnp.int32, (SUB, 2 * size), 0)
    square_row = lax.broadcasted_iota(jnp.int32, (SUB, size), 0)
    square_col = lax.broadcasted_iota(jnp.int32, (SUB, size), 1)
    work = []
    for i in range(blocks):
        unit = jnp.where(square_col == square_row + SUB * i, 1.0, 0.0).astype(jnp.float32)
        work.append(jnp.concatenate([matrix[SUB * i : SUB * (i + 1), :], unit], axis=1))
    rows = []
    for b in range(blocks):
        for unused in range(-(-len(beside) // (blocks - b))):
            beside.pop(0)()
        columns = [
            {
                i: jnp.broadcast_to(work[i][:, SUB * b + j : SUB * b + j + 1], (SUB, 2 * size))
                for i in range(b, blocks)
            }
            for j in range(SUB)
        ]
        pivots = jnp.zeros((SUB, 2 * size), jnp.float32)
        for k in range(SUB):
            pivot = jnp.broadcast_to(columns[k][b][k : k + 1, :], (SUB, 2 * size))
            reciprocal = 1.0 / pivot
            pivots = jnp.where(row_index == k, pivot, pivots)
            work_row = jnp.broadcast_to(work[b][k : k + 1, :], (SUB, 2 * size))
            later = [
                jnp.broadcast_to(columns[j][b][k : k + 1, :], (SUB, 2 * size))
                for j in range(k + 1, SUB)
            ]
            for i in range(b, blocks):
                factor = columns[k][i] * reciprocal
                if i == b:
                    factor = jnp.where(row_index > k, factor, 0.0)
                for j in range(k + 1, SUB):
                    columns[j][i] = columns[j][i] - factor * later[j - k - 1]
                work[i] = work[i] - factor * work_row
        rows.append(work[b] * lax.rsqrt(pivots))
    both = jnp.concatenate(rows, axis=0)
    keep = lax.broadcasted_iota(jnp.int32, (size, size), 1) >= lax.broadcasted_iota(
        jnp.int32, (size, size), 0
    )
    return jnp.where(keep, both[:, :size], 0.0), both[:, size:]


def shifted(whole_gram):
    size = whole_gram.shape[0]
    diagonal = lax.broadcasted_iota(jnp.int32, (size, size), 0) == lax.broadcasted_iota(
        jnp.int32, (size, size), 1
    )
    on_diagonal = jnp.where(diagonal, whole_gram, 0.0)
    trace = jnp.sum(jnp.sum(on_diagonal, axis=1, keepdims=True), axis=0, keepdims=True)
    return jnp.where(diagonal, whole_gram + shift_ratio * trace, whole_gram)


def wide_of(at_ref, z_refs):
    chunks = [z_ref[at_ref[i]] for z_ref in z_refs for i in range(at_ref.shape[0])]
    return jnp.concatenate(chunks, axis=1)


def first_pass(at_ref, z_refs):
    wide = wide_of(at_ref, z_refs)
    upper, inverse_one = eliminate(shifted(gram_of(wide)))
    return small_times_wide(inverse_one, wide), upper


def back_product(at_ref, z_refs, a):
    first, unused = first_pass(at_ref, z_refs)
    rank = first.shape[0]
    terms = jnp.concatenate(terms_of(first), axis=0)
    tiles = []

    def tile(start):
        back = dot_nn(terms, a[:, start : start + TILE])
        tiles.append(back[:rank] + (back[rank : 2 * rank] + back[2 * rank :]))

    starts = range(0, a.shape[1], TILE)
    work = [functools.partial(tile, start) for start in starts]
    unused, inverse_two = eliminate(gram_of(first), work)
    return small_times_wide(inverse_two, jnp.concatenate(tiles, axis=1))


def forth_product(weights, a_ref, at_ref, part_ref):
    chunks, unused, width = part_ref.shape
    forth = dot_nt(weights.astype(jnp.bfloat16), a_ref[: chunks * width, :])
    for i in range(chunks):
        part_ref[at_ref[i]] = forth[:, width * i : width * (i + 1)]


def orth_kernel(at_ref, z_ref, other_ref, basis_ref, upper_ref):
    first, upper = first_pass(at_ref, (z_ref, other_ref))
    unused, inverse_two = eliminate(gram_of(first))
    basis_ref[...] = small_times_wide(inverse_two, first).astype(jnp.bfloat16)
    upper_ref[...] = upper


def power_kernel(at_ref, basis_ref, *refs):
    piece_refs, a_ref, part_ref = refs[:-2], refs[-2], refs[-1]
    rows = piece_refs[0].shape[0]
    for s, piece_ref in enumerate(piece_refs):
        a_ref[rows * s : rows * (s + 1), :] = piece_ref[...]
    forth_product(dot_nn(basis_ref[...], a_ref[...]), a_ref, at_ref, part_ref)


def orth_power_kernel(at_ref, z_ref, other_ref, a_ref, part_ref):
    weights = back_product(at_ref, (z_ref, other_ref), a_ref[...])
    forth_product(weights, a_ref, at_ref, part_ref)


def last_kernel(at_ref, core_ref, z_ref, other_ref, a_ref, out_ref):
    cols = out_ref.shape[1]
    start = pl.multiple_of(core_ref[0] * cols, cols)
    out_ref[...] = back_product(at_ref, (z_ref, other_ref), a_ref[:, pl.ds(start, cols)])


def call(kernel, out_shapes, flops, scalars, *operands):
    moved = sum(x.size * x.dtype.itemsize for x in operands)
    return pl.pallas_call(
        kernel,
        out_shape=out_shapes,
        in_specs=[pl.BlockSpec(memory_space=pltpu.SMEM)] * len(scalars)
        + [pl.BlockSpec(memory_space=pltpu.VMEM)] * len(operands),
        out_specs=jax.tree.map(lambda _: pl.BlockSpec(memory_space=pltpu.VMEM), out_shapes),
        compiler_params=pltpu.CompilerParams(vmem_limit_bytes=20 * 1024 * 1024),
        cost_estimate=pl.CostEstimate(flops=flops, bytes_accessed=moved, transcendentals=0),
    )(*scalars, *operands)


def bits(size):
    return [1 << k for k in range(size.bit_length() - 1)]


def from_xor(value, axis, offset):
    size = math.prod(lax.axis_size(name) for name in axis)
    return lax.ppermute(value, axis, [(i, i ^ offset) for i in range(size)])


def sum_parts(total, dtype):
    for bit in bits(lax.axis_size("col")):
        half = total.shape[0] // 2
        other = from_xor(total[half:].astype(dtype), ("col",), bit)
        total = total[:half] + other.astype(jnp.float32)
    for bit in bits(lax.axis_size("z")):
        mine = total.astype(dtype)
        total = mine.astype(jnp.float32) + from_xor(mine, ("z",), bit).astype(jnp.float32)
    return total.astype(dtype)


def gather_parts(own):
    for bit in bits(lax.axis_size("col"))[::-1]:
        own = jnp.concatenate([own, from_xor(own, ("col",), bit)])
    return own, from_xor(own, ("core",), 1)


def chunk_places(digits):
    n_z, n_col = lax.axis_size("z"), lax.axis_size("col")
    index = jnp.arange(n_z * n_col, dtype=jnp.int32)
    z_at, col_at = lax.axis_index("z"), lax.axis_index("col")
    column = index % n_col
    relative = {"z": index // n_col, "col": column ^ col_at}
    absolute = {"z": relative["z"] ^ z_at, "col": column}
    place = jnp.zeros_like(index)
    for axis, bit, is_relative in digits:
        place = place * 2 + ((relative if is_relative else absolute)[axis] // bit) % 2
    return place.astype(jnp.int32)


def per_device_transposed(sketch_base, states):
    n_z, n_core, n_col = lax.axis_size("z"), lax.axis_size("core"), lax.axis_size("col")
    n_row = n_z * n_core
    rows_local, width_local = states.shape
    rows_total, width_total = rows_local * n_row, width_local * n_col
    chunk = rows_local // n_col
    cols = width_local // n_z
    chunks = n_z * n_col
    z_at, col = lax.axis_index("z"), lax.axis_index("col")
    pieces = {}

    def move(slab, offset):
        block = lax.dynamic_slice_in_dim(slab, (z_at ^ offset) * cols, cols, 1)
        pieces[offset] = from_xor(block, ("z",), offset) if offset else block

    feature_index = col * width_local + jnp.arange(width_local, dtype=jnp.int32)
    omega = sketch_table(sketch_base[0], feature_index, RANK)
    z = lax.dot_general(
        omega, states, (((0,), (1,)), ((), ())), preferred_element_type=jnp.float32
    )
    z = z.reshape(RANK, n_col, chunk).transpose(1, 0, 2)
    z_bits = bits(n_z)[::-1]
    far = z_bits[0]
    move(states, 0)
    z, slab = lax.optimization_barrier((z, states))
    move(slab, far)
    z = jnp.concatenate([z, from_xor(z, ("z",), far)])
    z, slab = lax.optimization_barrier((z, slab))
    for offset in sorted(set(range(1, n_z)) - {far}, reverse=True):
        move(slab, offset)
    for bit in z_bits[1:]:
        z = jnp.concatenate([z, from_xor(z, ("z",), bit)])
    for bit in bits(n_col):
        z = z + from_xor(z, ("col",), bit)
    z, pieces[far] = lax.optimization_barrier((z, pieces[far]))
    z = z, from_xor(z, ("core",), 1)
    absolute_col = [("col", bit, False) for bit in bits(n_col)[::-1]]
    at_first = chunk_places([("z", bit, True) for bit in z_bits[::-1]] + absolute_col)
    relative_col = [("col", bit, True) for bit in bits(n_col)]
    at = chunk_places(relative_col + [("z", bit, False) for bit in z_bits])
    early = [0, far]
    late = [offset for offset in range(n_z) if offset not in early]
    others = {offset: from_xor(pieces[offset], ("core",), 1) for offset in early}

    f32 = jnp.float32
    square = jax.ShapeDtypeStruct((RANK, RANK), f32)
    wide = jax.ShapeDtypeStruct((RANK, rows_total), jnp.bfloat16)
    slab = jax.ShapeDtypeStruct((rows_total, cols), states.dtype)
    parts = jax.ShapeDtypeStruct((chunks, RANK, chunk), f32)
    loadings = jax.ShapeDtypeStruct((RANK, cols // n_core), f32)
    orth_flops = 8 * 64 * 64 * rows_total * 6
    flops = orth_flops + 4 * 64 * rows_total * cols

    basis, upper = call(orth_kernel, (wide, square), orth_flops, (at_first,), *z)
    basis, moved = lax.optimization_barrier((basis, [pieces[offset] for offset in late]))
    pieces.update(zip(late, moved))
    others.update((offset, from_xor(pieces[offset], ("core",), 1)) for offset in late)
    blocks = [half[offset] for half in (pieces, others) for offset in range(n_z)]
    factor = upper.T * (1.0 / math.sqrt(rows_total * width_total))
    a, total = call(power_kernel, (slab, parts), flops, (at,), basis, *blocks)
    z = gather_parts(sum_parts(total, f32))
    for step in range(POWER - 1):
        total = call(orth_power_kernel, parts, flops, (at,), *z, a)
        z = gather_parts(sum_parts(total, jnp.bfloat16))
    core = lax.axis_index("core")[None].astype(jnp.int32)
    return call(last_kernel, loadings, flops, (at, core), *z, a).T, factor


def local_gram(basis):
    return jnp.dot(basis.T, basis, precision=lax.Precision.HIGHEST)


def orthonormal_block(sketch):
    whole_gram = lax.psum(local_gram(sketch), "row")
    identity = jnp.eye(RANK, dtype=jnp.float32)
    lower = jnp.linalg.cholesky(whole_gram + shift_ratio * jnp.trace(whole_gram) * identity)
    first = jax.scipy.linalg.solve_triangular(lower, sketch.T, lower=True).T
    lower_two = jnp.linalg.cholesky(lax.psum(local_gram(first), "row"))
    return jax.scipy.linalg.solve_triangular(lower_two, first.T, lower=True).T, lower


def per_device_slabs(sketch_base, states):
    width_local = states.shape[1]
    rows_total = states.shape[0] * lax.axis_size("row")
    width_total = width_local * lax.axis_size("col")
    feature_index = lax.axis_index("col") * width_local + jnp.arange(width_local, dtype=jnp.int32)
    omega = sketch_table(sketch_base[0], feature_index, RANK)

    def row_basis(right):
        partial_sketch = jnp.dot(states, right, preferred_element_type=jnp.float32)
        basis_new, lower = orthonormal_block(lax.psum(partial_sketch, "col"))
        return basis_new.astype(jnp.bfloat16), lower

    def back(basis):
        return lax.dot_general(
            states, basis, (((0,), (0,)), ((), ())), preferred_element_type=jnp.float32
        )

    basis, first_lower = row_basis(omega)
    factor = first_lower * (1.0 / math.sqrt(rows_total * width_total))
    for step in range(POWER):
        basis, unused = row_basis(lax.psum(back(basis), "row").astype(jnp.bfloat16))
    return lax.psum_scatter(back(basis), "row", scatter_dimension=0, tiled=True), factor


def solution(mesh):
    n_grp, n_row, n_col = (mesh.shape[name] for name in ("grp", "row", "col"))
    fits = n_row % 2 == 0 and n_row & (n_row - 1) == 0

    def run(sketch_base, states):
        rows_local = states.shape[0] // (n_grp * n_row)
        width_local = states.shape[1] // n_col
        tiled = rows_local % (n_col * LANES) == 0 and width_local % (n_row * LANES) == 0
        if fits and tiled:
            split = mesh.devices.reshape(n_grp, n_row // 2, 2, n_col)
            inner = jax.sharding.Mesh(split, ("grp", "z", "core", "col"))
            row, step = ("z", "core"), per_device_transposed
        else:
            inner, row, step = mesh, ("row",), per_device_slabs
        return jax.shard_map(
            step,
            mesh=inner,
            in_specs=(P("grp"), P(("grp",) + row, "col")),
            out_specs=(P(("col",) + row, "grp"), P("grp", None)),
            check_vma=False,
        )(sketch_base, states)

    return run
```

```python
import functools
import math

import jax
import jax.numpy as jnp
from jax import lax
from jax.experimental import pallas as pl
from jax.experimental.pallas import tpu as pltpu
from jax.sharding import PartitionSpec as P

RANK = 64
POWER = 4
LANES = 128
SUB = 8
TILE = 256


shift_ratio = 0.005


def scramble(value):
    value = value ^ jnp.right_shift(value, 16) & 65535
    value = value * 73244475
    value = value ^ jnp.right_shift(value, 16) & 65535
    value = value * 73244475
    value = value ^ jnp.right_shift(value, 16) & 65535
    return value


def sketch_table(base_value, feature_index, rank):
    counter = feature_index[:, None] * rank + jnp.arange(rank, dtype=jnp.int32)[None, :]
    offset = scramble(base_value)
    total = jnp.zeros(counter.shape, jnp.float32)
    for j in range(4):
        hashed = scramble(counter * 4 + j + offset)
        total = total + (hashed & 16777215).astype(jnp.float32) * (1.0 / 16777216.0)
    return ((total - 2.0) * 1.7320508).astype(jnp.bfloat16)


def terms_of(value):
    if value.dtype == jnp.bfloat16:
        return [value]
    high = value.astype(jnp.bfloat16)
    rest = value - high.astype(jnp.float32)
    middle = rest.astype(jnp.bfloat16)
    low = (rest - middle.astype(jnp.float32)).astype(jnp.bfloat16)
    return [high, middle, low]


def dot_nn(left, right):
    return lax.dot_general(
        left, right, (((1,), (0,)), ((), ())), preferred_element_type=jnp.float32
    )


def dot_nt(left, right):
    return lax.dot_general(
        left, right, (((1,), (1,)), ((), ())), preferred_element_type=jnp.float32
    )


def small_times_wide(small, wide):
    left, right = terms_of(small), terms_of(wide)
    pairs = [(i, d - i) for d in (2, 1, 0) for i in range(d + 1)]
    pairs = [(i, j) for i, j in pairs if i < len(left) and j < len(right)]
    return dot_nn(
        jnp.concatenate([left[i] for i, unused in pairs], axis=1),
        jnp.concatenate([right[j] for unused, j in pairs], axis=0),
    )


def gram_of(wide):
    terms = terms_of(wide)
    if len(terms) == 1:
        return dot_nt(terms[0], terms[0])
    rank = wide.shape[0]
    stacked = jnp.concatenate(terms, axis=0)
    both = dot_nt(stacked, stacked)
    cross = both[rank : 2 * rank, :rank] + both[2 * rank :, :rank]
    return both[:rank, :rank] + ((cross + cross.T) + both[rank : 2 * rank, rank : 2 * rank])


def eliminate(matrix, beside=()):
    beside = list(beside)
    size = matrix.shape[0]
    blocks = size // SUB
    row_index = lax.broadcasted_iota(jnp.int32, (SUB, 2 * size), 0)
    square_row = lax.broadcasted_iota(jnp.int32, (SUB, size), 0)
    square_col = lax.broadcasted_iota(jnp.int32, (SUB, size), 1)
    work = []
    for i in range(blocks):
        unit = jnp.where(square_col == square_row + SUB * i, 1.0, 0.0).astype(jnp.float32)
        work.append(jnp.concatenate([matrix[SUB * i : SUB * (i + 1), :], unit], axis=1))

    def fill(register, k):
        return jnp.broadcast_to(register[k : k + 1, :], (SUB, 2 * size))

    rows = []
    for b in range(blocks):
        for unused in range(-(-len(beside) // (blocks - b))):
            beside.pop(0)()
        columns = [
            {
                i: jnp.broadcast_to(work[i][:, SUB * b + j : SUB * b + j + 1], (SUB, 2 * size))
                for i in range(b, blocks)
            }
            for j in range(SUB)
        ]
        pivots = jnp.ones((SUB, 2 * size), jnp.float32)
        for k in range(0, SUB, 2):
            col_0, col_1 = columns[k], columns[k + 1]
            a, h, d = fill(col_0[b], k), fill(col_1[b], k), fill(col_1[b], k + 1)
            det = a * d - h * h
            over_det, over_a = 1.0 / det, 1.0 / a
            below_0 = jnp.where(row_index > k + 1, col_0[b], 0.0)
            below_1 = jnp.where(row_index > k + 1, col_1[b], 0.0)
            for j in range(k + 2, SUB):
                entry_0, entry_1 = fill(columns[j][b], k), fill(columns[j][b], k + 1)
                up_0 = d * entry_0 - h * entry_1
                up_1 = a * entry_1 - h * entry_0
                columns[j][b] = columns[j][b] - over_det * (below_0 * up_0 + below_1 * up_1)
                up_0, up_1 = over_det * up_0, over_det * up_1
                for i in range(b + 1, blocks):
                    columns[j][i] = columns[j][i] - (col_0[i] * up_0 + col_1[i] * up_1)
            row_0, row_1 = fill(work[b], k), fill(work[b], k + 1)
            up_0 = over_det * (d * row_0 - h * row_1)
            up_1 = over_det * (a * row_1 - h * row_0)
            for i in range(b + 1, blocks):
                work[i] = work[i] - (col_0[i] * up_0 + col_1[i] * up_1)
            second = jnp.where(row_index == k + 1, h * over_a, 0.0)
            work[b] = work[b] - (below_0 * up_0 + below_1 * up_1 + second * row_0)
            pivots = jnp.where(row_index == k, a, pivots)
            pivots = jnp.where(row_index == k + 1, det * over_a, pivots)
        rows.append(work[b] * lax.rsqrt(pivots))
    both = jnp.concatenate(rows, axis=0)
    keep = lax.broadcasted_iota(jnp.int32, (size, size), 1) >= lax.broadcasted_iota(
        jnp.int32, (size, size), 0
    )
    return jnp.where(keep, both[:, :size], 0.0), both[:, size:]


def shifted_factor(whole_gram):
    size = whole_gram.shape[0]
    diagonal = lax.broadcasted_iota(jnp.int32, (size, size), 0) == lax.broadcasted_iota(
        jnp.int32, (size, size), 1
    )
    on_diagonal = jnp.where(diagonal, whole_gram, 0.0)
    trace = jnp.sum(jnp.sum(on_diagonal, axis=1, keepdims=True), axis=0, keepdims=True)
    scaled = whole_gram * (1.0 / trace)
    upper, inverse = eliminate(jnp.where(diagonal, scaled + shift_ratio, scaled))
    root = jnp.sqrt(trace)
    return upper * root, inverse * (1.0 / root)


def wide_of(at_ref, z_refs):
    chunks = [z_ref[at_ref[i]] for z_ref in z_refs for i in range(at_ref.shape[0])]
    return jnp.concatenate(chunks, axis=1)


def first_pass(at_ref, z_refs):
    wide = wide_of(at_ref, z_refs)
    upper, inverse_one = shifted_factor(gram_of(wide))
    return small_times_wide(inverse_one, wide), upper


def back_product(at_ref, z_refs, a):
    first, unused = first_pass(at_ref, z_refs)
    rank = first.shape[0]
    terms = jnp.concatenate(terms_of(first), axis=0)
    tiles = []

    def tile(start):
        back = dot_nn(terms, a[:, start : start + TILE])
        tiles.append(back[:rank] + (back[rank : 2 * rank] + back[2 * rank :]))

    starts = range(0, a.shape[1], TILE)
    work = [functools.partial(tile, start) for start in starts]
    unused, inverse_two = eliminate(gram_of(first), work)
    return small_times_wide(inverse_two, jnp.concatenate(tiles, axis=1))


def forth_product(weights, a_ref, at_ref, part_ref):
    chunks, unused, width = part_ref.shape
    forth = dot_nt(weights.astype(jnp.bfloat16), a_ref[: chunks * width, :])
    for i in range(chunks):
        part_ref[at_ref[i]] = forth[:, width * i : width * (i + 1)]


def orth_kernel(at_ref, z_ref, other_ref, basis_ref, upper_ref):
    first, upper = first_pass(at_ref, (z_ref, other_ref))
    unused, inverse_two = eliminate(gram_of(first))
    basis_ref[...] = small_times_wide(inverse_two, first).astype(jnp.bfloat16)
    upper_ref[...] = upper


def power_kernel(at_ref, basis_ref, *refs):
    piece_refs, a_ref, part_ref = refs[:-2], refs[-2], refs[-1]
    rows = piece_refs[0].shape[0]
    for s, piece_ref in enumerate(piece_refs):
        a_ref[rows * s : rows * (s + 1), :] = piece_ref[...]
    forth_product(dot_nn(basis_ref[...], a_ref[...]), a_ref, at_ref, part_ref)


def orth_power_kernel(at_ref, z_ref, other_ref, a_ref, part_ref):
    weights = back_product(at_ref, (z_ref, other_ref), a_ref[...])
    forth_product(weights, a_ref, at_ref, part_ref)


def last_kernel(at_ref, core_ref, z_ref, other_ref, a_ref, out_ref):
    cols = out_ref.shape[1]
    start = pl.multiple_of(core_ref[0] * cols, cols)
    out_ref[...] = back_product(at_ref, (z_ref, other_ref), a_ref[:, pl.ds(start, cols)])


def call(kernel, out_shapes, flops, scalars, *operands):
    moved = sum(x.size * x.dtype.itemsize for x in operands)
    return pl.pallas_call(
        kernel,
        out_shape=out_shapes,
        in_specs=[pl.BlockSpec(memory_space=pltpu.SMEM)] * len(scalars)
        + [pl.BlockSpec(memory_space=pltpu.VMEM)] * len(operands),
        out_specs=jax.tree.map(lambda _: pl.BlockSpec(memory_space=pltpu.VMEM), out_shapes),
        compiler_params=pltpu.CompilerParams(vmem_limit_bytes=20 * 1024 * 1024),
        cost_estimate=pl.CostEstimate(flops=flops, bytes_accessed=moved, transcendentals=0),
    )(*scalars, *operands)


def bits(size):
    return [1 << k for k in range(size.bit_length() - 1)]


def from_xor(value, axis, offset):
    size = math.prod(lax.axis_size(name) for name in axis)
    return lax.ppermute(value, axis, [(i, i ^ offset) for i in range(size)])


def sum_parts(total, dtype):
    for bit in bits(lax.axis_size("col")):
        half = total.shape[0] // 2
        other = from_xor(total[half:].astype(dtype), ("col",), bit)
        total = total[:half] + other.astype(jnp.float32)
    for bit in bits(lax.axis_size("z")):
        mine = total.astype(dtype)
        total = mine.astype(jnp.float32) + from_xor(mine, ("z",), bit).astype(jnp.float32)
    return total.astype(dtype)


def gather_parts(own):
    for bit in bits(lax.axis_size("col"))[::-1]:
        own = jnp.concatenate([own, from_xor(own, ("col",), bit)])
    return own, from_xor(own, ("core",), 1)


def chunk_places(digits):
    n_z, n_col = lax.axis_size("z"), lax.axis_size("col")
    index = jnp.arange(n_z * n_col, dtype=jnp.int32)
    z_at, col_at = lax.axis_index("z"), lax.axis_index("col")
    column = index % n_col
    relative = {"z": index // n_col, "col": column ^ col_at}
    absolute = {"z": relative["z"] ^ z_at, "col": column}
    place = jnp.zeros_like(index)
    for axis, bit, is_relative in digits:
        place = place * 2 + ((relative if is_relative else absolute)[axis] // bit) % 2
    return place.astype(jnp.int32)


def per_device_transposed(sketch_base, states):
    n_z, n_core, n_col = lax.axis_size("z"), lax.axis_size("core"), lax.axis_size("col")
    n_row = n_z * n_core
    rows_local, width_local = states.shape
    rows_total, width_total = rows_local * n_row, width_local * n_col
    chunk = rows_local // n_col
    cols = width_local // n_z
    chunks = n_z * n_col
    z_at, col = lax.axis_index("z"), lax.axis_index("col")
    pieces = {}

    def move(slab, offset):
        block = lax.dynamic_slice_in_dim(slab, (z_at ^ offset) * cols, cols, 1)
        pieces[offset] = from_xor(block, ("z",), offset) if offset else block

    feature_index = col * width_local + jnp.arange(width_local, dtype=jnp.int32)
    omega = sketch_table(sketch_base[0], feature_index, RANK)
    z = lax.dot_general(
        omega, states, (((0,), (1,)), ((), ())), preferred_element_type=jnp.float32
    )
    z = z.reshape(RANK, n_col, chunk).transpose(1, 0, 2)
    z_bits = bits(n_z)[::-1]
    far = z_bits[0]
    move(states, 0)
    z, slab = lax.optimization_barrier((z, states))
    move(slab, far)
    z = jnp.concatenate([z, from_xor(z, ("z",), far)])
    z, slab = lax.optimization_barrier((z, slab))
    for offset in sorted(set(range(1, n_z)) - {far}, reverse=True):
        move(slab, offset)
    for bit in z_bits[1:]:
        z = jnp.concatenate([z, from_xor(z, ("z",), bit)])
    for bit in bits(n_col):
        z = z + from_xor(z, ("col",), bit)
    z, pieces[far] = lax.optimization_barrier((z, pieces[far]))
    z = z, from_xor(z, ("core",), 1)
    absolute_col = [("col", bit, False) for bit in bits(n_col)[::-1]]
    at_first = chunk_places([("z", bit, True) for bit in z_bits[::-1]] + absolute_col)
    relative_col = [("col", bit, True) for bit in bits(n_col)]
    at = chunk_places(relative_col + [("z", bit, False) for bit in z_bits])
    early = [0, far]
    late = [offset for offset in range(n_z) if offset not in early]
    others = {offset: from_xor(pieces[offset], ("core",), 1) for offset in early}

    f32 = jnp.float32
    square = jax.ShapeDtypeStruct((RANK, RANK), f32)
    wide = jax.ShapeDtypeStruct((RANK, rows_total), jnp.bfloat16)
    slab = jax.ShapeDtypeStruct((rows_total, cols), states.dtype)
    parts = jax.ShapeDtypeStruct((chunks, RANK, chunk), f32)
    loadings = jax.ShapeDtypeStruct((RANK, cols // n_core), f32)
    orth_flops = 8 * 64 * 64 * rows_total * 6
    flops = orth_flops + 4 * 64 * rows_total * cols

    basis, upper = call(orth_kernel, (wide, square), orth_flops, (at_first,), *z)
    basis, moved = lax.optimization_barrier((basis, [pieces[offset] for offset in late]))
    pieces.update(zip(late, moved))
    others.update((offset, from_xor(pieces[offset], ("core",), 1)) for offset in late)
    blocks = [half[offset] for half in (pieces, others) for offset in range(n_z)]
    factor = upper.T * (1.0 / math.sqrt(rows_total * width_total))
    a, total = call(power_kernel, (slab, parts), flops, (at,), basis, *blocks)
    z = gather_parts(sum_parts(total, f32))
    for step in range(POWER - 1):
        total = call(orth_power_kernel, parts, flops, (at,), *z, a)
        z = gather_parts(sum_parts(total, jnp.bfloat16))
    core = lax.axis_index("core")[None].astype(jnp.int32)
    return call(last_kernel, loadings, flops, (at, core), *z, a).T, factor


def local_gram(basis):
    return jnp.dot(basis.T, basis, precision=lax.Precision.HIGHEST)


def orthonormal_block(sketch):
    whole_gram = lax.psum(local_gram(sketch), "row")
    identity = jnp.eye(RANK, dtype=jnp.float32)
    lower = jnp.linalg.cholesky(whole_gram + shift_ratio * jnp.trace(whole_gram) * identity)
    first = jax.scipy.linalg.solve_triangular(lower, sketch.T, lower=True).T
    lower_two = jnp.linalg.cholesky(lax.psum(local_gram(first), "row"))
    return jax.scipy.linalg.solve_triangular(lower_two, first.T, lower=True).T, lower


def per_device_slabs(sketch_base, states):
    width_local = states.shape[1]
    rows_total = states.shape[0] * lax.axis_size("row")
    width_total = width_local * lax.axis_size("col")
    feature_index = lax.axis_index("col") * width_local + jnp.arange(width_local, dtype=jnp.int32)
    omega = sketch_table(sketch_base[0], feature_index, RANK)

    def row_basis(right):
        partial_sketch = jnp.dot(states, right, preferred_element_type=jnp.float32)
        basis_new, lower = orthonormal_block(lax.psum(partial_sketch, "col"))
        return basis_new.astype(jnp.bfloat16), lower

    def back(basis):
        return lax.dot_general(
            states, basis, (((0,), (0,)), ((), ())), preferred_element_type=jnp.float32
        )

    basis, first_lower = row_basis(omega)
    factor = first_lower * (1.0 / math.sqrt(rows_total * width_total))
    for step in range(POWER):
        basis, unused = row_basis(lax.psum(back(basis), "row").astype(jnp.bfloat16))
    return lax.psum_scatter(back(basis), "row", scatter_dimension=0, tiled=True), factor


def solution(mesh):
    n_grp, n_row, n_col = (mesh.shape[name] for name in ("grp", "row", "col"))
    fits = n_row % 2 == 0 and n_row & (n_row - 1) == 0

    def run(sketch_base, states):
        rows_local = states.shape[0] // (n_grp * n_row)
        width_local = states.shape[1] // n_col
        tiled = rows_local % (n_col * LANES) == 0 and width_local % (n_row * LANES) == 0
        if fits and tiled:
            split = mesh.devices.reshape(n_grp, n_row // 2, 2, n_col)
            inner = jax.sharding.Mesh(split, ("grp", "z", "core", "col"))
            row, step = ("z", "core"), per_device_transposed
        else:
            inner, row, step = mesh, ("row",), per_device_slabs
        return jax.shard_map(
            step,
            mesh=inner,
            in_specs=(P("grp"), P(("grp",) + row, "col")),
            out_specs=(P(("col",) + row, "grp"), P("grp", None)),
            check_vma=False,
        )(sketch_base, states)

    return run
```

```python
import functools
import math

import jax
import jax.numpy as jnp
from jax import lax
from jax.experimental import pallas as pl
from jax.experimental.pallas import tpu as pltpu
from jax.sharding import PartitionSpec as P

RANK = 64
POWER = 4
LANES = 128
SUB = 8
TILE = 256


shift_ratio = 0.005


def scramble(value):
    value = value ^ jnp.right_shift(value, 16) & 65535
    value = value * 73244475
    value = value ^ jnp.right_shift(value, 16) & 65535
    value = value * 73244475
    value = value ^ jnp.right_shift(value, 16) & 65535
    return value


def sketch_table(base_value, feature_index, rank):
    counter = feature_index[:, None] * rank + jnp.arange(rank, dtype=jnp.int32)[None, :]
    offset = scramble(base_value)
    total = jnp.zeros(counter.shape, jnp.float32)
    for j in range(4):
        hashed = scramble(counter * 4 + j + offset)
        total = total + (hashed & 16777215).astype(jnp.float32) * (1.0 / 16777216.0)
    return ((total - 2.0) * 1.7320508).astype(jnp.bfloat16)


def terms_of(value):
    if value.dtype == jnp.bfloat16:
        return [value]
    high = value.astype(jnp.bfloat16)
    rest = value - high.astype(jnp.float32)
    middle = rest.astype(jnp.bfloat16)
    low = (rest - middle.astype(jnp.float32)).astype(jnp.bfloat16)
    return [high, middle, low]


def dot_nn(left, right):
    return lax.dot_general(
        left, right, (((1,), (0,)), ((), ())), preferred_element_type=jnp.float32
    )


def dot_nt(left, right):
    return lax.dot_general(
        left, right, (((1,), (1,)), ((), ())), preferred_element_type=jnp.float32
    )


def small_times_wide(small, wide):
    left, right = terms_of(small), terms_of(wide)
    pairs = [(i, d - i) for d in (2, 1, 0) for i in range(d + 1)]
    pairs = [(i, j) for i, j in pairs if i < len(left) and j < len(right)]
    return dot_nn(
        jnp.concatenate([left[i] for i, unused in pairs], axis=1),
        jnp.concatenate([right[j] for unused, j in pairs], axis=0),
    )


def gram_of(wide):
    terms = terms_of(wide)
    if len(terms) == 1:
        return dot_nt(terms[0], terms[0])
    rank = wide.shape[0]
    stacked = jnp.concatenate(terms, axis=0)
    both = dot_nt(stacked, stacked)
    cross = both[rank : 2 * rank, :rank] + both[2 * rank :, :rank]
    return both[:rank, :rank] + ((cross + cross.T) + both[rank : 2 * rank, rank : 2 * rank])


def eliminate(matrix, beside=()):
    beside = list(beside)
    size = matrix.shape[0]
    blocks = size // SUB
    row_index = lax.broadcasted_iota(jnp.int32, (SUB, 2 * size), 0)
    square_row = lax.broadcasted_iota(jnp.int32, (SUB, size), 0)
    square_col = lax.broadcasted_iota(jnp.int32, (SUB, size), 1)
    work = []
    for i in range(blocks):
        unit = jnp.where(square_col == square_row + SUB * i, 1.0, 0.0).astype(jnp.float32)
        work.append(jnp.concatenate([matrix[SUB * i : SUB * (i + 1), :], unit], axis=1))

    def fill(register, k):
        return jnp.broadcast_to(register[k : k + 1, :], (SUB, 2 * size))

    rows = []
    for b in range(blocks):
        for unused in range(-(-len(beside) // (blocks - b))):
            beside.pop(0)()
        columns = [
            {
                i: jnp.broadcast_to(work[i][:, SUB * b + j : SUB * b + j + 1], (SUB, 2 * size))
                for i in range(b, blocks)
            }
            for j in range(SUB)
        ]
        pivots = jnp.ones((SUB, 2 * size), jnp.float32)
        for k in range(0, SUB, 2):
            col_0, col_1 = columns[k], columns[k + 1]
            a, h, d = fill(col_0[b], k), fill(col_1[b], k), fill(col_1[b], k + 1)
            det = a * d - h * h
            over_det, over_a = 1.0 / det, 1.0 / a
            below_0 = jnp.where(row_index > k + 1, col_0[b], 0.0)
            below_1 = jnp.where(row_index > k + 1, col_1[b], 0.0)
            for j in range(k + 2, SUB):
                entry_0, entry_1 = fill(columns[j][b], k), fill(columns[j][b], k + 1)
                up_0 = d * entry_0 - h * entry_1
                up_1 = a * entry_1 - h * entry_0
                columns[j][b] = columns[j][b] - over_det * (below_0 * up_0 + below_1 * up_1)
                up_0, up_1 = over_det * up_0, over_det * up_1
                for i in range(b + 1, blocks):
                    columns[j][i] = columns[j][i] - (col_0[i] * up_0 + col_1[i] * up_1)
            row_0, row_1 = fill(work[b], k), fill(work[b], k + 1)
            up_0 = over_det * (d * row_0 - h * row_1)
            up_1 = over_det * (a * row_1 - h * row_0)
            for i in range(b + 1, blocks):
                work[i] = work[i] - (col_0[i] * up_0 + col_1[i] * up_1)
            second = jnp.where(row_index == k + 1, h * over_a, 0.0)
            work[b] = work[b] - (below_0 * up_0 + below_1 * up_1 + second * row_0)
            pivots = jnp.where(row_index == k, a, pivots)
            pivots = jnp.where(row_index == k + 1, det * over_a, pivots)
        rows.append(work[b] * lax.rsqrt(pivots))
    both = jnp.concatenate(rows, axis=0)
    keep = lax.broadcasted_iota(jnp.int32, (size, size), 1) >= lax.broadcasted_iota(
        jnp.int32, (size, size), 0
    )
    return jnp.where(keep, both[:, :size], 0.0), both[:, size:]


def shifted_factor(whole_gram):
    size = whole_gram.shape[0]
    diagonal = lax.broadcasted_iota(jnp.int32, (size, size), 0) == lax.broadcasted_iota(
        jnp.int32, (size, size), 1
    )
    on_diagonal = jnp.where(diagonal, whole_gram, 0.0)
    trace = jnp.sum(jnp.sum(on_diagonal, axis=1, keepdims=True), axis=0, keepdims=True)
    scaled = whole_gram * (1.0 / trace)
    upper, inverse = eliminate(jnp.where(diagonal, scaled + shift_ratio, scaled))
    root = jnp.sqrt(trace)
    return upper * root, inverse * (1.0 / root)


def wide_of(at_ref, z_refs):
    chunks = [z_ref[at_ref[i]] for z_ref in z_refs for i in range(at_ref.shape[0])]
    return jnp.concatenate(chunks, axis=1)


def first_pass(at_ref, z_refs):
    wide = wide_of(at_ref, z_refs)
    upper, inverse_one = shifted_factor(gram_of(wide))
    return small_times_wide(inverse_one, wide), upper


def back_product(at_ref, z_refs, a):
    first, unused = first_pass(at_ref, z_refs)
    rank = first.shape[0]
    terms = jnp.concatenate(terms_of(first), axis=0)
    tiles = []

    def tile(start):
        back = dot_nn(terms, a[:, start : start + TILE])
        tiles.append(back[:rank] + (back[rank : 2 * rank] + back[2 * rank :]))

    starts = range(0, a.shape[1], TILE)
    work = [functools.partial(tile, start) for start in starts]
    unused, inverse_two = eliminate(gram_of(first), work)
    return small_times_wide(inverse_two, jnp.concatenate(tiles, axis=1))


def forth_product(weights, a_ref, at_ref, part_ref):
    chunks, unused, width = part_ref.shape
    forth = dot_nt(weights.astype(jnp.bfloat16), a_ref[: chunks * width, :])
    for i in range(chunks):
        part_ref[at_ref[i]] = forth[:, width * i : width * (i + 1)]


def orth_kernel(at_ref, z_ref, other_ref, basis_ref, upper_ref):
    first, upper = first_pass(at_ref, (z_ref, other_ref))
    unused, inverse_two = eliminate(gram_of(first))
    basis_ref[...] = small_times_wide(inverse_two, first).astype(jnp.bfloat16)
    upper_ref[...] = upper


def power_kernel(at_ref, basis_ref, *refs):
    piece_refs, a_ref, part_ref = refs[:-2], refs[-2], refs[-1]
    start = 0
    for piece_ref in piece_refs:
        a_ref[start : start + piece_ref.shape[0], :] = piece_ref[...]
        start += piece_ref.shape[0]
    forth_product(dot_nn(basis_ref[...], a_ref[...]), a_ref, at_ref, part_ref)


def orth_power_kernel(at_ref, z_ref, other_ref, a_ref, part_ref):
    weights = back_product(at_ref, (z_ref, other_ref), a_ref[...])
    forth_product(weights, a_ref, at_ref, part_ref)


def last_kernel(at_ref, core_ref, z_ref, other_ref, a_ref, out_ref):
    cols = out_ref.shape[1]
    start = pl.multiple_of(core_ref[0] * cols, cols)
    out_ref[...] = back_product(at_ref, (z_ref, other_ref), a_ref[:, pl.ds(start, cols)])


def call(kernel, out_shapes, flops, scalars, *operands):
    moved = sum(x.size * x.dtype.itemsize for x in operands)
    return pl.pallas_call(
        kernel,
        out_shape=out_shapes,
        in_specs=[pl.BlockSpec(memory_space=pltpu.SMEM)] * len(scalars)
        + [pl.BlockSpec(memory_space=pltpu.VMEM)] * len(operands),
        out_specs=jax.tree.map(lambda _: pl.BlockSpec(memory_space=pltpu.VMEM), out_shapes),
        compiler_params=pltpu.CompilerParams(vmem_limit_bytes=20 * 1024 * 1024),
        cost_estimate=pl.CostEstimate(flops=flops, bytes_accessed=moved, transcendentals=0),
    )(*scalars, *operands)


def bits(size):
    return [1 << k for k in range(size.bit_length() - 1)]


def from_xor(value, axis, offset):
    size = math.prod(lax.axis_size(name) for name in axis)
    return lax.ppermute(value, axis, [(i, i ^ offset) for i in range(size)])


def sum_parts(total, dtype):
    for bit in bits(lax.axis_size("col")):
        half = total.shape[0] // 2
        other = from_xor(total[half:].astype(dtype), ("col",), bit)
        total = total[:half] + other.astype(jnp.float32)
    for bit in bits(lax.axis_size("z")):
        mine = total.astype(dtype)
        total = mine.astype(jnp.float32) + from_xor(mine, ("z",), bit).astype(jnp.float32)
    return total.astype(dtype)


def gather_parts(own):
    for bit in bits(lax.axis_size("col"))[::-1]:
        own = jnp.concatenate([own, from_xor(own, ("col",), bit)])
    return own, from_xor(own, ("core",), 1)


def chunk_places(digits):
    n_z, n_col = lax.axis_size("z"), lax.axis_size("col")
    index = jnp.arange(n_z * n_col, dtype=jnp.int32)
    z_at, col_at = lax.axis_index("z"), lax.axis_index("col")
    column = index % n_col
    relative = {"z": index // n_col, "col": column ^ col_at}
    absolute = {"z": relative["z"] ^ z_at, "col": column}
    place = jnp.zeros_like(index)
    for axis, bit, is_relative in digits:
        place = place * 2 + ((relative if is_relative else absolute)[axis] // bit) % 2
    return place.astype(jnp.int32)


def per_device_transposed(sketch_base, states):
    n_z, n_core, n_col = lax.axis_size("z"), lax.axis_size("core"), lax.axis_size("col")
    n_row = n_z * n_core
    rows_local, width_local = states.shape
    rows_total, width_total = rows_local * n_row, width_local * n_col
    chunk = rows_local // n_col
    cols = width_local // n_z
    chunks = n_z * n_col
    z_at, col = lax.axis_index("z"), lax.axis_index("col")
    pieces = {}

    def move(slab, offset, part=0, parts=1):
        rows = rows_local // parts
        start = (part * rows, (z_at ^ offset) * cols)
        block = lax.dynamic_slice(slab, start, (rows, cols))
        pieces[offset, part] = from_xor(block, ("z",), offset) if offset else block

    def hold(value, names):
        value, moved = lax.optimization_barrier((value, [pieces[name] for name in names]))
        pieces.update(zip(names, moved))
        return value

    feature_index = col * width_local + jnp.arange(width_local, dtype=jnp.int32)
    omega = sketch_table(sketch_base[0], feature_index, RANK)
    z = lax.dot_general(
        omega, states, (((0,), (1,)), ((), ())), preferred_element_type=jnp.float32
    )
    z = z.reshape(RANK, n_col, chunk).transpose(1, 0, 2)
    z_bits = bits(n_z)[::-1]
    far = z_bits[0]
    for offset in [0, far, *range(1, far)]:
        move(states, offset)
    first = list(pieces)
    z = jnp.concatenate([z, from_xor(z, ("z",), far)])
    z, slab = lax.optimization_barrier((z, states))
    for offset in range(far + 1, n_z):
        move(slab, offset, 0, 2)
        move(slab, offset, 1, 2)
    for bit in bits(n_col):
        z = z + from_xor(z, ("col",), bit)
    z = hold(z, first)
    for bit in z_bits[1:]:
        z = jnp.concatenate([z, from_xor(z, ("z",), bit)])
    z = hold(z, [(offset, 0) for offset in range(far + 1, n_z)])
    z = z, from_xor(z, ("core",), 1)
    absolute_col = [("col", bit, False) for bit in bits(n_col)[::-1]]
    at_first = chunk_places([("z", bit, True) for bit in z_bits[::-1]] + absolute_col)
    relative_col = [("col", bit, True) for bit in bits(n_col)]
    at = chunk_places(relative_col + [("z", bit, False) for bit in z_bits])
    late = [name for name in pieces if name[0] > far]
    others = {name: from_xor(pieces[name], ("core",), 1) for name in first}

    f32 = jnp.float32
    square = jax.ShapeDtypeStruct((RANK, RANK), f32)
    wide = jax.ShapeDtypeStruct((RANK, rows_total), jnp.bfloat16)
    slab = jax.ShapeDtypeStruct((rows_total, cols), states.dtype)
    parts = jax.ShapeDtypeStruct((chunks, RANK, chunk), f32)
    loadings = jax.ShapeDtypeStruct((RANK, cols // n_core), f32)
    orth_flops = 8 * 64 * 64 * rows_total * 6
    flops = orth_flops + 4 * 64 * rows_total * cols

    basis, upper = call(orth_kernel, (wide, square), orth_flops, (at_first,), *z)
    basis = hold(basis, late)
    others.update((name, from_xor(pieces[name], ("core",), 1)) for name in late)
    blocks = [half[name] for half in (pieces, others) for name in sorted(half)]
    factor = upper.T * (1.0 / math.sqrt(rows_total * width_total))
    a, total = call(power_kernel, (slab, parts), flops, (at,), basis, *blocks)
    z = gather_parts(sum_parts(total, f32))
    for step in range(POWER - 1):
        total = call(orth_power_kernel, parts, flops, (at,), *z, a)
        z = gather_parts(sum_parts(total, jnp.bfloat16))
    core = lax.axis_index("core")[None].astype(jnp.int32)
    return call(last_kernel, loadings, flops, (at, core), *z, a).T, factor


def local_gram(basis):
    return jnp.dot(basis.T, basis, precision=lax.Precision.HIGHEST)


def orthonormal_block(sketch):
    whole_gram = lax.psum(local_gram(sketch), "row")
    identity = jnp.eye(RANK, dtype=jnp.float32)
    lower = jnp.linalg.cholesky(whole_gram + shift_ratio * jnp.trace(whole_gram) * identity)
    first = jax.scipy.linalg.solve_triangular(lower, sketch.T, lower=True).T
    lower_two = jnp.linalg.cholesky(lax.psum(local_gram(first), "row"))
    return jax.scipy.linalg.solve_triangular(lower_two, first.T, lower=True).T, lower


def per_device_slabs(sketch_base, states):
    width_local = states.shape[1]
    rows_total = states.shape[0] * lax.axis_size("row")
    width_total = width_local * lax.axis_size("col")
    feature_index = lax.axis_index("col") * width_local + jnp.arange(width_local, dtype=jnp.int32)
    omega = sketch_table(sketch_base[0], feature_index, RANK)

    def row_basis(right):
        partial_sketch = jnp.dot(states, right, preferred_element_type=jnp.float32)
        basis_new, lower = orthonormal_block(lax.psum(partial_sketch, "col"))
        return basis_new.astype(jnp.bfloat16), lower

    def back(basis):
        return lax.dot_general(
            states, basis, (((0,), (0,)), ((), ())), preferred_element_type=jnp.float32
        )

    basis, first_lower = row_basis(omega)
    factor = first_lower * (1.0 / math.sqrt(rows_total * width_total))
    for step in range(POWER):
        basis, unused = row_basis(lax.psum(back(basis), "row").astype(jnp.bfloat16))
    return lax.psum_scatter(back(basis), "row", scatter_dimension=0, tiled=True), factor


def solution(mesh):
    n_grp, n_row, n_col = (mesh.shape[name] for name in ("grp", "row", "col"))
    fits = n_row >= 4 and n_row & (n_row - 1) == 0

    def run(sketch_base, states):
        rows_local = states.shape[0] // (n_grp * n_row)
        width_local = states.shape[1] // n_col
        tiled = rows_local % (n_col * LANES) == 0 and width_local % (n_row * LANES) == 0
        if fits and tiled:
            split = mesh.devices.reshape(n_grp, n_row // 2, 2, n_col)
            inner = jax.sharding.Mesh(split, ("grp", "z", "core", "col"))
            row, step = ("z", "core"), per_device_transposed
        else:
            inner, row, step = mesh, ("row",), per_device_slabs
        return jax.shard_map(
            step,
            mesh=inner,
            in_specs=(P("grp"), P(("grp",) + row, "col")),
            out_specs=(P(("col",) + row, "grp"), P("grp", None)),
            check_vma=False,
        )(sketch_base, states)

    return run
```

```python
import functools
import math

import jax
import jax.numpy as jnp
from jax import lax
from jax.experimental import pallas as pl
from jax.experimental.pallas import tpu as pltpu
from jax.sharding import PartitionSpec as P

RANK = 64
POWER = 4
LANES = 128
SUB = 8
TILE = 256


shift_ratio = 0.005


def scramble(value):
    value = value ^ jnp.right_shift(value, 16) & 65535
    value = value * 73244475
    value = value ^ jnp.right_shift(value, 16) & 65535
    value = value * 73244475
    value = value ^ jnp.right_shift(value, 16) & 65535
    return value


def sketch_table(base_value, feature_index, rank):
    counter = feature_index[:, None] * rank + jnp.arange(rank, dtype=jnp.int32)[None, :]
    offset = scramble(base_value)
    total = jnp.zeros(counter.shape, jnp.float32)
    for j in range(4):
        hashed = scramble(counter * 4 + j + offset)
        total = total + (hashed & 16777215).astype(jnp.float32) * (1.0 / 16777216.0)
    return ((total - 2.0) * 1.7320508).astype(jnp.bfloat16)


def terms_of(value):
    if value.dtype == jnp.bfloat16:
        return [value]
    high = value.astype(jnp.bfloat16)
    rest = value - high.astype(jnp.float32)
    middle = rest.astype(jnp.bfloat16)
    low = (rest - middle.astype(jnp.float32)).astype(jnp.bfloat16)
    return [high, middle, low]


def dot_nn(left, right):
    return lax.dot_general(
        left, right, (((1,), (0,)), ((), ())), preferred_element_type=jnp.float32
    )


def dot_nt(left, right):
    return lax.dot_general(
        left, right, (((1,), (1,)), ((), ())), preferred_element_type=jnp.float32
    )


def small_times_wide(small, wide):
    left, right = terms_of(small), terms_of(wide)
    pairs = [(i, d - i) for d in (2, 1, 0) for i in range(d + 1)]
    pairs = [(i, j) for i, j in pairs if i < len(left) and j < len(right)]
    return dot_nn(
        jnp.concatenate([left[i] for i, unused in pairs], axis=1),
        jnp.concatenate([right[j] for unused, j in pairs], axis=0),
    )


def gram_of(wide):
    terms = terms_of(wide)
    if len(terms) == 1:
        return dot_nt(terms[0], terms[0])
    rank = wide.shape[0]
    stacked = jnp.concatenate(terms, axis=0)
    both = dot_nt(stacked, stacked)
    cross = both[rank : 2 * rank, :rank] + both[2 * rank :, :rank]
    return both[:rank, :rank] + ((cross + cross.T) + both[rank : 2 * rank, rank : 2 * rank])


def eliminate(matrix, beside=()):
    beside = list(beside)
    size = matrix.shape[0]
    blocks = size // SUB
    row_index = lax.broadcasted_iota(jnp.int32, (SUB, 2 * size), 0)
    square_row = lax.broadcasted_iota(jnp.int32, (SUB, size), 0)
    square_col = lax.broadcasted_iota(jnp.int32, (SUB, size), 1)
    work = []
    for i in range(blocks):
        unit = jnp.where(square_col == square_row + SUB * i, 1.0, 0.0).astype(jnp.float32)
        work.append(jnp.concatenate([matrix[SUB * i : SUB * (i + 1), :], unit], axis=1))

    def fill(register, k):
        return jnp.broadcast_to(register[k : k + 1, :], (SUB, 2 * size))

    rows = []
    for b in range(blocks):
        for unused in range(-(-len(beside) // (blocks - b))):
            beside.pop(0)()
        columns = [
            {
                i: jnp.broadcast_to(work[i][:, SUB * b + j : SUB * b + j + 1], (SUB, 2 * size))
                for i in range(b, blocks)
            }
            for j in range(SUB)
        ]
        pivots = jnp.ones((SUB, 2 * size), jnp.float32)
        for k in range(0, SUB, 2):
            col_0, col_1 = columns[k], columns[k + 1]
            a, h, d = fill(col_0[b], k), fill(col_1[b], k), fill(col_1[b], k + 1)
            det = a * d - h * h
            over_det, over_a = 1.0 / det, 1.0 / a
            below_0 = jnp.where(row_index > k + 1, col_0[b], 0.0)
            below_1 = jnp.where(row_index > k + 1, col_1[b], 0.0)
            for j in range(k + 2, SUB):
                entry_0, entry_1 = fill(columns[j][b], k), fill(columns[j][b], k + 1)
                up_0 = d * entry_0 - h * entry_1
                up_1 = a * entry_1 - h * entry_0
                columns[j][b] = columns[j][b] - over_det * (below_0 * up_0 + below_1 * up_1)
                up_0, up_1 = over_det * up_0, over_det * up_1
                for i in range(b + 1, blocks):
                    columns[j][i] = columns[j][i] - (col_0[i] * up_0 + col_1[i] * up_1)
            row_0, row_1 = fill(work[b], k), fill(work[b], k + 1)
            up_0 = over_det * (d * row_0 - h * row_1)
            up_1 = over_det * (a * row_1 - h * row_0)
            for i in range(b + 1, blocks):
                work[i] = work[i] - (col_0[i] * up_0 + col_1[i] * up_1)
            second = jnp.where(row_index == k + 1, h * over_a, 0.0)
            work[b] = work[b] - (below_0 * up_0 + below_1 * up_1 + second * row_0)
            pivots = jnp.where(row_index == k, a, pivots)
            pivots = jnp.where(row_index == k + 1, det * over_a, pivots)
        rows.append(work[b] * lax.rsqrt(pivots))
    both = jnp.concatenate(rows, axis=0)
    keep = lax.broadcasted_iota(jnp.int32, (size, size), 1) >= lax.broadcasted_iota(
        jnp.int32, (size, size), 0
    )
    return jnp.where(keep, both[:, :size], 0.0), both[:, size:]


def shifted_factor(whole_gram):
    size = whole_gram.shape[0]
    diagonal = lax.broadcasted_iota(jnp.int32, (size, size), 0) == lax.broadcasted_iota(
        jnp.int32, (size, size), 1
    )
    on_diagonal = jnp.where(diagonal, whole_gram, 0.0)
    trace = jnp.sum(jnp.sum(on_diagonal, axis=1, keepdims=True), axis=0, keepdims=True)
    scaled = whole_gram * (1.0 / trace)
    upper, inverse = eliminate(jnp.where(diagonal, scaled + shift_ratio, scaled))
    root = jnp.sqrt(trace)
    return upper * root, inverse * (1.0 / root)


def wide_of(at_ref, z_refs):
    chunks = [z_ref[at_ref[i]] for z_ref in z_refs for i in range(at_ref.shape[0])]
    return jnp.concatenate(chunks, axis=1)


def first_pass(at_ref, z_refs):
    wide = wide_of(at_ref, z_refs)
    upper, inverse_one = shifted_factor(gram_of(wide))
    return small_times_wide(inverse_one, wide), upper


def back_product(at_ref, z_refs, a):
    first, unused = first_pass(at_ref, z_refs)
    rank = first.shape[0]
    terms = jnp.concatenate(terms_of(first), axis=0)
    tiles = []

    def tile(start):
        back = dot_nn(terms, a[:, start : start + TILE])
        tiles.append(back[:rank] + (back[rank : 2 * rank] + back[2 * rank :]))

    starts = range(0, a.shape[1], TILE)
    work = [functools.partial(tile, start) for start in starts]
    unused, inverse_two = eliminate(gram_of(first), work)
    return small_times_wide(inverse_two, jnp.concatenate(tiles, axis=1))


def forth_product(weights, a_ref, at_ref, part_ref):
    chunks, unused, width = part_ref.shape
    forth = dot_nt(weights.astype(jnp.bfloat16), a_ref[: chunks * width, :])
    for i in range(chunks):
        part_ref[at_ref[i]] = forth[:, width * i : width * (i + 1)]


def orth_kernel(at_ref, z_ref, other_ref, basis_ref, upper_ref):
    first, upper = first_pass(at_ref, (z_ref, other_ref))
    unused, inverse_two = eliminate(gram_of(first))
    basis_ref[...] = small_times_wide(inverse_two, first).astype(jnp.bfloat16)
    upper_ref[...] = upper


def power_kernel(at_ref, basis_ref, *refs):
    piece_refs, a_ref, part_ref = refs[:-2], refs[-2], refs[-1]
    start = 0
    for piece_ref in piece_refs:
        a_ref[start : start + piece_ref.shape[0], :] = piece_ref[...]
        start += piece_ref.shape[0]
    forth_product(dot_nn(basis_ref[...], a_ref[...]), a_ref, at_ref, part_ref)


def orth_power_kernel(at_ref, z_ref, other_ref, a_ref, part_ref):
    weights = back_product(at_ref, (z_ref, other_ref), a_ref[...])
    forth_product(weights, a_ref, at_ref, part_ref)


def last_kernel(at_ref, core_ref, z_ref, other_ref, a_ref, out_ref):
    cols = out_ref.shape[1]
    start = pl.multiple_of(core_ref[0] * cols, cols)
    out_ref[...] = back_product(at_ref, (z_ref, other_ref), a_ref[:, pl.ds(start, cols)])


def call(kernel, out_shapes, flops, scalars, *operands):
    moved = sum(x.size * x.dtype.itemsize for x in operands)
    return pl.pallas_call(
        kernel,
        out_shape=out_shapes,
        in_specs=[pl.BlockSpec(memory_space=pltpu.SMEM)] * len(scalars)
        + [pl.BlockSpec(memory_space=pltpu.VMEM)] * len(operands),
        out_specs=jax.tree.map(lambda _: pl.BlockSpec(memory_space=pltpu.VMEM), out_shapes),
        compiler_params=pltpu.CompilerParams(vmem_limit_bytes=20 * 1024 * 1024),
        cost_estimate=pl.CostEstimate(flops=flops, bytes_accessed=moved, transcendentals=0),
    )(*scalars, *operands)


def bits(size):
    return [1 << k for k in range(size.bit_length() - 1)]


def from_xor(value, axis, offset):
    size = math.prod(lax.axis_size(name) for name in axis)
    return lax.ppermute(value, axis, [(i, i ^ offset) for i in range(size)])


def sum_parts(total, dtype):
    for bit in bits(lax.axis_size("col")):
        half = total.shape[0] // 2
        other = from_xor(total[half:].astype(dtype), ("col",), bit)
        total = total[:half] + other.astype(jnp.float32)
    for bit in bits(lax.axis_size("z")):
        mine = total.astype(dtype)
        total = mine.astype(jnp.float32) + from_xor(mine, ("z",), bit).astype(jnp.float32)
    return total.astype(dtype)


def gather_parts(own):
    for bit in bits(lax.axis_size("col"))[::-1]:
        own = jnp.concatenate([own, from_xor(own, ("col",), bit)])
    return own, from_xor(own, ("core",), 1)


def chunk_places(digits):
    n_z, n_col = lax.axis_size("z"), lax.axis_size("col")
    index = jnp.arange(n_z * n_col, dtype=jnp.int32)
    z_at, col_at = lax.axis_index("z"), lax.axis_index("col")
    column = index % n_col
    relative = {"z": index // n_col, "col": column ^ col_at}
    absolute = {"z": relative["z"] ^ z_at, "col": column}
    place = jnp.zeros_like(index)
    for axis, bit, is_relative in digits:
        place = place * 2 + ((relative if is_relative else absolute)[axis] // bit) % 2
    return place.astype(jnp.int32)


def per_device_transposed(sketch_base, states):
    n_z, n_core, n_col = lax.axis_size("z"), lax.axis_size("core"), lax.axis_size("col")
    n_row = n_z * n_core
    rows_local, width_local = states.shape
    rows_total, width_total = rows_local * n_row, width_local * n_col
    chunk = rows_local // n_col
    cols = width_local // n_z
    chunks = n_z * n_col
    z_at, col = lax.axis_index("z"), lax.axis_index("col")
    pieces = {}

    def move(slab, offset, part=0, parts=1):
        rows = rows_local // parts
        start = (part * rows, (z_at ^ offset) * cols)
        block = lax.dynamic_slice(slab, start, (rows, cols))
        pieces[offset, part] = from_xor(block, ("z",), offset) if offset else block

    def hold(value, names):
        value, moved = lax.optimization_barrier((value, [pieces[name] for name in names]))
        pieces.update(zip(names, moved))
        return value

    feature_index = col * width_local + jnp.arange(width_local, dtype=jnp.int32)
    omega = sketch_table(sketch_base[0], feature_index, RANK)
    z = lax.dot_general(
        omega, states, (((0,), (1,)), ((), ())), preferred_element_type=jnp.float32
    )
    z = z.reshape(RANK, n_col, chunk).transpose(1, 0, 2)
    z_bits = bits(n_z)[::-1]
    far = z_bits[0]
    for offset in [0, far]:
        move(states, offset)
    first = list(pieces)
    z = jnp.concatenate([z, from_xor(z, ("z",), far)])
    z, slab = lax.optimization_barrier((z, states))
    for offset in range(far + 1, n_z):
        move(slab, offset, 0, 2)
        move(slab, offset, 1, 2)
    for offset in range(1, far):
        move(slab, offset)
    for bit in bits(n_col):
        z = z + from_xor(z, ("col",), bit)
    z = hold(z, first)
    for bit in z_bits[1:]:
        z = jnp.concatenate([z, from_xor(z, ("z",), bit)])
    z = hold(z, [(offset, 0) for offset in range(far + 1, n_z)])
    z = z, from_xor(z, ("core",), 1)
    absolute_col = [("col", bit, False) for bit in bits(n_col)[::-1]]
    at_first = chunk_places([("z", bit, True) for bit in z_bits[::-1]] + absolute_col)
    relative_col = [("col", bit, True) for bit in bits(n_col)]
    at = chunk_places(relative_col + [("z", bit, False) for bit in z_bits])
    late = [name for name in pieces if name not in first]
    others = {name: from_xor(pieces[name], ("core",), 1) for name in first}

    f32 = jnp.float32
    square = jax.ShapeDtypeStruct((RANK, RANK), f32)
    wide = jax.ShapeDtypeStruct((RANK, rows_total), jnp.bfloat16)
    slab = jax.ShapeDtypeStruct((rows_total, cols), states.dtype)
    parts = jax.ShapeDtypeStruct((chunks, RANK, chunk), f32)
    loadings = jax.ShapeDtypeStruct((RANK, cols // n_core), f32)
    orth_flops = 8 * 64 * 64 * rows_total * 6
    flops = orth_flops + 4 * 64 * rows_total * cols

    basis, upper = call(orth_kernel, (wide, square), orth_flops, (at_first,), *z)
    basis = hold(basis, late)
    others.update((name, from_xor(pieces[name], ("core",), 1)) for name in late)
    blocks = [half[name] for half in (pieces, others) for name in sorted(half)]
    factor = upper.T * (1.0 / math.sqrt(rows_total * width_total))
    a, total = call(power_kernel, (slab, parts), flops, (at,), basis, *blocks)
    z = gather_parts(sum_parts(total, f32))
    for step in range(POWER - 1):
        total = call(orth_power_kernel, parts, flops, (at,), *z, a)
        z = gather_parts(sum_parts(total, jnp.bfloat16))
    core = lax.axis_index("core")[None].astype(jnp.int32)
    return call(last_kernel, loadings, flops, (at, core), *z, a).T, factor


def local_gram(basis):
    return jnp.dot(basis.T, basis, precision=lax.Precision.HIGHEST)


def orthonormal_block(sketch):
    whole_gram = lax.psum(local_gram(sketch), "row")
    identity = jnp.eye(RANK, dtype=jnp.float32)
    lower = jnp.linalg.cholesky(whole_gram + shift_ratio * jnp.trace(whole_gram) * identity)
    first = jax.scipy.linalg.solve_triangular(lower, sketch.T, lower=True).T
    lower_two = jnp.linalg.cholesky(lax.psum(local_gram(first), "row"))
    return jax.scipy.linalg.solve_triangular(lower_two, first.T, lower=True).T, lower


def per_device_slabs(sketch_base, states):
    width_local = states.shape[1]
    rows_total = states.shape[0] * lax.axis_size("row")
    width_total = width_local * lax.axis_size("col")
    feature_index = lax.axis_index("col") * width_local + jnp.arange(width_local, dtype=jnp.int32)
    omega = sketch_table(sketch_base[0], feature_index, RANK)

    def row_basis(right):
        partial_sketch = jnp.dot(states, right, preferred_element_type=jnp.float32)
        basis_new, lower = orthonormal_block(lax.psum(partial_sketch, "col"))
        return basis_new.astype(jnp.bfloat16), lower

    def back(basis):
        return lax.dot_general(
            states, basis, (((0,), (0,)), ((), ())), preferred_element_type=jnp.float32
        )

    basis, first_lower = row_basis(omega)
    factor = first_lower * (1.0 / math.sqrt(rows_total * width_total))
    for step in range(POWER):
        basis, unused = row_basis(lax.psum(back(basis), "row").astype(jnp.bfloat16))
    return lax.psum_scatter(back(basis), "row", scatter_dimension=0, tiled=True), factor


def solution(mesh):
    n_grp, n_row, n_col = (mesh.shape[name] for name in ("grp", "row", "col"))
    fits = n_row >= 4 and n_row & (n_row - 1) == 0

    def run(sketch_base, states):
        rows_local = states.shape[0] // (n_grp * n_row)
        width_local = states.shape[1] // n_col
        tiled = rows_local % (n_col * LANES) == 0 and width_local % (n_row * LANES) == 0
        if fits and tiled:
            split = mesh.devices.reshape(n_grp, n_row // 2, 2, n_col)
            inner = jax.sharding.Mesh(split, ("grp", "z", "core", "col"))
            row, step = ("z", "core"), per_device_transposed
        else:
            inner, row, step = mesh, ("row",), per_device_slabs
        return jax.shard_map(
            step,
            mesh=inner,
            in_specs=(P("grp"), P(("grp",) + row, "col")),
            out_specs=(P(("col",) + row, "grp"), P("grp", None)),
            check_vma=False,
        )(sketch_base, states)

    return run
```

```python
import functools
import math

import jax
import jax.numpy as jnp
from jax import lax
from jax.experimental import pallas as pl
from jax.experimental.pallas import tpu as pltpu
from jax.sharding import PartitionSpec as P

RANK = 64
POWER = 4
LANES = 128
SUB = 8
TILE = 256


shift_ratio = 0.005


def scramble(value):
    value = value ^ jnp.right_shift(value, 16) & 65535
    value = value * 73244475
    value = value ^ jnp.right_shift(value, 16) & 65535
    value = value * 73244475
    value = value ^ jnp.right_shift(value, 16) & 65535
    return value


def sketch_table(base_value, feature_index, rank):
    counter = feature_index[:, None] * rank + jnp.arange(rank, dtype=jnp.int32)[None, :]
    offset = scramble(base_value)
    total = jnp.zeros(counter.shape, jnp.float32)
    for j in range(4):
        hashed = scramble(counter * 4 + j + offset)
        total = total + (hashed & 16777215).astype(jnp.float32) * (1.0 / 16777216.0)
    return ((total - 2.0) * 1.7320508).astype(jnp.bfloat16)


def terms_of(value):
    if value.dtype == jnp.bfloat16:
        return [value]
    high = value.astype(jnp.bfloat16)
    rest = value - high.astype(jnp.float32)
    middle = rest.astype(jnp.bfloat16)
    low = (rest - middle.astype(jnp.float32)).astype(jnp.bfloat16)
    return [high, middle, low]


def dot_nn(left, right):
    return lax.dot_general(
        left, right, (((1,), (0,)), ((), ())), preferred_element_type=jnp.float32
    )


def dot_nt(left, right):
    return lax.dot_general(
        left, right, (((1,), (1,)), ((), ())), preferred_element_type=jnp.float32
    )


def small_times_wide(small, wide):
    left, right = terms_of(small), terms_of(wide)
    pairs = [(i, d - i) for d in (2, 1, 0) for i in range(d + 1)]
    pairs = [(i, j) for i, j in pairs if i < len(left) and j < len(right)]
    return dot_nn(
        jnp.concatenate([left[i] for i, unused in pairs], axis=1),
        jnp.concatenate([right[j] for unused, j in pairs], axis=0),
    )


def gram_of(wide):
    terms = terms_of(wide)
    if len(terms) == 1:
        return dot_nt(terms[0], terms[0])
    rank = wide.shape[0]
    stacked = jnp.concatenate(terms, axis=0)
    both = dot_nt(stacked, stacked)
    cross = both[rank : 2 * rank, :rank] + both[2 * rank :, :rank]
    return both[:rank, :rank] + ((cross + cross.T) + both[rank : 2 * rank, rank : 2 * rank])


def eliminate(matrix, beside=()):
    beside = list(beside)
    size = matrix.shape[0]
    blocks = size // SUB
    row_index = lax.broadcasted_iota(jnp.int32, (SUB, 2 * size), 0)
    square_row = lax.broadcasted_iota(jnp.int32, (SUB, size), 0)
    square_col = lax.broadcasted_iota(jnp.int32, (SUB, size), 1)
    work = []
    for i in range(blocks):
        unit = jnp.where(square_col == square_row + SUB * i, 1.0, 0.0).astype(jnp.float32)
        work.append(jnp.concatenate([matrix[SUB * i : SUB * (i + 1), :], unit], axis=1))

    def fill(register, k):
        return jnp.broadcast_to(register[k : k + 1, :], (SUB, 2 * size))

    rows = []
    for b in range(blocks):
        for unused in range(-(-len(beside) // (blocks - b))):
            beside.pop(0)()
        columns = [
            {
                i: jnp.broadcast_to(work[i][:, SUB * b + j : SUB * b + j + 1], (SUB, 2 * size))
                for i in range(b, blocks)
            }
            for j in range(SUB)
        ]
        pivots = jnp.ones((SUB, 2 * size), jnp.float32)
        for k in range(0, SUB, 2):
            col_0, col_1 = columns[k], columns[k + 1]
            a, h, d = fill(col_0[b], k), fill(col_1[b], k), fill(col_1[b], k + 1)
            det = a * d - h * h
            over_det, over_a = 1.0 / det, 1.0 / a
            below_0 = jnp.where(row_index > k + 1, col_0[b], 0.0)
            below_1 = jnp.where(row_index > k + 1, col_1[b], 0.0)
            for j in range(k + 2, SUB):
                entry_0, entry_1 = fill(columns[j][b], k), fill(columns[j][b], k + 1)
                up_0 = d * entry_0 - h * entry_1
                up_1 = a * entry_1 - h * entry_0
                columns[j][b] = columns[j][b] - over_det * (below_0 * up_0 + below_1 * up_1)
                up_0, up_1 = over_det * up_0, over_det * up_1
                for i in range(b + 1, blocks):
                    columns[j][i] = columns[j][i] - (col_0[i] * up_0 + col_1[i] * up_1)
            row_0, row_1 = fill(work[b], k), fill(work[b], k + 1)
            up_0 = over_det * (d * row_0 - h * row_1)
            up_1 = over_det * (a * row_1 - h * row_0)
            for i in range(b + 1, blocks):
                work[i] = work[i] - (col_0[i] * up_0 + col_1[i] * up_1)
            second = jnp.where(row_index == k + 1, h * over_a, 0.0)
            work[b] = work[b] - (below_0 * up_0 + below_1 * up_1 + second * row_0)
            pivots = jnp.where(row_index == k, a, pivots)
            pivots = jnp.where(row_index == k + 1, det * over_a, pivots)
        rows.append(work[b] * lax.rsqrt(pivots))
    both = jnp.concatenate(rows, axis=0)
    keep = lax.broadcasted_iota(jnp.int32, (size, size), 1) >= lax.broadcasted_iota(
        jnp.int32, (size, size), 0
    )
    return jnp.where(keep, both[:, :size], 0.0), both[:, size:]


def shifted_factor(whole_gram):
    size = whole_gram.shape[0]
    diagonal = lax.broadcasted_iota(jnp.int32, (size, size), 0) == lax.broadcasted_iota(
        jnp.int32, (size, size), 1
    )
    on_diagonal = jnp.where(diagonal, whole_gram, 0.0)
    trace = jnp.sum(jnp.sum(on_diagonal, axis=1, keepdims=True), axis=0, keepdims=True)
    scaled = whole_gram * (1.0 / trace)
    upper, inverse = eliminate(jnp.where(diagonal, scaled + shift_ratio, scaled))
    root = jnp.sqrt(trace)
    return upper * root, inverse * (1.0 / root)


def wide_of(at_ref, z_refs):
    chunks = [z_ref[at_ref[i]] for z_ref in z_refs for i in range(at_ref.shape[0])]
    return jnp.concatenate(chunks, axis=1)


def first_pass(at_ref, z_refs):
    wide = wide_of(at_ref, z_refs)
    upper, inverse_one = shifted_factor(gram_of(wide))
    return small_times_wide(inverse_one, wide), upper


def back_product(at_ref, z_refs, a):
    first, unused = first_pass(at_ref, z_refs)
    rank = first.shape[0]
    terms = jnp.concatenate(terms_of(first), axis=0)
    tiles = []

    def tile(start):
        back = dot_nn(terms, a[:, start : start + TILE])
        tiles.append(back[:rank] + (back[rank : 2 * rank] + back[2 * rank :]))

    starts = range(0, a.shape[1], TILE)
    work = [functools.partial(tile, start) for start in starts]
    unused, inverse_two = eliminate(gram_of(first), work)
    return small_times_wide(inverse_two, jnp.concatenate(tiles, axis=1))


def forth_product(weights, a_ref, at_ref, part_ref):
    chunks, unused, width = part_ref.shape
    forth = dot_nt(weights.astype(jnp.bfloat16), a_ref[: chunks * width, :])
    for i in range(chunks):
        part_ref[at_ref[i]] = forth[:, width * i : width * (i + 1)]


def orth_kernel(at_ref, z_ref, other_ref, basis_ref, upper_ref):
    first, upper = first_pass(at_ref, (z_ref, other_ref))
    unused, inverse_two = eliminate(gram_of(first))
    basis_ref[...] = small_times_wide(inverse_two, first).astype(jnp.bfloat16)
    upper_ref[...] = upper


def power_kernel(at_ref, basis_ref, *refs):
    piece_refs, a_ref, part_ref = refs[:-2], refs[-2], refs[-1]
    start = 0
    for piece_ref in piece_refs:
        a_ref[start : start + piece_ref.shape[0], :] = piece_ref[...]
        start += piece_ref.shape[0]
    forth_product(dot_nn(basis_ref[...], a_ref[...]), a_ref, at_ref, part_ref)


def orth_power_kernel(at_ref, z_ref, other_ref, a_ref, part_ref):
    weights = back_product(at_ref, (z_ref, other_ref), a_ref[...])
    forth_product(weights, a_ref, at_ref, part_ref)


def last_kernel(at_ref, core_ref, z_ref, other_ref, a_ref, out_ref):
    cols = out_ref.shape[1]
    start = pl.multiple_of(core_ref[0] * cols, cols)
    out_ref[...] = back_product(at_ref, (z_ref, other_ref), a_ref[:, pl.ds(start, cols)])


def call(kernel, out_shapes, flops, scalars, *operands):
    moved = sum(x.size * x.dtype.itemsize for x in operands)
    return pl.pallas_call(
        kernel,
        out_shape=out_shapes,
        in_specs=[pl.BlockSpec(memory_space=pltpu.SMEM)] * len(scalars)
        + [pl.BlockSpec(memory_space=pltpu.VMEM)] * len(operands),
        out_specs=jax.tree.map(lambda _: pl.BlockSpec(memory_space=pltpu.VMEM), out_shapes),
        compiler_params=pltpu.CompilerParams(vmem_limit_bytes=20 * 1024 * 1024),
        cost_estimate=pl.CostEstimate(flops=flops, bytes_accessed=moved, transcendentals=0),
    )(*scalars, *operands)


def bits(size):
    return [1 << k for k in range(size.bit_length() - 1)]


def from_xor(value, axis, offset):
    size = math.prod(lax.axis_size(name) for name in axis)
    return lax.ppermute(value, axis, [(i, i ^ offset) for i in range(size)])


def square_devices():
    n_z, n_col = lax.axis_size("z"), lax.axis_size("col")
    sides = [(z, col) for z in range(2 if n_z > 2 else 1) for col in range(n_col)]
    return [(z * n_col + col, col * (2 if n_z > 2 else 1) + z) for z, col in sides[:0:-1]]


def sum_parts(total, dtype):
    offsets = square_devices()
    step = total.shape[0] // (len(offsets) + 1)
    others = [
        from_xor(total[step * place : step * (place + 1)].astype(dtype), ("z", "col"), offset)
        for offset, place in offsets
    ]
    total = functools.reduce(jnp.add, [x.astype(jnp.float32) for x in others], total[:step])
    for bit in far_bits():
        mine = total.astype(dtype)
        total = mine.astype(jnp.float32) + from_xor(mine, ("z",), bit).astype(jnp.float32)
    return total.astype(dtype)


def gather_parts(own):
    placed = {0: own}
    for offset, place in square_devices():
        placed[place] = from_xor(own, ("z", "col"), offset)
    own = jnp.concatenate([placed[place] for place in sorted(placed)])
    return own, from_xor(own, ("core",), 1)


def far_bits():
    return bits(lax.axis_size("z"))[1 if lax.axis_size("z") > 2 else 0 :]


def chunk_places(digits):
    n_z, n_col = lax.axis_size("z"), lax.axis_size("col")
    index = jnp.arange(n_z * n_col, dtype=jnp.int32)
    z_at, col_at = lax.axis_index("z"), lax.axis_index("col")
    column = index % n_col
    relative = {"z": index // n_col, "col": column ^ col_at}
    absolute = {"z": relative["z"] ^ z_at, "col": column}
    place = jnp.zeros_like(index)
    for axis, bit, is_relative in digits:
        place = place * 2 + ((relative if is_relative else absolute)[axis] // bit) % 2
    return place.astype(jnp.int32)


def per_device_transposed(sketch_base, states):
    n_z, n_core, n_col = lax.axis_size("z"), lax.axis_size("core"), lax.axis_size("col")
    n_row = n_z * n_core
    rows_local, width_local = states.shape
    rows_total, width_total = rows_local * n_row, width_local * n_col
    chunk = rows_local // n_col
    cols = width_local // n_z
    chunks = n_z * n_col
    z_at, col = lax.axis_index("z"), lax.axis_index("col")
    pieces = {}

    def move(slab, offset, part=0, parts=1):
        rows = rows_local // parts
        start = (part * rows, (z_at ^ offset) * cols)
        block = lax.dynamic_slice(slab, start, (rows, cols))
        pieces[offset, part] = from_xor(block, ("z",), offset) if offset else block

    def hold(value, names):
        value, moved = lax.optimization_barrier((value, [pieces[name] for name in names]))
        pieces.update(zip(names, moved))
        return value

    feature_index = col * width_local + jnp.arange(width_local, dtype=jnp.int32)
    omega = sketch_table(sketch_base[0], feature_index, RANK)
    z = lax.dot_general(
        omega, states, (((0,), (1,)), ((), ())), preferred_element_type=jnp.float32
    )
    z = z.reshape(RANK, n_col, chunk).transpose(1, 0, 2)
    z_bits = bits(n_z)[::-1]
    far = z_bits[0]
    for offset in [0, far, *range(1, far)]:
        move(states, offset)
    first = list(pieces)
    z = jnp.concatenate([z, from_xor(z, ("z",), far)])
    z, slab = lax.optimization_barrier((z, states))
    for offset in range(far + 1, n_z):
        move(slab, offset, 0, 2)
        move(slab, offset, 1, 2)
    for bit in bits(n_col):
        z = z + from_xor(z, ("col",), bit)
    z = hold(z, first)
    for bit in z_bits[1:]:
        z = jnp.concatenate([z, from_xor(z, ("z",), bit)])
    z = hold(z, [(offset, 0) for offset in range(far + 1, n_z)])
    z = z, from_xor(z, ("core",), 1)
    absolute_col = [("col", bit, False) for bit in bits(n_col)[::-1]]
    at_first = chunk_places([("z", bit, True) for bit in z_bits[::-1]] + absolute_col)
    digits = [("col", bit, True) for bit in bits(n_col)[::-1]]
    digits += [("z", 1, True)] if n_z > 2 else []
    at = chunk_places(digits + [("z", bit, False) for bit in far_bits()])
    late = [name for name in pieces if name[0] > far]
    others = {name: from_xor(pieces[name], ("core",), 1) for name in first}

    f32 = jnp.float32
    square = jax.ShapeDtypeStruct((RANK, RANK), f32)
    wide = jax.ShapeDtypeStruct((RANK, rows_total), jnp.bfloat16)
    slab = jax.ShapeDtypeStruct((rows_total, cols), states.dtype)
    parts = jax.ShapeDtypeStruct((chunks, RANK, chunk), f32)
    loadings = jax.ShapeDtypeStruct((RANK, cols // n_core), f32)
    orth_flops = 8 * 64 * 64 * rows_total * 6
    flops = orth_flops + 4 * 64 * rows_total * cols

    basis, upper = call(orth_kernel, (wide, square), orth_flops, (at_first,), *z)
    basis = hold(basis, late)
    others.update((name, from_xor(pieces[name], ("core",), 1)) for name in late)
    blocks = [half[name] for half in (pieces, others) for name in sorted(half)]
    factor = upper.T * (1.0 / math.sqrt(rows_total * width_total))
    a, total = call(power_kernel, (slab, parts), flops, (at,), basis, *blocks)
    z = gather_parts(sum_parts(total, f32))
    for step in range(POWER - 1):
        total = call(orth_power_kernel, parts, flops, (at,), *z, a)
        z = gather_parts(sum_parts(total, jnp.bfloat16))
    core = lax.axis_index("core")[None].astype(jnp.int32)
    return call(last_kernel, loadings, flops, (at, core), *z, a).T, factor


def local_gram(basis):
    return jnp.dot(basis.T, basis, precision=lax.Precision.HIGHEST)


def orthonormal_block(sketch):
    whole_gram = lax.psum(local_gram(sketch), "row")
    identity = jnp.eye(RANK, dtype=jnp.float32)
    lower = jnp.linalg.cholesky(whole_gram + shift_ratio * jnp.trace(whole_gram) * identity)
    first = jax.scipy.linalg.solve_triangular(lower, sketch.T, lower=True).T
    lower_two = jnp.linalg.cholesky(lax.psum(local_gram(first), "row"))
    return jax.scipy.linalg.solve_triangular(lower_two, first.T, lower=True).T, lower


def per_device_slabs(sketch_base, states):
    width_local = states.shape[1]
    rows_total = states.shape[0] * lax.axis_size("row")
    width_total = width_local * lax.axis_size("col")
    feature_index = lax.axis_index("col") * width_local + jnp.arange(width_local, dtype=jnp.int32)
    omega = sketch_table(sketch_base[0], feature_index, RANK)

    def row_basis(right):
        partial_sketch = jnp.dot(states, right, preferred_element_type=jnp.float32)
        basis_new, lower = orthonormal_block(lax.psum(partial_sketch, "col"))
        return basis_new.astype(jnp.bfloat16), lower

    def back(basis):
        return lax.dot_general(
            states, basis, (((0,), (0,)), ((), ())), preferred_element_type=jnp.float32
        )

    basis, first_lower = row_basis(omega)
    factor = first_lower * (1.0 / math.sqrt(rows_total * width_total))
    for step in range(POWER):
        basis, unused = row_basis(lax.psum(back(basis), "row").astype(jnp.bfloat16))
    return lax.psum_scatter(back(basis), "row", scatter_dimension=0, tiled=True), factor


def solution(mesh):
    n_grp, n_row, n_col = (mesh.shape[name] for name in ("grp", "row", "col"))
    fits = n_row >= 4 and n_row & (n_row - 1) == 0 and n_col & (n_col - 1) == 0

    def run(sketch_base, states):
        rows_local = states.shape[0] // (n_grp * n_row)
        width_local = states.shape[1] // n_col
        tiled = rows_local % (n_col * LANES) == 0 and width_local % (n_row * LANES) == 0
        if fits and tiled:
            split = mesh.devices.reshape(n_grp, n_row // 2, 2, n_col)
            inner = jax.sharding.Mesh(split, ("grp", "z", "core", "col"))
            row, step = ("z", "core"), per_device_transposed
        else:
            inner, row, step = mesh, ("row",), per_device_slabs
        return jax.shard_map(
            step,
            mesh=inner,
            in_specs=(P("grp"), P(("grp",) + row, "col")),
            out_specs=(P(("col",) + row, "grp"), P("grp", None)),
            check_vma=False,
        )(sketch_base, states)

    return run
```

```python
import functools
import math

import jax
import jax.numpy as jnp
from jax import lax
from jax.experimental import pallas as pl
from jax.experimental.pallas import tpu as pltpu
from jax.sharding import PartitionSpec as P

RANK = 64
POWER = 4
LANES = 128
SUB = 8
TILE = 256


shift_ratio = 0.005


def scramble(value):
    value = value ^ jnp.right_shift(value, 16) & 65535
    value = value * 73244475
    value = value ^ jnp.right_shift(value, 16) & 65535
    value = value * 73244475
    value = value ^ jnp.right_shift(value, 16) & 65535
    return value


def sketch_table(base_value, feature_index, rank):
    counter = feature_index[:, None] * rank + jnp.arange(rank, dtype=jnp.int32)[None, :]
    offset = scramble(base_value)
    total = jnp.zeros(counter.shape, jnp.float32)
    for j in range(4):
        hashed = scramble(counter * 4 + j + offset)
        total = total + (hashed & 16777215).astype(jnp.float32) * (1.0 / 16777216.0)
    return ((total - 2.0) * 1.7320508).astype(jnp.bfloat16)


def terms_of(value):
    if value.dtype == jnp.bfloat16:
        return [value]
    high = value.astype(jnp.bfloat16)
    rest = value - high.astype(jnp.float32)
    middle = rest.astype(jnp.bfloat16)
    low = (rest - middle.astype(jnp.float32)).astype(jnp.bfloat16)
    return [high, middle, low]


def dot_nn(left, right):
    return lax.dot_general(
        left, right, (((1,), (0,)), ((), ())), preferred_element_type=jnp.float32
    )


def dot_nt(left, right):
    return lax.dot_general(
        left, right, (((1,), (1,)), ((), ())), preferred_element_type=jnp.float32
    )


def small_times_wide(small, wide):
    left, right = terms_of(small), terms_of(wide)
    pairs = [(i, d - i) for d in (2, 1, 0) for i in range(d + 1)]
    pairs = [(i, j) for i, j in pairs if i < len(left) and j < len(right)]
    return dot_nn(
        jnp.concatenate([left[i] for i, unused in pairs], axis=1),
        jnp.concatenate([right[j] for unused, j in pairs], axis=0),
    )


def gram_of(wide):
    terms = terms_of(wide)
    if len(terms) == 1:
        return dot_nt(terms[0], terms[0])
    rank = wide.shape[0]
    stacked = jnp.concatenate(terms, axis=0)
    both = dot_nt(stacked, stacked)
    cross = both[rank : 2 * rank, :rank] + both[2 * rank :, :rank]
    return both[:rank, :rank] + ((cross + cross.T) + both[rank : 2 * rank, rank : 2 * rank])


def eliminate(matrix, beside=()):
    beside = list(beside)
    size = matrix.shape[0]
    blocks = size // SUB
    row_index = lax.broadcasted_iota(jnp.int32, (SUB, 2 * size), 0)
    square_row = lax.broadcasted_iota(jnp.int32, (SUB, size), 0)
    square_col = lax.broadcasted_iota(jnp.int32, (SUB, size), 1)
    work = []
    for i in range(blocks):
        unit = jnp.where(square_col == square_row + SUB * i, 1.0, 0.0).astype(jnp.float32)
        work.append(jnp.concatenate([matrix[SUB * i : SUB * (i + 1), :], unit], axis=1))

    def fill(register, k):
        return jnp.broadcast_to(register[k : k + 1, :], (SUB, 2 * size))

    rows = []
    for b in range(blocks):
        for unused in range(-(-len(beside) // (blocks - b))):
            beside.pop(0)()
        columns = [
            {
                i: jnp.broadcast_to(work[i][:, SUB * b + j : SUB * b + j + 1], (SUB, 2 * size))
                for i in range(b, blocks)
            }
            for j in range(SUB)
        ]
        pivots = jnp.ones((SUB, 2 * size), jnp.float32)
        for k in range(0, SUB, 2):
            col_0, col_1 = columns[k], columns[k + 1]
            a, h, d = fill(col_0[b], k), fill(col_1[b], k), fill(col_1[b], k + 1)
            det = a * d - h * h
            over_det, over_a = 1.0 / det, 1.0 / a
            below_0 = jnp.where(row_index > k + 1, col_0[b], 0.0)
            below_1 = jnp.where(row_index > k + 1, col_1[b], 0.0)
            for j in range(k + 2, SUB):
                entry_0, entry_1 = fill(columns[j][b], k), fill(columns[j][b], k + 1)
                up_0 = d * entry_0 - h * entry_1
                up_1 = a * entry_1 - h * entry_0
                columns[j][b] = columns[j][b] - over_det * (below_0 * up_0 + below_1 * up_1)
                up_0, up_1 = over_det * up_0, over_det * up_1
                for i in range(b + 1, blocks):
                    columns[j][i] = columns[j][i] - (col_0[i] * up_0 + col_1[i] * up_1)
            row_0, row_1 = fill(work[b], k), fill(work[b], k + 1)
            up_0 = over_det * (d * row_0 - h * row_1)
            up_1 = over_det * (a * row_1 - h * row_0)
            for i in range(b + 1, blocks):
                work[i] = work[i] - (col_0[i] * up_0 + col_1[i] * up_1)
            second = jnp.where(row_index == k + 1, h * over_a, 0.0)
            work[b] = work[b] - (below_0 * up_0 + below_1 * up_1 + second * row_0)
            pivots = jnp.where(row_index == k, a, pivots)
            pivots = jnp.where(row_index == k + 1, det * over_a, pivots)
        rows.append(work[b] * lax.rsqrt(pivots))
    both = jnp.concatenate(rows, axis=0)
    keep = lax.broadcasted_iota(jnp.int32, (size, size), 1) >= lax.broadcasted_iota(
        jnp.int32, (size, size), 0
    )
    return jnp.where(keep, both[:, :size], 0.0), both[:, size:]


def shifted_factor(whole_gram):
    size = whole_gram.shape[0]
    diagonal = lax.broadcasted_iota(jnp.int32, (size, size), 0) == lax.broadcasted_iota(
        jnp.int32, (size, size), 1
    )
    on_diagonal = jnp.where(diagonal, whole_gram, 0.0)
    trace = jnp.sum(jnp.sum(on_diagonal, axis=1, keepdims=True), axis=0, keepdims=True)
    scaled = whole_gram * (1.0 / trace)
    upper, inverse = eliminate(jnp.where(diagonal, scaled + shift_ratio, scaled))
    root = jnp.sqrt(trace)
    return upper * root, inverse * (1.0 / root)


def wide_of(at_ref, z_refs):
    chunks = [z_ref[at_ref[i]] for z_ref in z_refs for i in range(at_ref.shape[0])]
    return jnp.concatenate(chunks, axis=1)


def first_pass(at_ref, z_refs):
    wide = wide_of(at_ref, z_refs)
    upper, inverse_one = shifted_factor(gram_of(wide))
    return small_times_wide(inverse_one, wide), upper


def back_product(at_ref, z_refs, a):
    first, unused = first_pass(at_ref, z_refs)
    rank = first.shape[0]
    terms = jnp.concatenate(terms_of(first), axis=0)
    tiles = []

    def tile(start):
        back = dot_nn(terms, a[:, start : start + TILE])
        tiles.append(back[:rank] + (back[rank : 2 * rank] + back[2 * rank :]))

    starts = range(0, a.shape[1], TILE)
    work = [functools.partial(tile, start) for start in starts]
    unused, inverse_two = eliminate(gram_of(first), work)
    return small_times_wide(inverse_two, jnp.concatenate(tiles, axis=1))


def forth_product(weights, a_ref, at_ref, part_ref):
    chunks, unused, width = part_ref.shape
    forth = dot_nt(weights.astype(jnp.bfloat16), a_ref[...])
    for i in range(chunks):
        part_ref[at_ref[i]] = forth[:, width * i : width * (i + 1)]


def orth_kernel(at_ref, z_ref, other_ref, basis_ref, upper_ref):
    first, upper = first_pass(at_ref, (z_ref, other_ref))
    unused, inverse_two = eliminate(gram_of(first))
    basis_ref[...] = small_times_wide(inverse_two, first).astype(jnp.bfloat16)
    upper_ref[...] = upper


def power_kernel(at_ref, basis_ref, *refs):
    piece_refs, a_ref, part_ref = refs[:-2], refs[-2], refs[-1]
    start = 0
    for piece_ref in piece_refs:
        a_ref[start : start + piece_ref.shape[0], :] = piece_ref[...]
        start += piece_ref.shape[0]
    forth_product(dot_nn(basis_ref[...], a_ref[...]), a_ref, at_ref, part_ref)


def orth_power_kernel(at_ref, z_ref, a_ref, part_ref):
    weights = back_product(at_ref, (z_ref,), a_ref[...])
    forth_product(weights, a_ref, at_ref, part_ref)


def last_kernel(at_ref, core_ref, z_ref, a_ref, out_ref):
    cols = out_ref.shape[1]
    start = pl.multiple_of(core_ref[0] * cols, cols)
    out_ref[...] = back_product(at_ref, (z_ref,), a_ref[:, pl.ds(start, cols)])


def call(kernel, out_shapes, flops, scalars, *operands):
    moved = sum(x.size * x.dtype.itemsize for x in operands)
    return pl.pallas_call(
        kernel,
        out_shape=out_shapes,
        in_specs=[pl.BlockSpec(memory_space=pltpu.SMEM)] * len(scalars)
        + [pl.BlockSpec(memory_space=pltpu.VMEM)] * len(operands),
        out_specs=jax.tree.map(lambda _: pl.BlockSpec(memory_space=pltpu.VMEM), out_shapes),
        compiler_params=pltpu.CompilerParams(vmem_limit_bytes=20 * 1024 * 1024),
        cost_estimate=pl.CostEstimate(flops=flops, bytes_accessed=moved, transcendentals=0),
    )(*scalars, *operands)


def bits(size):
    return [1 << k for k in range(size.bit_length() - 1)]


def from_xor(value, axis, offset):
    size = math.prod(lax.axis_size(name) for name in axis)
    return lax.ppermute(value, axis, [(i, i ^ offset) for i in range(size)])


def from_chip(value, z_offset, col_offset):
    n_z, n_core, n_col = lax.axis_size("z"), lax.axis_size("core"), lax.axis_size("col")

    def device(z, col):
        return (z * n_core + 1) * n_col + col

    pairs = [
        (device(z, col), device(z ^ z_offset, col ^ col_offset))
        for z in range(n_z)
        for col in range(n_col)
    ]
    return lax.ppermute(value, ("z", "core", "col"), pairs)


def square_chips():
    near = 2 if lax.axis_size("z") > 2 else 1
    sides = [(z, col) for z in range(near) for col in range(lax.axis_size("col"))]
    return [((z, col), col * near + z) for z, col in sides[:0:-1]]


def sum_parts(total, dtype):
    chips = square_chips()
    step = total.shape[0] // (len(chips) + 1)
    others = [
        from_chip(total[step * place : step * (place + 1)].astype(dtype), *offsets)
        for offsets, place in chips
    ]
    total = functools.reduce(jnp.add, [x.astype(jnp.float32) for x in others], total[:step])
    for bit in far_bits():
        mine = total.astype(dtype)
        total = mine.astype(jnp.float32) + from_chip(mine, bit, 0).astype(jnp.float32)
    return total.astype(dtype)


def gather_parts(own):
    placed = {0: own}
    for offsets, place in square_chips():
        placed[place] = from_chip(own, *offsets)
    return jnp.concatenate([placed[place] for place in sorted(placed)])


def far_bits():
    return bits(lax.axis_size("z"))[1 if lax.axis_size("z") > 2 else 0 :]


def chunk_places(digits, halves):
    n_z, n_col = lax.axis_size("z"), lax.axis_size("col")
    index = jnp.arange(halves * n_z * n_col, dtype=jnp.int32)
    relative = {"core": index // (n_col * n_z), "z": index // n_col % n_z, "col": index % n_col}
    absolute = {name: value ^ lax.axis_index(name) for name, value in relative.items()}
    relative["col"], absolute["col"] = absolute["col"], relative["col"]
    place = jnp.zeros_like(index)
    for axis, bit, is_relative in digits:
        place = place * 2 + ((relative if is_relative else absolute)[axis] // bit) % 2
    return place.astype(jnp.int32)


def per_device_transposed(sketch_base, states):
    n_z, n_core, n_col = lax.axis_size("z"), lax.axis_size("core"), lax.axis_size("col")
    n_row = n_z * n_core
    rows_local, width_local = states.shape
    rows_total, width_total = rows_local * n_row, width_local * n_col
    chunk = rows_local // n_col
    cols = width_local // n_z
    chunks = n_row * n_col
    z_at, col = lax.axis_index("z"), lax.axis_index("col")
    pieces = {}

    def move(slab, offset, part=0, parts=1):
        rows = rows_local // parts
        start = (part * rows, (z_at ^ offset) * cols)
        block = lax.dynamic_slice(slab, start, (rows, cols))
        pieces[offset, part] = from_xor(block, ("z",), offset) if offset else block

    def hold(value, names):
        value, moved = lax.optimization_barrier((value, [pieces[name] for name in names]))
        pieces.update(zip(names, moved))
        return value

    feature_index = col * width_local + jnp.arange(width_local, dtype=jnp.int32)
    omega = sketch_table(sketch_base[0], feature_index, RANK)
    z = lax.dot_general(
        omega, states, (((0,), (1,)), ((), ())), preferred_element_type=jnp.float32
    )
    z = z.reshape(RANK, n_col, chunk).transpose(1, 0, 2)
    z_bits = bits(n_z)[::-1]
    far = z_bits[0]
    for offset in [0, far, *range(1, far)]:
        move(states, offset)
    first = list(pieces)
    z = jnp.concatenate([z, from_xor(z, ("z",), far)])
    z, slab = lax.optimization_barrier((z, states))
    for offset in range(far + 1, n_z):
        move(slab, offset, 0, 2)
        move(slab, offset, 1, 2)
    for bit in bits(n_col):
        z = z + from_xor(z, ("col",), bit)
    z = hold(z, first)
    for bit in z_bits[1:]:
        z = jnp.concatenate([z, from_xor(z, ("z",), bit)])
    z = hold(z, [(offset, 0) for offset in range(far + 1, n_z)])
    z = z, from_xor(z, ("core",), 1)
    absolute_col = [("col", bit, False) for bit in bits(n_col)[::-1]]
    at_first = chunk_places([("z", bit, True) for bit in z_bits[::-1]] + absolute_col, 1)
    digits = [("col", bit, True) for bit in bits(n_col)[::-1]]
    digits += [("z", 1, True)] if n_z > 2 else []
    digits += [("core", 1, False)] + [("z", bit, False) for bit in far_bits()]
    at = chunk_places(digits, 2)
    late = [name for name in pieces if name[0] > far]
    others = {name: from_xor(pieces[name], ("core",), 1) for name in first}

    f32 = jnp.float32
    square = jax.ShapeDtypeStruct((RANK, RANK), f32)
    wide = jax.ShapeDtypeStruct((RANK, rows_total), jnp.bfloat16)
    slab = jax.ShapeDtypeStruct((rows_total, cols), states.dtype)
    parts = jax.ShapeDtypeStruct((chunks, RANK, chunk), f32)
    loadings = jax.ShapeDtypeStruct((RANK, cols // n_core), f32)
    orth_flops = 8 * 64 * 64 * rows_total * 6
    flops = orth_flops + 4 * 64 * rows_total * cols

    basis, upper = call(orth_kernel, (wide, square), orth_flops, (at_first,), *z)
    basis = hold(basis, late)
    others.update((name, from_xor(pieces[name], ("core",), 1)) for name in late)
    blocks = [half[name] for half in (pieces, others) for name in sorted(half)]
    factor = upper.T * (1.0 / math.sqrt(rows_total * width_total))
    a, total = call(power_kernel, (slab, parts), flops, (at,), basis, *blocks)
    z = gather_parts(sum_parts(total, f32))
    for step in range(POWER - 1):
        total = call(orth_power_kernel, parts, flops, (at,), z, a)
        z = gather_parts(sum_parts(total, jnp.bfloat16))
    core = lax.axis_index("core")
    z = jnp.where(core == 1, z, lax.ppermute(z, "core", [(1, 0)]))
    at_core = core[None].astype(jnp.int32)
    return call(last_kernel, loadings, flops, (at, at_core), z, a).T, factor


def local_gram(basis):
    return jnp.dot(basis.T, basis, precision=lax.Precision.HIGHEST)


def orthonormal_block(sketch):
    whole_gram = lax.psum(local_gram(sketch), "row")
    identity = jnp.eye(RANK, dtype=jnp.float32)
    lower = jnp.linalg.cholesky(whole_gram + shift_ratio * jnp.trace(whole_gram) * identity)
    first = jax.scipy.linalg.solve_triangular(lower, sketch.T, lower=True).T
    lower_two = jnp.linalg.cholesky(lax.psum(local_gram(first), "row"))
    return jax.scipy.linalg.solve_triangular(lower_two, first.T, lower=True).T, lower


def per_device_slabs(sketch_base, states):
    width_local = states.shape[1]
    rows_total = states.shape[0] * lax.axis_size("row")
    width_total = width_local * lax.axis_size("col")
    feature_index = lax.axis_index("col") * width_local + jnp.arange(width_local, dtype=jnp.int32)
    omega = sketch_table(sketch_base[0], feature_index, RANK)

    def row_basis(right):
        partial_sketch = jnp.dot(states, right, preferred_element_type=jnp.float32)
        basis_new, lower = orthonormal_block(lax.psum(partial_sketch, "col"))
        return basis_new.astype(jnp.bfloat16), lower

    def back(basis):
        return lax.dot_general(
            states, basis, (((0,), (0,)), ((), ())), preferred_element_type=jnp.float32
        )

    basis, first_lower = row_basis(omega)
    factor = first_lower * (1.0 / math.sqrt(rows_total * width_total))
    for step in range(POWER):
        basis, unused = row_basis(lax.psum(back(basis), "row").astype(jnp.bfloat16))
    return lax.psum_scatter(back(basis), "row", scatter_dimension=0, tiled=True), factor


def solution(mesh):
    n_grp, n_row, n_col = (mesh.shape[name] for name in ("grp", "row", "col"))
    fits = n_row >= 4 and n_row & (n_row - 1) == 0 and n_col & (n_col - 1) == 0

    def run(sketch_base, states):
        rows_local = states.shape[0] // (n_grp * n_row)
        width_local = states.shape[1] // n_col
        tiled = rows_local % (n_col * LANES) == 0 and width_local % (n_row * LANES) == 0
        if fits and tiled:
            split = mesh.devices.reshape(n_grp, n_row // 2, 2, n_col)
            inner = jax.sharding.Mesh(split, ("grp", "z", "core", "col"))
            row, step = ("z", "core"), per_device_transposed
        else:
            inner, row, step = mesh, ("row",), per_device_slabs
        return jax.shard_map(
            step,
            mesh=inner,
            in_specs=(P("grp"), P(("grp",) + row, "col")),
            out_specs=(P(("col",) + row, "grp"), P("grp", None)),
            check_vma=False,
        )(sketch_base, states)

    return run
```

```python
import functools
import math

import jax
import jax.numpy as jnp
from jax import lax
from jax.experimental import pallas as pl
from jax.experimental.pallas import tpu as pltpu
from jax.sharding import PartitionSpec as P

RANK = 64
POWER = 4
LANES = 128
SUB = 8
TILE = 256


shift_ratio = 0.005


def scramble(value):
    value = value ^ jnp.right_shift(value, 16) & 65535
    value = value * 73244475
    value = value ^ jnp.right_shift(value, 16) & 65535
    value = value * 73244475
    value = value ^ jnp.right_shift(value, 16) & 65535
    return value


def sketch_table(base_value, feature_index, rank):
    counter = feature_index[:, None] * rank + jnp.arange(rank, dtype=jnp.int32)[None, :]
    offset = scramble(base_value)
    total = jnp.zeros(counter.shape, jnp.float32)
    for j in range(4):
        hashed = scramble(counter * 4 + j + offset)
        total = total + (hashed & 16777215).astype(jnp.float32) * (1.0 / 16777216.0)
    return ((total - 2.0) * 1.7320508).astype(jnp.bfloat16)


def terms_of(value):
    if value.dtype == jnp.bfloat16:
        return [value]
    high = value.astype(jnp.bfloat16)
    rest = value - high.astype(jnp.float32)
    middle = rest.astype(jnp.bfloat16)
    low = (rest - middle.astype(jnp.float32)).astype(jnp.bfloat16)
    return [high, middle, low]


def dot_nn(left, right):
    return lax.dot_general(
        left, right, (((1,), (0,)), ((), ())), preferred_element_type=jnp.float32
    )


def dot_nt(left, right):
    return lax.dot_general(
        left, right, (((1,), (1,)), ((), ())), preferred_element_type=jnp.float32
    )


def small_times_wide(small, wide):
    left, right = terms_of(small), terms_of(wide)
    pairs = [(i, d - i) for d in (2, 1, 0) for i in range(d + 1)]
    pairs = [(i, j) for i, j in pairs if i < len(left) and j < len(right)]
    return dot_nn(
        jnp.concatenate([left[i] for i, unused in pairs], axis=1),
        jnp.concatenate([right[j] for unused, j in pairs], axis=0),
    )


def gram_of(wide):
    terms = terms_of(wide)
    if len(terms) == 1:
        return dot_nt(terms[0], terms[0])
    rank = wide.shape[0]
    stacked = jnp.concatenate(terms, axis=0)
    both = dot_nt(stacked, stacked)
    cross = both[rank : 2 * rank, :rank] + both[2 * rank :, :rank]
    return both[:rank, :rank] + ((cross + cross.T) + both[rank : 2 * rank, rank : 2 * rank])


def eliminate(matrix, beside=()):
    beside = list(beside)
    size = matrix.shape[0]
    blocks = size // SUB
    row_index = lax.broadcasted_iota(jnp.int32, (SUB, 2 * size), 0)
    square_row = lax.broadcasted_iota(jnp.int32, (SUB, size), 0)
    square_col = lax.broadcasted_iota(jnp.int32, (SUB, size), 1)
    work = []
    for i in range(blocks):
        unit = jnp.where(square_col == square_row + SUB * i, 1.0, 0.0).astype(jnp.float32)
        work.append(jnp.concatenate([matrix[SUB * i : SUB * (i + 1), :], unit], axis=1))

    def fill(register, k):
        return jnp.broadcast_to(register[k : k + 1, :], (SUB, 2 * size))

    rows = []
    for b in range(blocks):
        for unused in range(-(-len(beside) // (blocks - b))):
            beside.pop(0)()
        columns = [
            {
                i: jnp.broadcast_to(work[i][:, SUB * b + j : SUB * b + j + 1], (SUB, 2 * size))
                for i in range(b, blocks)
            }
            for j in range(SUB)
        ]
        pivots = jnp.ones((SUB, 2 * size), jnp.float32)
        for k in range(0, SUB, 2):
            col_0, col_1 = columns[k], columns[k + 1]
            a, h, d = fill(col_0[b], k), fill(col_1[b], k), fill(col_1[b], k + 1)
            det = a * d - h * h
            over_det, over_a = 1.0 / det, 1.0 / a
            below_0 = jnp.where(row_index > k + 1, col_0[b], 0.0)
            below_1 = jnp.where(row_index > k + 1, col_1[b], 0.0)
            for j in range(k + 2, SUB):
                entry_0, entry_1 = fill(columns[j][b], k), fill(columns[j][b], k + 1)
                up_0 = d * entry_0 - h * entry_1
                up_1 = a * entry_1 - h * entry_0
                columns[j][b] = columns[j][b] - over_det * (below_0 * up_0 + below_1 * up_1)
                up_0, up_1 = over_det * up_0, over_det * up_1
                for i in range(b + 1, blocks):
                    columns[j][i] = columns[j][i] - (col_0[i] * up_0 + col_1[i] * up_1)
            row_0, row_1 = fill(work[b], k), fill(work[b], k + 1)
            up_0 = over_det * (d * row_0 - h * row_1)
            up_1 = over_det * (a * row_1 - h * row_0)
            for i in range(b + 1, blocks):
                work[i] = work[i] - (col_0[i] * up_0 + col_1[i] * up_1)
            second = jnp.where(row_index == k + 1, h * over_a, 0.0)
            work[b] = work[b] - (below_0 * up_0 + below_1 * up_1 + second * row_0)
            pivots = jnp.where(row_index == k, a, pivots)
            pivots = jnp.where(row_index == k + 1, det * over_a, pivots)
        rows.append(work[b] * lax.rsqrt(pivots))
    both = jnp.concatenate(rows, axis=0)
    keep = lax.broadcasted_iota(jnp.int32, (size, size), 1) >= lax.broadcasted_iota(
        jnp.int32, (size, size), 0
    )
    return jnp.where(keep, both[:, :size], 0.0), both[:, size:]


def shifted_factor(whole_gram):
    size = whole_gram.shape[0]
    diagonal = lax.broadcasted_iota(jnp.int32, (size, size), 0) == lax.broadcasted_iota(
        jnp.int32, (size, size), 1
    )
    on_diagonal = jnp.where(diagonal, whole_gram, 0.0)
    trace = jnp.sum(jnp.sum(on_diagonal, axis=1, keepdims=True), axis=0, keepdims=True)
    scaled = whole_gram * (1.0 / trace)
    upper, inverse = eliminate(jnp.where(diagonal, scaled + shift_ratio, scaled))
    root = jnp.sqrt(trace)
    return upper * root, inverse * (1.0 / root)


def wide_of(at_ref, z_refs):
    half = at_ref.shape[0] // len(z_refs)
    chunks = [z_ref[at_ref[half * s + i]] for s, z_ref in enumerate(z_refs) for i in range(half)]
    return jnp.concatenate(chunks, axis=1)


def first_pass(at_ref, z_refs):
    wide = wide_of(at_ref, z_refs)
    upper, inverse_one = shifted_factor(gram_of(wide))
    return small_times_wide(inverse_one, wide), upper


def back_product(at_ref, z_refs, a):
    first, unused = first_pass(at_ref, z_refs)
    rank = first.shape[0]
    terms = jnp.concatenate(terms_of(first), axis=0)
    tiles = []

    def tile(start):
        back = dot_nn(terms, a[:, start : start + TILE])
        tiles.append(back[:rank] + (back[rank : 2 * rank] + back[2 * rank :]))

    starts = range(0, a.shape[1], TILE)
    work = [functools.partial(tile, start) for start in starts]
    unused, inverse_two = eliminate(gram_of(first), work)
    return small_times_wide(inverse_two, jnp.concatenate(tiles, axis=1))


def forth_product(weights, a_ref, at_ref, part_ref):
    chunks, unused, width = part_ref.shape
    forth = dot_nt(weights.astype(jnp.bfloat16), a_ref[: chunks * width, :])
    for i in range(chunks):
        part_ref[at_ref[i]] = forth[:, width * i : width * (i + 1)]


def orth_kernel(at_ref, z_ref, other_ref, basis_ref, upper_ref):
    first, upper = first_pass(at_ref, (z_ref, other_ref))
    unused, inverse_two = eliminate(gram_of(first))
    basis_ref[...] = small_times_wide(inverse_two, first).astype(jnp.bfloat16)
    upper_ref[...] = upper


def power_kernel(at_ref, basis_ref, *refs):
    piece_refs, a_ref, part_ref = refs[:-2], refs[-2], refs[-1]
    start = 0
    for piece_ref in piece_refs:
        a_ref[start : start + piece_ref.shape[0], :] = piece_ref[...]
        start += piece_ref.shape[0]
    forth_product(dot_nn(basis_ref[...], a_ref[...]), a_ref, at_ref, part_ref)


def orth_power_kernel(at_ref, z_ref, other_ref, a_ref, part_ref):
    weights = back_product(at_ref, (z_ref, other_ref), a_ref[...])
    forth_product(weights, a_ref, at_ref, part_ref)


def last_kernel(at_ref, core_ref, z_ref, other_ref, a_ref, out_ref):
    cols = out_ref.shape[1]
    start = pl.multiple_of(core_ref[0] * cols, cols)
    out_ref[...] = back_product(at_ref, (z_ref, other_ref), a_ref[:, pl.ds(start, cols)])


def call(kernel, out_shapes, flops, scalars, *operands):
    moved = sum(x.size * x.dtype.itemsize for x in operands)
    return pl.pallas_call(
        kernel,
        out_shape=out_shapes,
        in_specs=[pl.BlockSpec(memory_space=pltpu.SMEM)] * len(scalars)
        + [pl.BlockSpec(memory_space=pltpu.VMEM)] * len(operands),
        out_specs=jax.tree.map(lambda _: pl.BlockSpec(memory_space=pltpu.VMEM), out_shapes),
        compiler_params=pltpu.CompilerParams(vmem_limit_bytes=20 * 1024 * 1024),
        cost_estimate=pl.CostEstimate(flops=flops, bytes_accessed=moved, transcendentals=0),
    )(*scalars, *operands)


def bits(size):
    return [1 << k for k in range(size.bit_length() - 1)]


def from_xor(value, axis, offset):
    size = math.prod(lax.axis_size(name) for name in axis)
    return lax.ppermute(value, axis, [(i, i ^ offset) for i in range(size)])


def square_devices():
    near = 2 if lax.axis_size("z") > 2 else 1
    by_z = [(z, col) for z in range(near) for col in range(lax.axis_size("col"))]
    by_col = [(z, col) for col in range(lax.axis_size("col")) for z in range(near)]
    return by_z, by_col if near == lax.axis_size("col") else by_z


def from_square(value, place):
    n_z, n_core, n_col = lax.axis_size("z"), lax.axis_size("core"), lax.axis_size("col")
    pairs = []
    for core, offsets in enumerate(square_devices()):
        z_offset, col_offset = offsets[place]
        for z in range(n_z):
            for col in range(n_col):
                target = ((z ^ z_offset) * n_core + core) * n_col + (col ^ col_offset)
                pairs.append(((z * n_core + core) * n_col + col, target))
    return lax.ppermute(value, ("z", "core", "col"), pairs)


def sum_parts(total, dtype):
    places = len(square_devices()[0])
    step = total.shape[0] // places
    others = [
        from_square(total[step * place : step * (place + 1)].astype(dtype), place)
        for place in range(1, places)
    ]
    total = functools.reduce(jnp.add, [x.astype(jnp.float32) for x in others], total[:step])
    for bit in far_bits():
        mine = total.astype(dtype)
        total = mine.astype(jnp.float32) + from_xor(mine, ("z",), bit).astype(jnp.float32)
    return total.astype(dtype)


def gather_parts(own):
    others = [from_square(own, place) for place in range(1, len(square_devices()[0]))]
    own = jnp.concatenate([own] + others)
    return own, from_xor(own, ("core",), 1)


def far_bits():
    return bits(lax.axis_size("z"))[1 if lax.axis_size("z") > 2 else 0 :]


def chunk_places(digits):
    n_z, n_col = lax.axis_size("z"), lax.axis_size("col")
    index = jnp.arange(n_z * n_col, dtype=jnp.int32)
    z_at, col_at = lax.axis_index("z"), lax.axis_index("col")
    column = index % n_col
    relative = {"z": index // n_col, "col": column ^ col_at}
    absolute = {"z": relative["z"] ^ z_at, "col": column}
    place = jnp.zeros_like(index)
    for axis, bit, is_relative in digits:
        place = place * 2 + ((relative if is_relative else absolute)[axis] // bit) % 2
    return place.astype(jnp.int32)


def per_device_transposed(sketch_base, states):
    n_z, n_core, n_col = lax.axis_size("z"), lax.axis_size("core"), lax.axis_size("col")
    n_row = n_z * n_core
    rows_local, width_local = states.shape
    rows_total, width_total = rows_local * n_row, width_local * n_col
    chunk = rows_local // n_col
    cols = width_local // n_z
    chunks = n_z * n_col
    z_at, col = lax.axis_index("z"), lax.axis_index("col")
    pieces = {}

    def move(slab, offset, part=0, parts=1):
        rows = rows_local // parts
        start = (part * rows, (z_at ^ offset) * cols)
        block = lax.dynamic_slice(slab, start, (rows, cols))
        pieces[offset, part] = from_xor(block, ("z",), offset) if offset else block

    def hold(value, names):
        value, moved = lax.optimization_barrier((value, [pieces[name] for name in names]))
        pieces.update(zip(names, moved))
        return value

    feature_index = col * width_local + jnp.arange(width_local, dtype=jnp.int32)
    omega = sketch_table(sketch_base[0], feature_index, RANK)
    z = lax.dot_general(
        omega, states, (((0,), (1,)), ((), ())), preferred_element_type=jnp.float32
    )
    z = z.reshape(RANK, n_col, chunk).transpose(1, 0, 2)
    z_bits = bits(n_z)[::-1]
    far = z_bits[0]
    move(states, far)
    move(states, 0)
    for offset in range(1, far):
        move(states, offset)
    first = list(pieces)
    z = jnp.concatenate([z, from_xor(z, ("z",), far)])
    z, slab = lax.optimization_barrier((z, states))
    for offset in range(far + 1, n_z):
        move(slab, offset, 0, 2)
        move(slab, offset, 1, 2)
    z = hold(z, [(far, 0)])
    for bit in bits(n_col):
        z = z + from_xor(z, ("col",), bit)
    z = hold(z, [(offset, 0) for offset in range(1, far)])
    for bit in z_bits[1:]:
        z = jnp.concatenate([z, from_xor(z, ("z",), bit)])
    z = hold(z, [(offset, 0) for offset in range(far + 1, n_z)])
    z = z, from_xor(z, ("core",), 1)
    absolute_col = [("col", bit, False) for bit in bits(n_col)[::-1]]
    at_first = chunk_places([("z", bit, True) for bit in z_bits[::-1]] + absolute_col)
    far_digits = [("z", bit, False) for bit in far_bits()]
    col_digits = [("col", bit, True) for bit in bits(n_col)[::-1]]
    near_digit = [("z", 1, True)] if n_z > 2 else []
    by_z, by_col = square_devices()
    at_0 = chunk_places(near_digit + col_digits + far_digits)
    at_1 = at_0 if by_z == by_col else chunk_places(col_digits + near_digit + far_digits)
    core = lax.axis_index("core")
    at_first = jnp.concatenate([at_first, at_first])
    at = jnp.concatenate([jnp.where(core == 0, at_0, at_1), jnp.where(core == 0, at_1, at_0)])
    late = [name for name in pieces if name[0] > far]
    others = {name: from_xor(pieces[name], ("core",), 1) for name in first}

    f32 = jnp.float32
    square = jax.ShapeDtypeStruct((RANK, RANK), f32)
    wide = jax.ShapeDtypeStruct((RANK, rows_total), jnp.bfloat16)
    slab = jax.ShapeDtypeStruct((rows_total, cols), states.dtype)
    parts = jax.ShapeDtypeStruct((chunks, RANK, chunk), f32)
    loadings = jax.ShapeDtypeStruct((RANK, cols // n_core), f32)
    orth_flops = 8 * 64 * 64 * rows_total * 6
    flops = orth_flops + 4 * 64 * rows_total * cols

    basis, upper = call(orth_kernel, (wide, square), orth_flops, (at_first,), *z)
    basis = hold(basis, late)
    others.update((name, from_xor(pieces[name], ("core",), 1)) for name in late)
    blocks = [half[name] for half in (pieces, others) for name in sorted(half)]
    factor = upper.T * (1.0 / math.sqrt(rows_total * width_total))
    a, total = call(power_kernel, (slab, parts), flops, (at,), basis, *blocks)
    z = gather_parts(sum_parts(total, f32))
    for step in range(POWER - 1):
        total = call(orth_power_kernel, parts, flops, (at,), *z, a)
        z = gather_parts(sum_parts(total, jnp.bfloat16))
    at_core = core[None].astype(jnp.int32)
    return call(last_kernel, loadings, flops, (at, at_core), *z, a).T, factor


def local_gram(basis):
    return jnp.dot(basis.T, basis, precision=lax.Precision.HIGHEST)


def orthonormal_block(sketch):
    whole_gram = lax.psum(local_gram(sketch), "row")
    identity = jnp.eye(RANK, dtype=jnp.float32)
    lower = jnp.linalg.cholesky(whole_gram + shift_ratio * jnp.trace(whole_gram) * identity)
    first = jax.scipy.linalg.solve_triangular(lower, sketch.T, lower=True).T
    lower_two = jnp.linalg.cholesky(lax.psum(local_gram(first), "row"))
    return jax.scipy.linalg.solve_triangular(lower_two, first.T, lower=True).T, lower


def per_device_slabs(sketch_base, states):
    width_local = states.shape[1]
    rows_total = states.shape[0] * lax.axis_size("row")
    width_total = width_local * lax.axis_size("col")
    feature_index = lax.axis_index("col") * width_local + jnp.arange(width_local, dtype=jnp.int32)
    omega = sketch_table(sketch_base[0], feature_index, RANK)

    def row_basis(right):
        partial_sketch = jnp.dot(states, right, preferred_element_type=jnp.float32)
        basis_new, lower = orthonormal_block(lax.psum(partial_sketch, "col"))
        return basis_new.astype(jnp.bfloat16), lower

    def back(basis):
        return lax.dot_general(
            states, basis, (((0,), (0,)), ((), ())), preferred_element_type=jnp.float32
        )

    basis, first_lower = row_basis(omega)
    factor = first_lower * (1.0 / math.sqrt(rows_total * width_total))
    for step in range(POWER):
        basis, unused = row_basis(lax.psum(back(basis), "row").astype(jnp.bfloat16))
    return lax.psum_scatter(back(basis), "row", scatter_dimension=0, tiled=True), factor


def solution(mesh):
    n_grp, n_row, n_col = (mesh.shape[name] for name in ("grp", "row", "col"))
    fits = n_row >= 4 and n_row & (n_row - 1) == 0 and n_col & (n_col - 1) == 0

    def run(sketch_base, states):
        rows_local = states.shape[0] // (n_grp * n_row)
        width_local = states.shape[1] // n_col
        tiled = rows_local % (n_col * LANES) == 0 and width_local % (n_row * LANES) == 0
        if fits and tiled:
            split = mesh.devices.reshape(n_grp, n_row // 2, 2, n_col)
            inner = jax.sharding.Mesh(split, ("grp", "z", "core", "col"))
            row, step = ("z", "core"), per_device_transposed
        else:
            inner, row, step = mesh, ("row",), per_device_slabs
        return jax.shard_map(
            step,
            mesh=inner,
            in_specs=(P("grp"), P(("grp",) + row, "col")),
            out_specs=(P(("col",) + row, "grp"), P("grp", None)),
            check_vma=False,
        )(sketch_base, states)

    return run
```

```python
import functools
import math

import jax
import jax.numpy as jnp
from jax import lax
from jax.experimental import pallas as pl
from jax.experimental.pallas import tpu as pltpu
from jax.sharding import PartitionSpec as P

RANK = 64
POWER = 4
LANES = 128
SUB = 8
TILE = 256


shift_ratio = 0.005


def scramble(value):
    value = value ^ jnp.right_shift(value, 16) & 65535
    value = value * 73244475
    value = value ^ jnp.right_shift(value, 16) & 65535
    value = value * 73244475
    value = value ^ jnp.right_shift(value, 16) & 65535
    return value


def sketch_table(base_value, feature_index, rank):
    counter = feature_index[:, None] * rank + jnp.arange(rank, dtype=jnp.int32)[None, :]
    offset = scramble(base_value)
    total = jnp.zeros(counter.shape, jnp.float32)
    for j in range(4):
        hashed = scramble(counter * 4 + j + offset)
        total = total + (hashed & 16777215).astype(jnp.float32) * (1.0 / 16777216.0)
    return ((total - 2.0) * 1.7320508).astype(jnp.bfloat16)


def terms_of(value):
    if value.dtype == jnp.bfloat16:
        return [value]
    high = value.astype(jnp.bfloat16)
    rest = value - high.astype(jnp.float32)
    middle = rest.astype(jnp.bfloat16)
    low = (rest - middle.astype(jnp.float32)).astype(jnp.bfloat16)
    return [high, middle, low]


def dot_nn(left, right):
    return lax.dot_general(
        left, right, (((1,), (0,)), ((), ())), preferred_element_type=jnp.float32
    )


def dot_nt(left, right):
    return lax.dot_general(
        left, right, (((1,), (1,)), ((), ())), preferred_element_type=jnp.float32
    )


def small_times_wide(small, wide):
    left, right = terms_of(small), terms_of(wide)
    pairs = [(i, d - i) for d in (2, 1, 0) for i in range(d + 1)]
    pairs = [(i, j) for i, j in pairs if i < len(left) and j < len(right)]
    return dot_nn(
        jnp.concatenate([left[i] for i, unused in pairs], axis=1),
        jnp.concatenate([right[j] for unused, j in pairs], axis=0),
    )


def gram_of(wide):
    terms = terms_of(wide)
    if len(terms) == 1:
        return dot_nt(terms[0], terms[0])
    rank = wide.shape[0]
    stacked = jnp.concatenate(terms, axis=0)
    both = dot_nt(stacked, stacked)
    cross = both[rank : 2 * rank, :rank] + both[2 * rank :, :rank]
    return both[:rank, :rank] + ((cross + cross.T) + both[rank : 2 * rank, rank : 2 * rank])


def eliminate(matrix, beside=()):
    beside = list(beside)
    size = matrix.shape[0]
    blocks = size // SUB
    row_index = lax.broadcasted_iota(jnp.int32, (SUB, 2 * size), 0)
    square_row = lax.broadcasted_iota(jnp.int32, (SUB, size), 0)
    square_col = lax.broadcasted_iota(jnp.int32, (SUB, size), 1)
    work = []
    for i in range(blocks):
        unit = jnp.where(square_col == square_row + SUB * i, 1.0, 0.0).astype(jnp.float32)
        work.append(jnp.concatenate([matrix[SUB * i : SUB * (i + 1), :], unit], axis=1))

    def fill(register, k):
        return jnp.broadcast_to(register[k : k + 1, :], (SUB, 2 * size))

    rows = []
    for b in range(blocks):
        for unused in range(-(-len(beside) // (blocks - b))):
            beside.pop(0)()
        columns = [
            {
                i: jnp.broadcast_to(work[i][:, SUB * b + j : SUB * b + j + 1], (SUB, 2 * size))
                for i in range(b, blocks)
            }
            for j in range(SUB)
        ]
        pivots = jnp.ones((SUB, 2 * size), jnp.float32)
        for k in range(0, SUB, 2):
            col_0, col_1 = columns[k], columns[k + 1]
            a, h, d = fill(col_0[b], k), fill(col_1[b], k), fill(col_1[b], k + 1)
            det = a * d - h * h
            over_det, over_a = 1.0 / det, 1.0 / a
            below_0 = jnp.where(row_index > k + 1, col_0[b], 0.0)
            below_1 = jnp.where(row_index > k + 1, col_1[b], 0.0)
            for j in range(k + 2, SUB):
                entry_0, entry_1 = fill(columns[j][b], k), fill(columns[j][b], k + 1)
                up_0 = d * entry_0 - h * entry_1
                up_1 = a * entry_1 - h * entry_0
                columns[j][b] = columns[j][b] - over_det * (below_0 * up_0 + below_1 * up_1)
                up_0, up_1 = over_det * up_0, over_det * up_1
                for i in range(b + 1, blocks):
                    columns[j][i] = columns[j][i] - (col_0[i] * up_0 + col_1[i] * up_1)
            row_0, row_1 = fill(work[b], k), fill(work[b], k + 1)
            up_0 = over_det * (d * row_0 - h * row_1)
            up_1 = over_det * (a * row_1 - h * row_0)
            for i in range(b + 1, blocks):
                work[i] = work[i] - (col_0[i] * up_0 + col_1[i] * up_1)
            second = jnp.where(row_index == k + 1, h * over_a, 0.0)
            work[b] = work[b] - (below_0 * up_0 + below_1 * up_1 + second * row_0)
            pivots = jnp.where(row_index == k, a, pivots)
            pivots = jnp.where(row_index == k + 1, det * over_a, pivots)
        rows.append(work[b] * lax.rsqrt(pivots))
    both = jnp.concatenate(rows, axis=0)
    keep = lax.broadcasted_iota(jnp.int32, (size, size), 1) >= lax.broadcasted_iota(
        jnp.int32, (size, size), 0
    )
    return jnp.where(keep, both[:, :size], 0.0), both[:, size:]


def shifted_factor(wide):
    whole_gram = gram_of(wide)
    squares = wide.astype(jnp.float32)
    squares = jnp.sum(squares * squares, axis=0, keepdims=True)
    trace = jnp.sum(squares, axis=1, keepdims=True)
    size = whole_gram.shape[0]
    diagonal = lax.broadcasted_iota(jnp.int32, (size, size), 0) == lax.broadcasted_iota(
        jnp.int32, (size, size), 1
    )
    scaled = whole_gram * (1.0 / trace)
    upper, inverse = eliminate(jnp.where(diagonal, scaled + shift_ratio, scaled))
    root = jnp.sqrt(trace)
    return upper * root, inverse * (1.0 / root)


def wide_of(at_ref, z_refs):
    chunks = [z_ref[at_ref[i]] for z_ref in z_refs for i in range(at_ref.shape[0])]
    return jnp.concatenate(chunks, axis=1)


def first_pass(at_ref, z_refs):
    wide = wide_of(at_ref, z_refs)
    upper, inverse_one = shifted_factor(wide)
    return small_times_wide(inverse_one, wide), upper


def back_product(at_ref, z_refs, a):
    first, unused = first_pass(at_ref, z_refs)
    rank = first.shape[0]
    terms = jnp.concatenate(terms_of(first), axis=0)
    tiles = []

    def tile(start):
        back = dot_nn(terms, a[:, start : start + TILE])
        tiles.append(back[:rank] + (back[rank : 2 * rank] + back[2 * rank :]))

    starts = range(0, a.shape[1], TILE)
    work = [functools.partial(tile, start) for start in starts]
    unused, inverse_two = eliminate(gram_of(first), work)
    return small_times_wide(inverse_two, jnp.concatenate(tiles, axis=1))


def store_parts(forth, at_ref, part_ref):
    chunks, unused, width = part_ref.shape
    for i in range(chunks):
        part_ref[at_ref[i]] = forth[:, width * i : width * (i + 1)]


def orth_kernel(at_ref, z_ref, other_ref, basis_ref, upper_ref):
    first, upper = first_pass(at_ref, (z_ref, other_ref))
    unused, inverse_two = eliminate(gram_of(first))
    basis_ref[...] = small_times_wide(inverse_two, first).astype(jnp.bfloat16)
    upper_ref[...] = upper


def power_kernel(at_ref, basis_ref, *refs):
    piece_refs, a_ref, part_ref = refs[:-2], refs[-2], refs[-1]
    start = 0
    for piece_ref in piece_refs:
        a_ref[start : start + piece_ref.shape[0], :] = piece_ref[...]
        start += piece_ref.shape[0]
    weights = dot_nn(basis_ref[...], a_ref[...]).astype(jnp.bfloat16)
    forth = dot_nt(weights, a_ref[: part_ref.shape[0] * part_ref.shape[2], :])
    store_parts(forth, at_ref, part_ref)


def turn_kernel(a_ref, turned_ref):
    turned_ref[...] = a_ref[: turned_ref.shape[1], :].T


def orth_power_kernel(at_ref, z_ref, other_ref, a_ref, turned_ref, part_ref):
    weights = back_product(at_ref, (z_ref, other_ref), a_ref[...]).astype(jnp.bfloat16)
    store_parts(dot_nn(weights, turned_ref[...]), at_ref, part_ref)


def last_kernel(at_ref, core_ref, z_ref, other_ref, a_ref, out_ref):
    cols = out_ref.shape[1]
    start = pl.multiple_of(core_ref[0] * cols, cols)
    out_ref[...] = back_product(at_ref, (z_ref, other_ref), a_ref[:, pl.ds(start, cols)])


def call(kernel, out_shapes, flops, scalars, *operands):
    moved = sum(x.size * x.dtype.itemsize for x in operands)
    return pl.pallas_call(
        kernel,
        out_shape=out_shapes,
        in_specs=[pl.BlockSpec(memory_space=pltpu.SMEM)] * len(scalars)
        + [pl.BlockSpec(memory_space=pltpu.VMEM)] * len(operands),
        out_specs=jax.tree.map(lambda _: pl.BlockSpec(memory_space=pltpu.VMEM), out_shapes),
        compiler_params=pltpu.CompilerParams(vmem_limit_bytes=20 * 1024 * 1024),
        cost_estimate=pl.CostEstimate(flops=flops, bytes_accessed=moved, transcendentals=0),
    )(*scalars, *operands)


def bits(size):
    return [1 << k for k in range(size.bit_length() - 1)]


def from_xor(value, axis, offset):
    size = math.prod(lax.axis_size(name) for name in axis)
    return lax.ppermute(value, axis, [(i, i ^ offset) for i in range(size)])


def square_devices():
    n_z, n_col = lax.axis_size("z"), lax.axis_size("col")
    sides = [(z, col) for z in range(2 if n_z > 2 else 1) for col in range(n_col)]
    return [(z * n_col + col, col * (2 if n_z > 2 else 1) + z) for z, col in sides[:0:-1]]


def sum_parts(total, dtype):
    offsets = square_devices()
    step = total.shape[0] // (len(offsets) + 1)
    others = [
        from_xor(total[step * place : step * (place + 1)].astype(dtype), ("z", "col"), offset)
        for offset, place in offsets
    ]
    total = functools.reduce(jnp.add, [x.astype(jnp.float32) for x in others], total[:step])
    for bit in far_bits():
        mine = total.astype(dtype)
        total = mine.astype(jnp.float32) + from_xor(mine, ("z",), bit).astype(jnp.float32)
    return total.astype(dtype)


def gather_parts(own):
    placed = {0: own}
    for offset, place in square_devices():
        placed[place] = from_xor(own, ("z", "col"), offset)
    own = jnp.concatenate([placed[place] for place in sorted(placed)])
    return own, from_xor(own, ("core",), 1)


def far_bits():
    return bits(lax.axis_size("z"))[1 if lax.axis_size("z") > 2 else 0 :]


def chunk_places(digits):
    n_z, n_col = lax.axis_size("z"), lax.axis_size("col")
    index = jnp.arange(n_z * n_col, dtype=jnp.int32)
    z_at, col_at = lax.axis_index("z"), lax.axis_index("col")
    column = index % n_col
    relative = {"z": index // n_col, "col": column ^ col_at}
    absolute = {"z": relative["z"] ^ z_at, "col": column}
    place = jnp.zeros_like(index)
    for axis, bit, is_relative in digits:
        place = place * 2 + ((relative if is_relative else absolute)[axis] // bit) % 2
    return place.astype(jnp.int32)


def per_device_transposed(sketch_base, states):
    n_z, n_core, n_col = lax.axis_size("z"), lax.axis_size("core"), lax.axis_size("col")
    n_row = n_z * n_core
    rows_local, width_local = states.shape
    rows_total, width_total = rows_local * n_row, width_local * n_col
    chunk = rows_local // n_col
    cols = width_local // n_z
    chunks = n_z * n_col
    z_at, col = lax.axis_index("z"), lax.axis_index("col")
    pieces = {}

    def move(slab, offset, part=0, parts=1):
        rows = rows_local // parts
        start = (part * rows, (z_at ^ offset) * cols)
        block = lax.dynamic_slice(slab, start, (rows, cols))
        pieces[offset, part] = from_xor(block, ("z",), offset) if offset else block

    def hold(value, names):
        value, moved = lax.optimization_barrier((value, [pieces[name] for name in names]))
        pieces.update(zip(names, moved))
        return value

    feature_index = col * width_local + jnp.arange(width_local, dtype=jnp.int32)
    omega = sketch_table(sketch_base[0], feature_index, RANK)
    z = lax.dot_general(
        omega, states, (((0,), (1,)), ((), ())), preferred_element_type=jnp.float32
    )
    z = z.reshape(RANK, n_col, chunk).transpose(1, 0, 2)
    z_bits = bits(n_z)[::-1]
    far = z_bits[0]
    for offset in [0, far, *range(1, far)]:
        move(states, offset)
    first = list(pieces)
    z = jnp.concatenate([z, from_xor(z, ("z",), far)])
    z, slab = lax.optimization_barrier((z, states))
    for offset in range(far + 1, n_z):
        move(slab, offset, 0, 2)
        move(slab, offset, 1, 2)
    for bit in bits(n_col):
        z = z + from_xor(z, ("col",), bit)
    z = hold(z, first)
    for bit in z_bits[1:]:
        z = jnp.concatenate([z, from_xor(z, ("z",), bit)])
    z = hold(z, [(offset, 0) for offset in range(far + 1, n_z)])
    z = z, from_xor(z, ("core",), 1)
    absolute_col = [("col", bit, False) for bit in bits(n_col)[::-1]]
    at_first = chunk_places([("z", bit, True) for bit in z_bits[::-1]] + absolute_col)
    digits = [("col", bit, True) for bit in bits(n_col)[::-1]]
    digits += [("z", 1, True)] if n_z > 2 else []
    at = chunk_places(digits + [("z", bit, False) for bit in far_bits()])
    late = [name for name in pieces if name[0] > far]
    others = {name: from_xor(pieces[name], ("core",), 1) for name in first}

    f32 = jnp.float32
    square = jax.ShapeDtypeStruct((RANK, RANK), f32)
    wide = jax.ShapeDtypeStruct((RANK, rows_total), jnp.bfloat16)
    slab = jax.ShapeDtypeStruct((rows_total, cols), states.dtype)
    parts = jax.ShapeDtypeStruct((chunks, RANK, chunk), f32)
    loadings = jax.ShapeDtypeStruct((RANK, cols // n_core), f32)
    orth_flops = 8 * 64 * 64 * rows_total * 6
    flops = orth_flops + 4 * 64 * rows_total * cols

    basis, upper = call(orth_kernel, (wide, square), orth_flops, (at_first,), *z)
    basis = hold(basis, late)
    others.update((name, from_xor(pieces[name], ("core",), 1)) for name in late)
    blocks = [half[name] for half in (pieces, others) for name in sorted(half)]
    factor = upper.T * (1.0 / math.sqrt(rows_total * width_total))
    a, total = call(power_kernel, (slab, parts), flops, (at,), basis, *blocks)
    turned = jax.ShapeDtypeStruct((cols, rows_total // n_core), states.dtype)
    turned = call(turn_kernel, turned, flops, (), a)
    share, turned = lax.optimization_barrier((sum_parts(total, f32), turned))
    z = gather_parts(share)
    for step in range(POWER - 1):
        total = call(orth_power_kernel, parts, flops, (at,), *z, a, turned)
        z = gather_parts(sum_parts(total, jnp.bfloat16))
    core = lax.axis_index("core")[None].astype(jnp.int32)
    return call(last_kernel, loadings, flops, (at, core), *z, a).T, factor


def local_gram(basis):
    return jnp.dot(basis.T, basis, precision=lax.Precision.HIGHEST)


def orthonormal_block(sketch):
    whole_gram = lax.psum(local_gram(sketch), "row")
    identity = jnp.eye(RANK, dtype=jnp.float32)
    lower = jnp.linalg.cholesky(whole_gram + shift_ratio * jnp.trace(whole_gram) * identity)
    first = jax.scipy.linalg.solve_triangular(lower, sketch.T, lower=True).T
    lower_two = jnp.linalg.cholesky(lax.psum(local_gram(first), "row"))
    return jax.scipy.linalg.solve_triangular(lower_two, first.T, lower=True).T, lower


def per_device_slabs(sketch_base, states):
    width_local = states.shape[1]
    rows_total = states.shape[0] * lax.axis_size("row")
    width_total = width_local * lax.axis_size("col")
    feature_index = lax.axis_index("col") * width_local + jnp.arange(width_local, dtype=jnp.int32)
    omega = sketch_table(sketch_base[0], feature_index, RANK)

    def row_basis(right):
        partial_sketch = jnp.dot(states, right, preferred_element_type=jnp.float32)
        basis_new, lower = orthonormal_block(lax.psum(partial_sketch, "col"))
        return basis_new.astype(jnp.bfloat16), lower

    def back(basis):
        return lax.dot_general(
            states, basis, (((0,), (0,)), ((), ())), preferred_element_type=jnp.float32
        )

    basis, first_lower = row_basis(omega)
    factor = first_lower * (1.0 / math.sqrt(rows_total * width_total))
    for step in range(POWER):
        basis, unused = row_basis(lax.psum(back(basis), "row").astype(jnp.bfloat16))
    return lax.psum_scatter(back(basis), "row", scatter_dimension=0, tiled=True), factor


def solution(mesh):
    n_grp, n_row, n_col = (mesh.shape[name] for name in ("grp", "row", "col"))
    fits = n_row >= 4 and n_row & (n_row - 1) == 0 and n_col & (n_col - 1) == 0

    def run(sketch_base, states):
        rows_local = states.shape[0] // (n_grp * n_row)
        width_local = states.shape[1] // n_col
        tiled = rows_local % (n_col * LANES) == 0 and width_local % (n_row * LANES) == 0
        if fits and tiled:
            split = mesh.devices.reshape(n_grp, n_row // 2, 2, n_col)
            inner = jax.sharding.Mesh(split, ("grp", "z", "core", "col"))
            row, step = ("z", "core"), per_device_transposed
        else:
            inner, row, step = mesh, ("row",), per_device_slabs
        return jax.shard_map(
            step,
            mesh=inner,
            in_specs=(P("grp"), P(("grp",) + row, "col")),
            out_specs=(P(("col",) + row, "grp"), P("grp", None)),
            check_vma=False,
        )(sketch_base, states)

    return run
```

```python
import functools
import math

import jax
import jax.numpy as jnp
from jax import lax
from jax.experimental import pallas as pl
from jax.experimental.pallas import tpu as pltpu
from jax.sharding import PartitionSpec as P

RANK = 64
POWER = 4
LANES = 128
SUB = 8
TILE = 256


shift_ratio = 0.005


def scramble(value):
    value = value ^ jnp.right_shift(value, 16) & 65535
    value = value * 73244475
    value = value ^ jnp.right_shift(value, 16) & 65535
    value = value * 73244475
    value = value ^ jnp.right_shift(value, 16) & 65535
    return value


def sketch_table(base_value, feature_index, rank):
    counter = feature_index[:, None] * rank + jnp.arange(rank, dtype=jnp.int32)[None, :]
    offset = scramble(base_value)
    total = jnp.zeros(counter.shape, jnp.float32)
    for j in range(4):
        hashed = scramble(counter * 4 + j + offset)
        total = total + (hashed & 16777215).astype(jnp.float32) * (1.0 / 16777216.0)
    return ((total - 2.0) * 1.7320508).astype(jnp.bfloat16)


def terms_of(value):
    if value.dtype == jnp.bfloat16:
        return [value]
    high = value.astype(jnp.bfloat16)
    rest = value - high.astype(jnp.float32)
    middle = rest.astype(jnp.bfloat16)
    low = (rest - middle.astype(jnp.float32)).astype(jnp.bfloat16)
    return [high, middle, low]


def dot_nn(left, right):
    return lax.dot_general(
        left, right, (((1,), (0,)), ((), ())), preferred_element_type=jnp.float32
    )


def dot_nt(left, right):
    return lax.dot_general(
        left, right, (((1,), (1,)), ((), ())), preferred_element_type=jnp.float32
    )


def small_times_wide(small, wide):
    left, right = terms_of(small), terms_of(wide)
    pairs = [(i, d - i) for d in (2, 1, 0) for i in range(d + 1)]
    pairs = [(i, j) for i, j in pairs if i < len(left) and j < len(right)]
    return dot_nn(
        jnp.concatenate([left[i] for i, unused in pairs], axis=1),
        jnp.concatenate([right[j] for unused, j in pairs], axis=0),
    )


def gram_of(wide):
    terms = terms_of(wide)
    if len(terms) == 1:
        return dot_nt(terms[0], terms[0])
    rank = wide.shape[0]
    stacked = jnp.concatenate(terms, axis=0)
    both = dot_nt(stacked, stacked)
    cross = both[rank : 2 * rank, :rank] + both[2 * rank :, :rank]
    return both[:rank, :rank] + ((cross + cross.T) + both[rank : 2 * rank, rank : 2 * rank])


def eliminate(matrix, beside=()):
    beside = list(beside)
    size = matrix.shape[0]
    blocks = size // SUB
    row_index = lax.broadcasted_iota(jnp.int32, (SUB, 2 * size), 0)
    square_row = lax.broadcasted_iota(jnp.int32, (SUB, size), 0)
    square_col = lax.broadcasted_iota(jnp.int32, (SUB, size), 1)
    work = []
    for i in range(blocks):
        unit = jnp.where(square_col == square_row + SUB * i, 1.0, 0.0).astype(jnp.float32)
        work.append(jnp.concatenate([matrix[SUB * i : SUB * (i + 1), :], unit], axis=1))

    def fill(register, k):
        return jnp.broadcast_to(register[k : k + 1, :], (SUB, 2 * size))

    rows = []
    for b in range(blocks):
        for unused in range(-(-len(beside) // (blocks - b))):
            beside.pop(0)()
        columns = [
            {
                i: jnp.broadcast_to(work[i][:, SUB * b + j : SUB * b + j + 1], (SUB, 2 * size))
                for i in range(b, blocks)
            }
            for j in range(SUB)
        ]
        pivots = jnp.ones((SUB, 2 * size), jnp.float32)
        for k in range(0, SUB, 2):
            col_0, col_1 = columns[k], columns[k + 1]
            a, h, d = fill(col_0[b], k), fill(col_1[b], k), fill(col_1[b], k + 1)
            det = a * d - h * h
            over_det, over_a = 1.0 / det, 1.0 / a
            below_0 = jnp.where(row_index > k + 1, col_0[b], 0.0)
            below_1 = jnp.where(row_index > k + 1, col_1[b], 0.0)
            for j in range(k + 2, SUB):
                entry_0, entry_1 = fill(columns[j][b], k), fill(columns[j][b], k + 1)
                up_0 = d * entry_0 - h * entry_1
                up_1 = a * entry_1 - h * entry_0
                columns[j][b] = columns[j][b] - over_det * (below_0 * up_0 + below_1 * up_1)
                up_0, up_1 = over_det * up_0, over_det * up_1
                for i in range(b + 1, blocks):
                    columns[j][i] = columns[j][i] - (col_0[i] * up_0 + col_1[i] * up_1)
            row_0, row_1 = fill(work[b], k), fill(work[b], k + 1)
            up_0 = over_det * (d * row_0 - h * row_1)
            up_1 = over_det * (a * row_1 - h * row_0)
            for i in range(b + 1, blocks):
                work[i] = work[i] - (col_0[i] * up_0 + col_1[i] * up_1)
            second = jnp.where(row_index == k + 1, h * over_a, 0.0)
            work[b] = work[b] - (below_0 * up_0 + below_1 * up_1 + second * row_0)
            pivots = jnp.where(row_index == k, a, pivots)
            pivots = jnp.where(row_index == k + 1, det * over_a, pivots)
        rows.append(work[b] * lax.rsqrt(pivots))
    both = jnp.concatenate(rows, axis=0)
    keep = lax.broadcasted_iota(jnp.int32, (size, size), 1) >= lax.broadcasted_iota(
        jnp.int32, (size, size), 0
    )
    return jnp.where(keep, both[:, :size], 0.0), both[:, size:]


def shifted_factor(wide):
    whole_gram = gram_of(wide)
    squares = wide.astype(jnp.float32)
    squares = jnp.sum(squares * squares, axis=0, keepdims=True)
    trace = jnp.sum(squares, axis=1, keepdims=True)
    size = whole_gram.shape[0]
    diagonal = lax.broadcasted_iota(jnp.int32, (size, size), 0) == lax.broadcasted_iota(
        jnp.int32, (size, size), 1
    )
    scaled = whole_gram * (1.0 / trace)
    upper, inverse = eliminate(jnp.where(diagonal, scaled + shift_ratio, scaled))
    root = jnp.sqrt(trace)
    return upper * root, inverse * (1.0 / root)


def wide_of(at_ref, z_refs):
    chunks = [z_ref[at_ref[i]] for z_ref in z_refs for i in range(at_ref.shape[0])]
    return jnp.concatenate(chunks, axis=1)


def first_pass(at_ref, z_refs):
    wide = wide_of(at_ref, z_refs)
    upper, inverse_one = shifted_factor(wide)
    return small_times_wide(inverse_one, wide), upper


def back_product(at_ref, z_refs, a):
    first, unused = first_pass(at_ref, z_refs)
    rank = first.shape[0]
    terms = jnp.concatenate(terms_of(first), axis=0)
    tiles = []

    def tile(start):
        back = dot_nn(terms, a[:, start : start + TILE])
        tiles.append(back[:rank] + (back[rank : 2 * rank] + back[2 * rank :]))

    starts = range(0, a.shape[1], TILE)
    work = [functools.partial(tile, start) for start in starts]
    unused, inverse_two = eliminate(gram_of(first), work)
    return small_times_wide(inverse_two, jnp.concatenate(tiles, axis=1))


def store_parts(forth, at_ref, part_ref):
    chunks, unused, width = part_ref.shape
    for i in range(chunks):
        part_ref[at_ref[i]] = forth[:, width * i : width * (i + 1)]


def orth_kernel(at_ref, z_ref, other_ref, basis_ref, upper_ref):
    first, upper = first_pass(at_ref, (z_ref, other_ref))
    unused, inverse_two = eliminate(gram_of(first))
    basis_ref[...] = small_times_wide(inverse_two, first).astype(jnp.bfloat16)
    upper_ref[...] = upper


def power_kernel(at_ref, basis_ref, *refs):
    piece_refs, a_ref, part_ref = refs[:-2], refs[-2], refs[-1]
    start = 0
    for piece_ref in piece_refs:
        a_ref[start : start + piece_ref.shape[0], :] = piece_ref[...]
        start += piece_ref.shape[0]
    weights = dot_nn(basis_ref[...], a_ref[...]).astype(jnp.bfloat16)
    forth = dot_nt(weights, a_ref[: part_ref.shape[0] * part_ref.shape[2], :])
    store_parts(forth, at_ref, part_ref)


def turn_kernel(a_ref, turned_ref):
    turned_ref[...] = a_ref[: turned_ref.shape[1], :].T


def orth_power_kernel(at_ref, z_ref, other_ref, a_ref, turned_ref, part_ref):
    weights = back_product(at_ref, (z_ref, other_ref), a_ref[...]).astype(jnp.bfloat16)
    store_parts(dot_nn(weights, turned_ref[...]), at_ref, part_ref)


def last_kernel(at_ref, core_ref, z_ref, other_ref, a_ref, out_ref):
    cols = out_ref.shape[1]
    start = pl.multiple_of(core_ref[0] * cols, cols)
    out_ref[...] = back_product(at_ref, (z_ref, other_ref), a_ref[:, pl.ds(start, cols)])


def call(kernel, out_shapes, flops, scalars, *operands):
    moved = sum(x.size * x.dtype.itemsize for x in operands)
    return pl.pallas_call(
        kernel,
        out_shape=out_shapes,
        in_specs=[pl.BlockSpec(memory_space=pltpu.SMEM)] * len(scalars)
        + [pl.BlockSpec(memory_space=pltpu.VMEM)] * len(operands),
        out_specs=jax.tree.map(lambda _: pl.BlockSpec(memory_space=pltpu.VMEM), out_shapes),
        compiler_params=pltpu.CompilerParams(vmem_limit_bytes=20 * 1024 * 1024),
        cost_estimate=pl.CostEstimate(flops=flops, bytes_accessed=moved, transcendentals=0),
    )(*scalars, *operands)


def bits(size):
    return [1 << k for k in range(size.bit_length() - 1)]


def from_xor(value, axis, offset):
    size = math.prod(lax.axis_size(name) for name in axis)
    return lax.ppermute(value, axis, [(i, i ^ offset) for i in range(size)])


def square_devices():
    n_z, n_col = lax.axis_size("z"), lax.axis_size("col")
    sides = [(z, col) for z in range(2 if n_z > 2 else 1) for col in range(n_col)]
    return [(z * n_col + col, col * (2 if n_z > 2 else 1) + z) for z, col in sides[:0:-1]]


def sum_parts(total, dtype):
    offsets = square_devices()
    step = total.shape[0] // (len(offsets) + 1)
    others = [
        from_xor(total[step * place : step * (place + 1)].astype(dtype), ("z", "col"), offset)
        for offset, place in offsets
    ]
    total = functools.reduce(jnp.add, [x.astype(jnp.float32) for x in others], total[:step])
    for bit in far_bits():
        mine = total.astype(dtype)
        total = mine.astype(jnp.float32) + from_xor(mine, ("z",), bit).astype(jnp.float32)
    return total.astype(dtype)


def gather_parts(own):
    placed = {0: own}
    for offset, place in square_devices():
        placed[place] = from_xor(own, ("z", "col"), offset)
    own = jnp.concatenate([placed[place] for place in sorted(placed)])
    return own, from_xor(own, ("core",), 1)


def far_bits():
    return bits(lax.axis_size("z"))[1 if lax.axis_size("z") > 2 else 0 :]


def chunk_places(digits):
    n_z, n_col = lax.axis_size("z"), lax.axis_size("col")
    index = jnp.arange(n_z * n_col, dtype=jnp.int32)
    z_at, col_at = lax.axis_index("z"), lax.axis_index("col")
    column = index % n_col
    relative = {"z": index // n_col, "col": column ^ col_at}
    absolute = {"z": relative["z"] ^ z_at, "col": column}
    place = jnp.zeros_like(index)
    for axis, bit, is_relative in digits:
        place = place * 2 + ((relative if is_relative else absolute)[axis] // bit) % 2
    return place.astype(jnp.int32)


def per_device_transposed(sketch_base, states):
    n_z, n_core, n_col = lax.axis_size("z"), lax.axis_size("core"), lax.axis_size("col")
    n_row = n_z * n_core
    rows_local, width_local = states.shape
    rows_total, width_total = rows_local * n_row, width_local * n_col
    chunk = rows_local // n_col
    cols = width_local // n_z
    chunks = n_z * n_col
    z_at, col = lax.axis_index("z"), lax.axis_index("col")
    pieces = {}

    def block(offset, part=0, parts=1):
        rows = rows_local // parts
        start = (part * rows, (z_at ^ offset) * cols)
        return lax.dynamic_slice(states, start, (rows, cols))

    def move(blocks):
        for name, value in blocks.items():
            pieces[name] = from_xor(value, ("z",), name[0]) if name[0] else value

    def hold(value, names):
        value, moved = lax.optimization_barrier((value, [pieces[name] for name in names]))
        pieces.update(zip(names, moved))
        return value

    feature_index = col * width_local + jnp.arange(width_local, dtype=jnp.int32)
    omega = sketch_table(sketch_base[0], feature_index, RANK)
    z = lax.dot_general(
        omega, states, (((0,), (1,)), ((), ())), preferred_element_type=jnp.float32
    )
    z = z.reshape(RANK, n_col, chunk).transpose(1, 0, 2)
    z_bits = bits(n_z)[::-1]
    far = z_bits[0]
    move({(offset, 0): block(offset) for offset in [0, far, *range(1, far)]})
    first = list(pieces)
    late = {(o, part): block(o, part, 2) for o in range(far + 1, n_z) for part in range(2)}
    z = jnp.concatenate([z, from_xor(z, ("z",), far)])
    z, late = lax.optimization_barrier((z, late))
    move(late)
    for bit in bits(n_col):
        z = z + from_xor(z, ("col",), bit)
    z = hold(z, first)
    for bit in z_bits[1:]:
        z = jnp.concatenate([z, from_xor(z, ("z",), bit)])
    z = hold(z, [(offset, 0) for offset in range(far + 1, n_z)])
    z = z, from_xor(z, ("core",), 1)
    absolute_col = [("col", bit, False) for bit in bits(n_col)[::-1]]
    at_first = chunk_places([("z", bit, True) for bit in z_bits[::-1]] + absolute_col)
    digits = [("col", bit, True) for bit in bits(n_col)[::-1]]
    digits += [("z", 1, True)] if n_z > 2 else []
    at = chunk_places(digits + [("z", bit, False) for bit in far_bits()])
    late = list(late)
    others = {name: from_xor(pieces[name], ("core",), 1) for name in first}

    f32 = jnp.float32
    square = jax.ShapeDtypeStruct((RANK, RANK), f32)
    wide = jax.ShapeDtypeStruct((RANK, rows_total), jnp.bfloat16)
    slab = jax.ShapeDtypeStruct((rows_total, cols), states.dtype)
    parts = jax.ShapeDtypeStruct((chunks, RANK, chunk), f32)
    loadings = jax.ShapeDtypeStruct((RANK, cols // n_core), f32)
    orth_flops = 8 * 64 * 64 * rows_total * 6
    flops = orth_flops + 4 * 64 * rows_total * cols

    basis, upper = call(orth_kernel, (wide, square), orth_flops, (at_first,), *z)
    basis = hold(basis, late)
    others.update((name, from_xor(pieces[name], ("core",), 1)) for name in late)
    blocks = [half[name] for half in (pieces, others) for name in sorted(half)]
    factor = upper.T * (1.0 / math.sqrt(rows_total * width_total))
    a, total = call(power_kernel, (slab, parts), flops, (at,), basis, *blocks)
    turned = jax.ShapeDtypeStruct((cols, rows_total // n_core), states.dtype)
    turned = call(turn_kernel, turned, flops, (), a)
    share, turned = lax.optimization_barrier((sum_parts(total, f32), turned))
    z = gather_parts(share)
    for step in range(POWER - 1):
        total = call(orth_power_kernel, parts, flops, (at,), *z, a, turned)
        z = gather_parts(sum_parts(total, jnp.bfloat16))
    core = lax.axis_index("core")[None].astype(jnp.int32)
    return call(last_kernel, loadings, flops, (at, core), *z, a).T, factor


def local_gram(basis):
    return jnp.dot(basis.T, basis, precision=lax.Precision.HIGHEST)


def orthonormal_block(sketch):
    whole_gram = lax.psum(local_gram(sketch), "row")
    identity = jnp.eye(RANK, dtype=jnp.float32)
    lower = jnp.linalg.cholesky(whole_gram + shift_ratio * jnp.trace(whole_gram) * identity)
    first = jax.scipy.linalg.solve_triangular(lower, sketch.T, lower=True).T
    lower_two = jnp.linalg.cholesky(lax.psum(local_gram(first), "row"))
    return jax.scipy.linalg.solve_triangular(lower_two, first.T, lower=True).T, lower


def per_device_slabs(sketch_base, states):
    width_local = states.shape[1]
    rows_total = states.shape[0] * lax.axis_size("row")
    width_total = width_local * lax.axis_size("col")
    feature_index = lax.axis_index("col") * width_local + jnp.arange(width_local, dtype=jnp.int32)
    omega = sketch_table(sketch_base[0], feature_index, RANK)

    def row_basis(right):
        partial_sketch = jnp.dot(states, right, preferred_element_type=jnp.float32)
        basis_new, lower = orthonormal_block(lax.psum(partial_sketch, "col"))
        return basis_new.astype(jnp.bfloat16), lower

    def back(basis):
        return lax.dot_general(
            states, basis, (((0,), (0,)), ((), ())), preferred_element_type=jnp.float32
        )

    basis, first_lower = row_basis(omega)
    factor = first_lower * (1.0 / math.sqrt(rows_total * width_total))
    for step in range(POWER):
        basis, unused = row_basis(lax.psum(back(basis), "row").astype(jnp.bfloat16))
    return lax.psum_scatter(back(basis), "row", scatter_dimension=0, tiled=True), factor


def solution(mesh):
    n_grp, n_row, n_col = (mesh.shape[name] for name in ("grp", "row", "col"))
    fits = n_row >= 4 and n_row & (n_row - 1) == 0 and n_col & (n_col - 1) == 0

    def run(sketch_base, states):
        rows_local = states.shape[0] // (n_grp * n_row)
        width_local = states.shape[1] // n_col
        tiled = rows_local % (n_col * LANES) == 0 and width_local % (n_row * LANES) == 0
        if fits and tiled:
            split = mesh.devices.reshape(n_grp, n_row // 2, 2, n_col)
            inner = jax.sharding.Mesh(split, ("grp", "z", "core", "col"))
            row, step = ("z", "core"), per_device_transposed
        else:
            inner, row, step = mesh, ("row",), per_device_slabs
        return jax.shard_map(
            step,
            mesh=inner,
            in_specs=(P("grp"), P(("grp",) + row, "col")),
            out_specs=(P(("col",) + row, "grp"), P("grp", None)),
            check_vma=False,
        )(sketch_base, states)

    return run
```

```python
import functools
import math

import jax
import jax.numpy as jnp
from jax import lax
from jax.experimental import pallas as pl
from jax.experimental.pallas import tpu as pltpu
from jax.sharding import PartitionSpec as P

RANK = 64
POWER = 4
LANES = 128
SUB = 8
TILE = 256


shift_ratio = 0.005


def scramble(value):
    value = value ^ jnp.right_shift(value, 16) & 65535
    value = value * 73244475
    value = value ^ jnp.right_shift(value, 16) & 65535
    value = value * 73244475
    value = value ^ jnp.right_shift(value, 16) & 65535
    return value


def sketch_table(base_value, feature_index, rank):
    counter = feature_index[:, None] * rank + jnp.arange(rank, dtype=jnp.int32)[None, :]
    offset = scramble(base_value)
    total = jnp.zeros(counter.shape, jnp.float32)
    for j in range(4):
        hashed = scramble(counter * 4 + j + offset)
        total = total + (hashed & 16777215).astype(jnp.float32) * (1.0 / 16777216.0)
    return ((total - 2.0) * 1.7320508).astype(jnp.bfloat16)


def terms_of(value):
    if value.dtype == jnp.bfloat16:
        return [value]
    high = value.astype(jnp.bfloat16)
    rest = value - high.astype(jnp.float32)
    middle = rest.astype(jnp.bfloat16)
    low = (rest - middle.astype(jnp.float32)).astype(jnp.bfloat16)
    return [high, middle, low]


def dot_nn(left, right):
    return lax.dot_general(
        left, right, (((1,), (0,)), ((), ())), preferred_element_type=jnp.float32
    )


def dot_nt(left, right):
    return lax.dot_general(
        left, right, (((1,), (1,)), ((), ())), preferred_element_type=jnp.float32
    )


def small_times_wide(small, right):
    left = terms_of(small)
    pairs = [(i, d - i) for d in (2, 1, 0) for i in range(d + 1)]
    pairs = [(i, j) for i, j in pairs if i < len(left) and j < len(right)]
    return dot_nn(
        jnp.concatenate([left[i] for i, unused in pairs], axis=1),
        jnp.concatenate([right[j] for unused, j in pairs], axis=0),
    )


def gram_of(terms):
    if len(terms) == 1:
        return dot_nt(terms[0], terms[0])
    rank = terms[0].shape[0]
    stacked = jnp.concatenate(terms, axis=0)
    both = dot_nt(stacked, stacked)
    cross = both[rank : 2 * rank, :rank] + both[2 * rank :, :rank]
    return both[:rank, :rank] + ((cross + cross.T) + both[rank : 2 * rank, rank : 2 * rank])


def eliminate(matrix, beside=()):
    beside = list(beside)
    size = matrix.shape[0]
    blocks = size // SUB
    row_index = lax.broadcasted_iota(jnp.int32, (SUB, 2 * size), 0)
    square_row = lax.broadcasted_iota(jnp.int32, (SUB, size), 0)
    square_col = lax.broadcasted_iota(jnp.int32, (SUB, size), 1)
    work = []
    for i in range(blocks):
        unit = jnp.where(square_col == square_row + SUB * i, 1.0, 0.0).astype(jnp.float32)
        work.append(jnp.concatenate([matrix[SUB * i : SUB * (i + 1), :], unit], axis=1))

    def fill(register, k):
        return jnp.broadcast_to(register[k : k + 1, :], (SUB, 2 * size))

    rows = []
    for b in range(blocks):
        for unused in range(-(-len(beside) // (blocks - b))):
            beside.pop(0)()
        columns = [
            {
                i: jnp.broadcast_to(work[i][:, SUB * b + j : SUB * b + j + 1], (SUB, 2 * size))
                for i in range(b, blocks)
            }
            for j in range(SUB)
        ]
        pivots = jnp.ones((SUB, 2 * size), jnp.float32)
        for k in range(0, SUB, 2):
            col_0, col_1 = columns[k], columns[k + 1]
            a, h, d = fill(col_0[b], k), fill(col_1[b], k), fill(col_1[b], k + 1)
            det = a * d - h * h
            over_det, over_a = 1.0 / det, 1.0 / a
            below_0 = jnp.where(row_index > k + 1, col_0[b], 0.0)
            below_1 = jnp.where(row_index > k + 1, col_1[b], 0.0)
            for j in range(k + 2, SUB):
                entry_0, entry_1 = fill(columns[j][b], k), fill(columns[j][b], k + 1)
                up_0 = d * entry_0 - h * entry_1
                up_1 = a * entry_1 - h * entry_0
                columns[j][b] = columns[j][b] - over_det * (below_0 * up_0 + below_1 * up_1)
                up_0, up_1 = over_det * up_0, over_det * up_1
                for i in range(b + 1, blocks):
                    columns[j][i] = columns[j][i] - (col_0[i] * up_0 + col_1[i] * up_1)
            row_0, row_1 = fill(work[b], k), fill(work[b], k + 1)
            up_0 = over_det * (d * row_0 - h * row_1)
            up_1 = over_det * (a * row_1 - h * row_0)
            for i in range(b + 1, blocks):
                work[i] = work[i] - (col_0[i] * up_0 + col_1[i] * up_1)
            second = jnp.where(row_index == k + 1, h * over_a, 0.0)
            work[b] = work[b] - (below_0 * up_0 + below_1 * up_1 + second * row_0)
            pivots = jnp.where(row_index == k, a, pivots)
            pivots = jnp.where(row_index == k + 1, det * over_a, pivots)
        rows.append(work[b] * lax.rsqrt(pivots))
    both = jnp.concatenate(rows, axis=0)
    keep = lax.broadcasted_iota(jnp.int32, (size, size), 1) >= lax.broadcasted_iota(
        jnp.int32, (size, size), 0
    )
    return jnp.where(keep, both[:, :size], 0.0), both[:, size:]


def shifted_factor(wide, terms):
    whole_gram = gram_of(terms)
    squares = wide.astype(jnp.float32)
    squares = jnp.sum(squares * squares, axis=0, keepdims=True)
    trace = jnp.sum(squares, axis=1, keepdims=True)
    size = whole_gram.shape[0]
    diagonal = lax.broadcasted_iota(jnp.int32, (size, size), 0) == lax.broadcasted_iota(
        jnp.int32, (size, size), 1
    )
    scaled = whole_gram * (1.0 / trace)
    upper, inverse = eliminate(jnp.where(diagonal, scaled + shift_ratio, scaled))
    root = jnp.sqrt(trace)
    return upper * root, inverse * (1.0 / root)


def wide_of(at_ref, z_refs):
    chunks = [z_ref[at_ref[i]] for z_ref in z_refs for i in range(at_ref.shape[0])]
    return jnp.concatenate(chunks, axis=1)


def first_pass(at_ref, z_refs):
    wide = wide_of(at_ref, z_refs)
    terms = terms_of(wide)
    upper, inverse_one = shifted_factor(wide, terms)
    return terms_of(small_times_wide(inverse_one, terms)), upper


def back_product(at_ref, z_refs, a):
    terms, unused = first_pass(at_ref, z_refs)
    rank = terms[0].shape[0]
    stacked = jnp.concatenate(terms, axis=0)
    tiles = []

    def tile(start):
        back = dot_nn(stacked, a[:, start : start + TILE])
        tiles.append(back[:rank] + (back[rank : 2 * rank] + back[2 * rank :]))

    starts = range(0, a.shape[1], TILE)
    work = [functools.partial(tile, start) for start in starts]
    unused, inverse_two = eliminate(gram_of(terms), work)
    return small_times_wide(inverse_two, terms_of(jnp.concatenate(tiles, axis=1)))


def store_parts(forth, at_ref, part_ref):
    chunks, unused, width = part_ref.shape
    for i in range(chunks):
        part_ref[at_ref[i]] = forth[:, width * i : width * (i + 1)]


def orth_kernel(at_ref, z_ref, other_ref, basis_ref, upper_ref):
    terms, upper = first_pass(at_ref, (z_ref, other_ref))
    unused, inverse_two = eliminate(gram_of(terms))
    basis_ref[...] = small_times_wide(inverse_two, terms).astype(jnp.bfloat16)
    upper_ref[...] = upper


def power_kernel(at_ref, basis_ref, *refs):
    piece_refs, a_ref, part_ref = refs[:-2], refs[-2], refs[-1]
    start = 0
    for piece_ref in piece_refs:
        a_ref[start : start + piece_ref.shape[0], :] = piece_ref[...]
        start += piece_ref.shape[0]
    weights = dot_nn(basis_ref[...], a_ref[...]).astype(jnp.bfloat16)
    forth = dot_nt(weights, a_ref[: part_ref.shape[0] * part_ref.shape[2], :])
    store_parts(forth, at_ref, part_ref)


def turn_kernel(a_ref, turned_ref):
    turned_ref[...] = a_ref[: turned_ref.shape[1], :].T


def orth_power_kernel(at_ref, z_ref, other_ref, a_ref, turned_ref, part_ref):
    weights = back_product(at_ref, (z_ref, other_ref), a_ref[...]).astype(jnp.bfloat16)
    store_parts(dot_nn(weights, turned_ref[...]), at_ref, part_ref)


def last_kernel(at_ref, core_ref, z_ref, other_ref, a_ref, out_ref):
    cols = out_ref.shape[1]
    start = pl.multiple_of(core_ref[0] * cols, cols)
    out_ref[...] = back_product(at_ref, (z_ref, other_ref), a_ref[:, pl.ds(start, cols)])


def call(kernel, out_shapes, flops, scalars, *operands):
    moved = sum(x.size * x.dtype.itemsize for x in operands)
    return pl.pallas_call(
        kernel,
        out_shape=out_shapes,
        in_specs=[pl.BlockSpec(memory_space=pltpu.SMEM)] * len(scalars)
        + [pl.BlockSpec(memory_space=pltpu.VMEM)] * len(operands),
        out_specs=jax.tree.map(lambda _: pl.BlockSpec(memory_space=pltpu.VMEM), out_shapes),
        compiler_params=pltpu.CompilerParams(vmem_limit_bytes=20 * 1024 * 1024),
        cost_estimate=pl.CostEstimate(flops=flops, bytes_accessed=moved, transcendentals=0),
    )(*scalars, *operands)


def bits(size):
    return [1 << k for k in range(size.bit_length() - 1)]


def from_xor(value, axis, offset):
    size = math.prod(lax.axis_size(name) for name in axis)
    return lax.ppermute(value, axis, [(i, i ^ offset) for i in range(size)])


def square_devices():
    n_z, n_col = lax.axis_size("z"), lax.axis_size("col")
    sides = [(z, col) for z in range(2 if n_z > 2 else 1) for col in range(n_col)]
    return [(z * n_col + col, col * (2 if n_z > 2 else 1) + z) for z, col in sides[1:]]


def sum_parts(total, dtype):
    offsets = square_devices()
    step = total.shape[0] // (len(offsets) + 1)
    others = [
        from_xor(total[step * place : step * (place + 1)].astype(dtype), ("z", "col"), offset)
        for offset, place in offsets
    ]
    total = functools.reduce(jnp.add, [x.astype(jnp.float32) for x in others], total[:step])
    for bit in far_bits():
        mine = total.astype(dtype)
        total = mine.astype(jnp.float32) + from_xor(mine, ("z",), bit).astype(jnp.float32)
    return total.astype(dtype)


def gather_parts(own):
    placed = {0: own}
    for offset, place in square_devices():
        placed[place] = from_xor(own, ("z", "col"), offset)
    own = jnp.concatenate([placed[place] for place in sorted(placed)])
    return own, from_xor(own, ("core",), 1)


def far_bits():
    return bits(lax.axis_size("z"))[1 if lax.axis_size("z") > 2 else 0 :]


def chunk_places(digits):
    n_z, n_col = lax.axis_size("z"), lax.axis_size("col")
    index = jnp.arange(n_z * n_col, dtype=jnp.int32)
    z_at, col_at = lax.axis_index("z"), lax.axis_index("col")
    column = index % n_col
    relative = {"z": index // n_col, "col": column ^ col_at}
    absolute = {"z": relative["z"] ^ z_at, "col": column}
    place = jnp.zeros_like(index)
    for axis, bit, is_relative in digits:
        place = place * 2 + ((relative if is_relative else absolute)[axis] // bit) % 2
    return place.astype(jnp.int32)


def per_device_transposed(sketch_base, states):
    n_z, n_core, n_col = lax.axis_size("z"), lax.axis_size("core"), lax.axis_size("col")
    n_row = n_z * n_core
    rows_local, width_local = states.shape
    rows_total, width_total = rows_local * n_row, width_local * n_col
    chunk = rows_local // n_col
    cols = width_local // n_z
    chunks = n_z * n_col
    z_at, col = lax.axis_index("z"), lax.axis_index("col")
    pieces = {}

    def block(offset, part=0, parts=1):
        rows = rows_local // parts
        start = (part * rows, (z_at ^ offset) * cols)
        return lax.dynamic_slice(states, start, (rows, cols))

    def move(blocks):
        for name, value in blocks.items():
            pieces[name] = from_xor(value, ("z",), name[0]) if name[0] else value

    def hold(value, names):
        value, moved = lax.optimization_barrier((value, [pieces[name] for name in names]))
        pieces.update(zip(names, moved))
        return value

    feature_index = col * width_local + jnp.arange(width_local, dtype=jnp.int32)
    omega = sketch_table(sketch_base[0], feature_index, RANK)
    z = lax.dot_general(
        omega, states, (((0,), (1,)), ((), ())), preferred_element_type=jnp.float32
    )
    z = z.reshape(RANK, n_col, chunk).transpose(1, 0, 2)
    z_bits = bits(n_z)[::-1]
    far = z_bits[0]
    move({(offset, 0): block(offset) for offset in [0, far, *range(1, far)]})
    first = list(pieces)
    late = {(o, part): block(o, part, 2) for o in range(far + 1, n_z) for part in range(2)}
    z = jnp.concatenate([z, from_xor(z, ("z",), far)])
    z, late = lax.optimization_barrier((z, late))
    move(late)
    for bit in bits(n_col):
        z = z + from_xor(z, ("col",), bit)
    z = hold(z, first)
    for bit in z_bits[1:]:
        z = jnp.concatenate([z, from_xor(z, ("z",), bit)])
    z = hold(z, [(offset, 0) for offset in range(far + 1, n_z)])
    z = z, from_xor(z, ("core",), 1)
    absolute_col = [("col", bit, False) for bit in bits(n_col)[::-1]]
    at_first = chunk_places([("z", bit, True) for bit in z_bits[::-1]] + absolute_col)
    digits = [("col", bit, True) for bit in bits(n_col)[::-1]]
    digits += [("z", 1, True)] if n_z > 2 else []
    at = chunk_places(digits + [("z", bit, False) for bit in far_bits()])
    late = list(late)
    others = {name: from_xor(pieces[name], ("core",), 1) for name in first}

    f32 = jnp.float32
    square = jax.ShapeDtypeStruct((RANK, RANK), f32)
    wide = jax.ShapeDtypeStruct((RANK, rows_total), jnp.bfloat16)
    slab = jax.ShapeDtypeStruct((rows_total, cols), states.dtype)
    parts = jax.ShapeDtypeStruct((chunks, RANK, chunk), f32)
    loadings = jax.ShapeDtypeStruct((RANK, cols // n_core), f32)
    orth_flops = 8 * 64 * 64 * rows_total * 6
    flops = orth_flops + 4 * 64 * rows_total * cols

    basis, upper = call(orth_kernel, (wide, square), orth_flops, (at_first,), *z)
    basis = hold(basis, late)
    others.update((name, from_xor(pieces[name], ("core",), 1)) for name in late)
    blocks = [half[name] for half in (pieces, others) for name in sorted(half)]
    factor = upper.T * (1.0 / math.sqrt(rows_total * width_total))
    a, total = call(power_kernel, (slab, parts), flops, (at,), basis, *blocks)
    turned = jax.ShapeDtypeStruct((cols, rows_total // n_core), states.dtype)
    turned = call(turn_kernel, turned, flops, (), a)
    share, turned = lax.optimization_barrier((sum_parts(total, f32), turned))
    z = gather_parts(share)
    for step in range(POWER - 1):
        total = call(orth_power_kernel, parts, flops, (at,), *z, a, turned)
        z = gather_parts(sum_parts(total, jnp.bfloat16))
    core = lax.axis_index("core")[None].astype(jnp.int32)
    return call(last_kernel, loadings, flops, (at, core), *z, a).T, factor


def local_gram(basis):
    return jnp.dot(basis.T, basis, precision=lax.Precision.HIGHEST)


def orthonormal_block(sketch):
    whole_gram = lax.psum(local_gram(sketch), "row")
    identity = jnp.eye(RANK, dtype=jnp.float32)
    lower = jnp.linalg.cholesky(whole_gram + shift_ratio * jnp.trace(whole_gram) * identity)
    first = jax.scipy.linalg.solve_triangular(lower, sketch.T, lower=True).T
    lower_two = jnp.linalg.cholesky(lax.psum(local_gram(first), "row"))
    return jax.scipy.linalg.solve_triangular(lower_two, first.T, lower=True).T, lower


def per_device_slabs(sketch_base, states):
    width_local = states.shape[1]
    rows_total = states.shape[0] * lax.axis_size("row")
    width_total = width_local * lax.axis_size("col")
    feature_index = lax.axis_index("col") * width_local + jnp.arange(width_local, dtype=jnp.int32)
    omega = sketch_table(sketch_base[0], feature_index, RANK)

    def row_basis(right):
        partial_sketch = jnp.dot(states, right, preferred_element_type=jnp.float32)
        basis_new, lower = orthonormal_block(lax.psum(partial_sketch, "col"))
        return basis_new.astype(jnp.bfloat16), lower

    def back(basis):
        return lax.dot_general(
            states, basis, (((0,), (0,)), ((), ())), preferred_element_type=jnp.float32
        )

    basis, first_lower = row_basis(omega)
    factor = first_lower * (1.0 / math.sqrt(rows_total * width_total))
    for step in range(POWER):
        basis, unused = row_basis(lax.psum(back(basis), "row").astype(jnp.bfloat16))
    return lax.psum_scatter(back(basis), "row", scatter_dimension=0, tiled=True), factor


def solution(mesh):
    n_grp, n_row, n_col = (mesh.shape[name] for name in ("grp", "row", "col"))
    fits = n_row >= 4 and n_row & (n_row - 1) == 0 and n_col & (n_col - 1) == 0

    def run(sketch_base, states):
        rows_local = states.shape[0] // (n_grp * n_row)
        width_local = states.shape[1] // n_col
        tiled = rows_local % (n_col * LANES) == 0 and width_local % (n_row * LANES) == 0
        if fits and tiled:
            split = mesh.devices.reshape(n_grp, n_row // 2, 2, n_col)
            inner = jax.sharding.Mesh(split, ("grp", "z", "core", "col"))
            row, step = ("z", "core"), per_device_transposed
        else:
            inner, row, step = mesh, ("row",), per_device_slabs
        return jax.shard_map(
            step,
            mesh=inner,
            in_specs=(P("grp"), P(("grp",) + row, "col")),
            out_specs=(P(("col",) + row, "grp"), P("grp", None)),
            check_vma=False,
        )(sketch_base, states)

    return run
```

```python
import functools
import math

import jax
import jax.numpy as jnp
from jax import lax
from jax.experimental import pallas as pl
from jax.experimental.pallas import tpu as pltpu
from jax.sharding import PartitionSpec as P

RANK = 64
POWER = 4
LANES = 128
SUB = 8
TILE = 256
ROW_TILE = 512


shift_ratio = 0.005


def scramble(value):
    value = value ^ jnp.right_shift(value, 16) & 65535
    value = value * 73244475
    value = value ^ jnp.right_shift(value, 16) & 65535
    value = value * 73244475
    value = value ^ jnp.right_shift(value, 16) & 65535
    return value


def sketch_table(base_value, feature_index, rank):
    counter = feature_index[:, None] * rank + jnp.arange(rank, dtype=jnp.int32)[None, :]
    offset = scramble(base_value)
    total = jnp.zeros(counter.shape, jnp.float32)
    for j in range(4):
        hashed = scramble(counter * 4 + j + offset)
        total = total + (hashed & 16777215).astype(jnp.float32) * (1.0 / 16777216.0)
    return ((total - 2.0) * 1.7320508).astype(jnp.bfloat16)


def terms_of(value):
    if value.dtype == jnp.bfloat16:
        return [value]
    high = value.astype(jnp.bfloat16)
    rest = value - high.astype(jnp.float32)
    middle = rest.astype(jnp.bfloat16)
    low = (rest - middle.astype(jnp.float32)).astype(jnp.bfloat16)
    return [high, middle, low]


def dot_nn(left, right):
    return lax.dot_general(
        left, right, (((1,), (0,)), ((), ())), preferred_element_type=jnp.float32
    )


def dot_nt(left, right):
    return lax.dot_general(
        left, right, (((1,), (1,)), ((), ())), preferred_element_type=jnp.float32
    )


def small_times_wide(small, right):
    left = terms_of(small)
    pairs = [(i, d - i) for d in (2, 1, 0) for i in range(d + 1)]
    pairs = [(i, j) for i, j in pairs if i < len(left) and j < len(right)]
    return dot_nn(
        jnp.concatenate([left[i] for i, unused in pairs], axis=1),
        jnp.concatenate([right[j] for unused, j in pairs], axis=0),
    )


def gram_of(terms):
    if len(terms) == 1:
        return dot_nt(terms[0], terms[0])
    stacked = jnp.concatenate(terms, axis=0)
    return fold_gram(dot_nt(stacked, stacked))


def fold_gram(both):
    rank = both.shape[0] // 3
    cross = both[rank : 2 * rank, :rank] + both[2 * rank :, :rank]
    return both[:rank, :rank] + ((cross + cross.T) + both[rank : 2 * rank, rank : 2 * rank])


def eliminate(matrix, beside=()):
    beside = list(beside)
    size = matrix.shape[0]
    blocks = size // SUB
    row_index = lax.broadcasted_iota(jnp.int32, (SUB, 2 * size), 0)
    square_row = lax.broadcasted_iota(jnp.int32, (SUB, size), 0)
    square_col = lax.broadcasted_iota(jnp.int32, (SUB, size), 1)
    work = []
    for i in range(blocks):
        unit = jnp.where(square_col == square_row + SUB * i, 1.0, 0.0).astype(jnp.float32)
        work.append(jnp.concatenate([matrix[SUB * i : SUB * (i + 1), :], unit], axis=1))

    def fill(register, k):
        return jnp.broadcast_to(register[k : k + 1, :], (SUB, 2 * size))

    rows = []
    for b in range(blocks):
        for unused in range(-(-len(beside) // (blocks - b))):
            beside.pop(0)()
        columns = [
            {
                i: jnp.broadcast_to(work[i][:, SUB * b + j : SUB * b + j + 1], (SUB, 2 * size))
                for i in range(b, blocks)
            }
            for j in range(SUB)
        ]
        pivots = jnp.ones((SUB, 2 * size), jnp.float32)
        for k in range(0, SUB, 2):
            col_0, col_1 = columns[k], columns[k + 1]
            a, h, d = fill(col_0[b], k), fill(col_1[b], k), fill(col_1[b], k + 1)
            det = a * d - h * h
            over_det, over_a = 1.0 / det, 1.0 / a
            below_0 = jnp.where(row_index > k + 1, col_0[b], 0.0)
            below_1 = jnp.where(row_index > k + 1, col_1[b], 0.0)
            for j in range(k + 2, SUB):
                entry_0, entry_1 = fill(columns[j][b], k), fill(columns[j][b], k + 1)
                up_0 = d * entry_0 - h * entry_1
                up_1 = a * entry_1 - h * entry_0
                columns[j][b] = columns[j][b] - over_det * (below_0 * up_0 + below_1 * up_1)
                up_0, up_1 = over_det * up_0, over_det * up_1
                for i in range(b + 1, blocks):
                    columns[j][i] = columns[j][i] - (col_0[i] * up_0 + col_1[i] * up_1)
            row_0, row_1 = fill(work[b], k), fill(work[b], k + 1)
            up_0 = over_det * (d * row_0 - h * row_1)
            up_1 = over_det * (a * row_1 - h * row_0)
            for i in range(b + 1, blocks):
                work[i] = work[i] - (col_0[i] * up_0 + col_1[i] * up_1)
            second = jnp.where(row_index == k + 1, h * over_a, 0.0)
            work[b] = work[b] - (below_0 * up_0 + below_1 * up_1 + second * row_0)
            pivots = jnp.where(row_index == k, a, pivots)
            pivots = jnp.where(row_index == k + 1, det * over_a, pivots)
        rows.append(work[b] * lax.rsqrt(pivots))
    both = jnp.concatenate(rows, axis=0)
    keep = lax.broadcasted_iota(jnp.int32, (size, size), 1) >= lax.broadcasted_iota(
        jnp.int32, (size, size), 0
    )
    return jnp.where(keep, both[:, :size], 0.0), both[:, size:]


def shifted_factor(wide, terms):
    whole_gram = gram_of(terms)
    squares = wide.astype(jnp.float32)
    squares = jnp.sum(squares * squares, axis=0, keepdims=True)
    trace = jnp.sum(squares, axis=1, keepdims=True)
    size = whole_gram.shape[0]
    diagonal = lax.broadcasted_iota(jnp.int32, (size, size), 0) == lax.broadcasted_iota(
        jnp.int32, (size, size), 1
    )
    scaled = whole_gram * (1.0 / trace)
    upper, inverse = eliminate(jnp.where(diagonal, scaled + shift_ratio, scaled))
    root = jnp.sqrt(trace)
    return upper * root, inverse * (1.0 / root)


def wide_of(at_ref, z_refs):
    chunks = [z_ref[at_ref[i]] for z_ref in z_refs for i in range(at_ref.shape[0])]
    return jnp.concatenate(chunks, axis=1)


def first_pass(at_ref, z_refs):
    wide = wide_of(at_ref, z_refs)
    terms = terms_of(wide)
    upper, inverse_one = shifted_factor(wide, terms)
    tiles, both = [], 0.0
    for start in range(0, wide.shape[1], ROW_TILE):
        part = small_times_wide(inverse_one, [term[:, start : start + ROW_TILE] for term in terms])
        tiles.append(jnp.concatenate(terms_of(part), axis=0))
        both = both + dot_nt(tiles[-1], tiles[-1])
    return jnp.concatenate(tiles, axis=1), fold_gram(both), upper


def back_product(at_ref, z_refs, a):
    stacked, gram, unused = first_pass(at_ref, z_refs)
    rank = gram.shape[0]
    tiles = []

    def tile(start):
        back = dot_nn(stacked, a[:, start : start + TILE])
        tiles.append(back[:rank] + (back[rank : 2 * rank] + back[2 * rank :]))

    starts = range(0, a.shape[1], TILE)
    work = [functools.partial(tile, start) for start in starts]
    unused, inverse_two = eliminate(gram, work)
    return small_times_wide(inverse_two, terms_of(jnp.concatenate(tiles, axis=1)))


def store_parts(forth, at_ref, part_ref):
    chunks, unused, width = part_ref.shape
    for i in range(chunks):
        part_ref[at_ref[i]] = forth[:, width * i : width * (i + 1)]


def orth_kernel(at_ref, z_ref, other_ref, basis_ref, upper_ref):
    stacked, gram, upper = first_pass(at_ref, (z_ref, other_ref))
    unused, inverse_two = eliminate(gram)
    rank = gram.shape[0]
    terms = [stacked[rank * i : rank * (i + 1)] for i in range(3)]
    basis_ref[...] = small_times_wide(inverse_two, terms).astype(jnp.bfloat16)
    upper_ref[...] = upper


def power_kernel(at_ref, basis_ref, *refs):
    piece_refs, a_ref, part_ref = refs[:-2], refs[-2], refs[-1]
    start = 0
    for piece_ref in piece_refs:
        a_ref[start : start + piece_ref.shape[0], :] = piece_ref[...]
        start += piece_ref.shape[0]
    weights = dot_nn(basis_ref[...], a_ref[...]).astype(jnp.bfloat16)
    forth = dot_nt(weights, a_ref[: part_ref.shape[0] * part_ref.shape[2], :])
    store_parts(forth, at_ref, part_ref)


def turn_kernel(a_ref, turned_ref):
    turned_ref[...] = a_ref[: turned_ref.shape[1], :].T


def orth_power_kernel(at_ref, z_ref, other_ref, a_ref, turned_ref, part_ref):
    weights = back_product(at_ref, (z_ref, other_ref), a_ref[...]).astype(jnp.bfloat16)
    store_parts(dot_nn(weights, turned_ref[...]), at_ref, part_ref)


def last_kernel(at_ref, core_ref, z_ref, other_ref, a_ref, out_ref):
    cols = out_ref.shape[1]
    start = pl.multiple_of(core_ref[0] * cols, cols)
    out_ref[...] = back_product(at_ref, (z_ref, other_ref), a_ref[:, pl.ds(start, cols)])


def call(kernel, out_shapes, flops, scalars, *operands):
    moved = sum(x.size * x.dtype.itemsize for x in operands)
    return pl.pallas_call(
        kernel,
        out_shape=out_shapes,
        in_specs=[pl.BlockSpec(memory_space=pltpu.SMEM)] * len(scalars)
        + [pl.BlockSpec(memory_space=pltpu.VMEM)] * len(operands),
        out_specs=jax.tree.map(lambda _: pl.BlockSpec(memory_space=pltpu.VMEM), out_shapes),
        compiler_params=pltpu.CompilerParams(vmem_limit_bytes=20 * 1024 * 1024),
        cost_estimate=pl.CostEstimate(flops=flops, bytes_accessed=moved, transcendentals=0),
    )(*scalars, *operands)


def bits(size):
    return [1 << k for k in range(size.bit_length() - 1)]


def from_xor(value, axis, offset):
    size = math.prod(lax.axis_size(name) for name in axis)
    return lax.ppermute(value, axis, [(i, i ^ offset) for i in range(size)])


def square_devices():
    n_z, n_col = lax.axis_size("z"), lax.axis_size("col")
    sides = [(z, col) for z in range(2 if n_z > 2 else 1) for col in range(n_col)]
    return [(z * n_col + col, col * (2 if n_z > 2 else 1) + z) for z, col in sides[:0:-1]]


def sum_parts(total, dtype):
    offsets = square_devices()
    step = total.shape[0] // (len(offsets) + 1)
    others = [
        from_xor(total[step * place : step * (place + 1)].astype(dtype), ("z", "col"), offset)
        for offset, place in offsets
    ]
    total = functools.reduce(jnp.add, [x.astype(jnp.float32) for x in others], total[:step])
    for bit in far_bits():
        mine = total.astype(dtype)
        total = mine.astype(jnp.float32) + from_xor(mine, ("z",), bit).astype(jnp.float32)
    return total.astype(dtype)


def gather_parts(own):
    placed = {0: own}
    for offset, place in square_devices():
        placed[place] = from_xor(own, ("z", "col"), offset)
    own = jnp.concatenate([placed[place] for place in sorted(placed)])
    return own, from_xor(own, ("core",), 1)


def far_bits():
    return bits(lax.axis_size("z"))[1 if lax.axis_size("z") > 2 else 0 :]


def chunk_places(digits):
    n_z, n_col = lax.axis_size("z"), lax.axis_size("col")
    index = jnp.arange(n_z * n_col, dtype=jnp.int32)
    z_at, col_at = lax.axis_index("z"), lax.axis_index("col")
    column = index % n_col
    relative = {"z": index // n_col, "col": column ^ col_at}
    absolute = {"z": relative["z"] ^ z_at, "col": column}
    place = jnp.zeros_like(index)
    for axis, bit, is_relative in digits:
        place = place * 2 + ((relative if is_relative else absolute)[axis] // bit) % 2
    return place.astype(jnp.int32)


def per_device_transposed(sketch_base, states):
    n_z, n_core, n_col = lax.axis_size("z"), lax.axis_size("core"), lax.axis_size("col")
    n_row = n_z * n_core
    rows_local, width_local = states.shape
    rows_total, width_total = rows_local * n_row, width_local * n_col
    chunk = rows_local // n_col
    cols = width_local // n_z
    chunks = n_z * n_col
    z_at, col = lax.axis_index("z"), lax.axis_index("col")
    pieces = {}

    def block(offset, part=0, parts=1):
        rows = rows_local // parts
        start = (part * rows, (z_at ^ offset) * cols)
        return lax.dynamic_slice(states, start, (rows, cols))

    def move(blocks):
        for name, value in blocks.items():
            pieces[name] = from_xor(value, ("z",), name[0]) if name[0] else value

    def hold(value, names):
        value, moved = lax.optimization_barrier((value, [pieces[name] for name in names]))
        pieces.update(zip(names, moved))
        return value

    feature_index = col * width_local + jnp.arange(width_local, dtype=jnp.int32)
    omega = sketch_table(sketch_base[0], feature_index, RANK)
    z = lax.dot_general(
        omega, states, (((0,), (1,)), ((), ())), preferred_element_type=jnp.float32
    )
    z = z.reshape(RANK, n_col, chunk).transpose(1, 0, 2)
    z_bits = bits(n_z)[::-1]
    far = z_bits[0]
    move({(offset, 0): block(offset) for offset in [0, far, *range(1, far)]})
    first = list(pieces)
    late = {(o, part): block(o, part, 2) for o in range(far + 1, n_z) for part in range(2)}
    z = jnp.concatenate([z, from_xor(z, ("z",), far)])
    z, late = lax.optimization_barrier((z, late))
    move(late)
    for bit in bits(n_col):
        z = z + from_xor(z, ("col",), bit)
    z = hold(z, first)
    for bit in z_bits[1:]:
        z = jnp.concatenate([z, from_xor(z, ("z",), bit)])
    z = hold(z, [(offset, 0) for offset in range(far + 1, n_z)])
    z = z, from_xor(z, ("core",), 1)
    absolute_col = [("col", bit, False) for bit in bits(n_col)[::-1]]
    at_first = chunk_places([("z", bit, True) for bit in z_bits[::-1]] + absolute_col)
    digits = [("col", bit, True) for bit in bits(n_col)[::-1]]
    digits += [("z", 1, True)] if n_z > 2 else []
    at = chunk_places(digits + [("z", bit, False) for bit in far_bits()])
    late = list(late)
    others = {name: from_xor(pieces[name], ("core",), 1) for name in first}

    f32 = jnp.float32
    square = jax.ShapeDtypeStruct((RANK, RANK), f32)
    wide = jax.ShapeDtypeStruct((RANK, rows_total), jnp.bfloat16)
    slab = jax.ShapeDtypeStruct((rows_total, cols), states.dtype)
    parts = jax.ShapeDtypeStruct((chunks, RANK, chunk), f32)
    loadings = jax.ShapeDtypeStruct((RANK, cols // n_core), f32)
    orth_flops = 8 * 64 * 64 * rows_total * 6
    flops = orth_flops + 4 * 64 * rows_total * cols

    basis, upper = call(orth_kernel, (wide, square), orth_flops, (at_first,), *z)
    basis = hold(basis, late)
    others.update((name, from_xor(pieces[name], ("core",), 1)) for name in late)
    blocks = [half[name] for half in (pieces, others) for name in sorted(half)]
    factor = upper.T * (1.0 / math.sqrt(rows_total * width_total))
    a, total = call(power_kernel, (slab, parts), flops, (at,), basis, *blocks)
    turned = jax.ShapeDtypeStruct((cols, rows_total // n_core), states.dtype)
    turned = call(turn_kernel, turned, flops, (), a)
    share, turned = lax.optimization_barrier((sum_parts(total, f32), turned))
    z = gather_parts(share)
    for step in range(POWER - 1):
        total = call(orth_power_kernel, parts, flops, (at,), *z, a, turned)
        z = gather_parts(sum_parts(total, jnp.bfloat16))
    core = lax.axis_index("core")[None].astype(jnp.int32)
    return call(last_kernel, loadings, flops, (at, core), *z, a).T, factor


def local_gram(basis):
    return jnp.dot(basis.T, basis, precision=lax.Precision.HIGHEST)


def orthonormal_block(sketch):
    whole_gram = lax.psum(local_gram(sketch), "row")
    identity = jnp.eye(RANK, dtype=jnp.float32)
    lower = jnp.linalg.cholesky(whole_gram + shift_ratio * jnp.trace(whole_gram) * identity)
    first = jax.scipy.linalg.solve_triangular(lower, sketch.T, lower=True).T
    lower_two = jnp.linalg.cholesky(lax.psum(local_gram(first), "row"))
    return jax.scipy.linalg.solve_triangular(lower_two, first.T, lower=True).T, lower


def per_device_slabs(sketch_base, states):
    width_local = states.shape[1]
    rows_total = states.shape[0] * lax.axis_size("row")
    width_total = width_local * lax.axis_size("col")
    feature_index = lax.axis_index("col") * width_local + jnp.arange(width_local, dtype=jnp.int32)
    omega = sketch_table(sketch_base[0], feature_index, RANK)

    def row_basis(right):
        partial_sketch = jnp.dot(states, right, preferred_element_type=jnp.float32)
        basis_new, lower = orthonormal_block(lax.psum(partial_sketch, "col"))
        return basis_new.astype(jnp.bfloat16), lower

    def back(basis):
        return lax.dot_general(
            states, basis, (((0,), (0,)), ((), ())), preferred_element_type=jnp.float32
        )

    basis, first_lower = row_basis(omega)
    factor = first_lower * (1.0 / math.sqrt(rows_total * width_total))
    for step in range(POWER):
        basis, unused = row_basis(lax.psum(back(basis), "row").astype(jnp.bfloat16))
    return lax.psum_scatter(back(basis), "row", scatter_dimension=0, tiled=True), factor


def solution(mesh):
    n_grp, n_row, n_col = (mesh.shape[name] for name in ("grp", "row", "col"))
    fits = n_row >= 4 and n_row & (n_row - 1) == 0 and n_col & (n_col - 1) == 0

    def run(sketch_base, states):
        rows_local = states.shape[0] // (n_grp * n_row)
        width_local = states.shape[1] // n_col
        tiled = rows_local % (n_col * LANES) == 0 and width_local % (n_row * LANES) == 0
        if fits and tiled:
            split = mesh.devices.reshape(n_grp, n_row // 2, 2, n_col)
            inner = jax.sharding.Mesh(split, ("grp", "z", "core", "col"))
            row, step = ("z", "core"), per_device_transposed
        else:
            inner, row, step = mesh, ("row",), per_device_slabs
        return jax.shard_map(
            step,
            mesh=inner,
            in_specs=(P("grp"), P(("grp",) + row, "col")),
            out_specs=(P(("col",) + row, "grp"), P("grp", None)),
            check_vma=False,
        )(sketch_base, states)

    return run
```

```python
import functools
import math

import jax
import jax.numpy as jnp
from jax import lax
from jax.experimental import pallas as pl
from jax.experimental.pallas import tpu as pltpu
from jax.sharding import PartitionSpec as P

RANK = 64
POWER = 4
LANES = 128
SUB = 8
TILE = 256


shift_ratio = 0.005


def scramble(value):
    value = value ^ jnp.right_shift(value, 16) & 65535
    value = value * 73244475
    value = value ^ jnp.right_shift(value, 16) & 65535
    value = value * 73244475
    value = value ^ jnp.right_shift(value, 16) & 65535
    return value


def sketch_table(base_value, feature_index, rank):
    counter = feature_index[:, None] * rank + jnp.arange(rank, dtype=jnp.int32)[None, :]
    offset = scramble(base_value)
    total = jnp.zeros(counter.shape, jnp.float32)
    for j in range(4):
        hashed = scramble(counter * 4 + j + offset)
        total = total + (hashed & 16777215).astype(jnp.float32) * (1.0 / 16777216.0)
    return ((total - 2.0) * 1.7320508).astype(jnp.bfloat16)


def terms_of(value):
    if value.dtype == jnp.bfloat16:
        return [value]
    high = value.astype(jnp.bfloat16)
    rest = value - high.astype(jnp.float32)
    middle = rest.astype(jnp.bfloat16)
    low = (rest - middle.astype(jnp.float32)).astype(jnp.bfloat16)
    return [high, middle, low]


def dot_nn(left, right):
    return lax.dot_general(
        left, right, (((1,), (0,)), ((), ())), preferred_element_type=jnp.float32
    )


def dot_nt(left, right):
    return lax.dot_general(
        left, right, (((1,), (1,)), ((), ())), preferred_element_type=jnp.float32
    )


def small_times_wide(small, wide):
    left, right = terms_of(small), terms_of(wide)
    pairs = [(i, d - i) for d in (2, 1, 0) for i in range(d + 1)]
    pairs = [(i, j) for i, j in pairs if i < len(left) and j < len(right)]
    return dot_nn(
        jnp.concatenate([left[i] for i, unused in pairs], axis=1),
        jnp.concatenate([right[j] for unused, j in pairs], axis=0),
    )


def gram_of(wide):
    terms = terms_of(wide)
    if len(terms) == 1:
        return dot_nt(terms[0], terms[0])
    rank = wide.shape[0]
    stacked = jnp.concatenate(terms, axis=0)
    both = dot_nt(stacked, stacked)
    cross = both[rank : 2 * rank, :rank] + both[2 * rank :, :rank]
    return both[:rank, :rank] + ((cross + cross.T) + both[rank : 2 * rank, rank : 2 * rank])


def eliminate(matrix, beside=()):
    share = len(beside) / (matrix.shape[0] // SUB)
    size = matrix.shape[0]
    blocks = size // SUB
    row_index = lax.broadcasted_iota(jnp.int32, (SUB, 2 * size), 0)
    square_row = lax.broadcasted_iota(jnp.int32, (SUB, size), 0)
    square_col = lax.broadcasted_iota(jnp.int32, (SUB, size), 1)
    work = []
    for i in range(blocks):
        unit = jnp.where(square_col == square_row + SUB * i, 1.0, 0.0).astype(jnp.float32)
        work.append(jnp.concatenate([matrix[SUB * i : SUB * (i + 1), :], unit], axis=1))

    def fill(register, k):
        return jnp.broadcast_to(register[k : k + 1, :], (SUB, 2 * size))

    rows = []
    for b in range(blocks):
        for extra in beside[math.ceil(b * share) : math.ceil((b + 1) * share)]:
            extra()
        columns = [
            {
                i: jnp.broadcast_to(work[i][:, SUB * b + j : SUB * b + j + 1], (SUB, 2 * size))
                for i in range(b, blocks)
            }
            for j in range(SUB)
        ]
        pivots = jnp.ones((SUB, 2 * size), jnp.float32)
        for k in range(0, SUB, 2):
            col_0, col_1 = columns[k], columns[k + 1]
            a, h, d = fill(col_0[b], k), fill(col_1[b], k), fill(col_1[b], k + 1)
            det = a * d - h * h
            over_det, over_a = 1.0 / det, 1.0 / a
            below_0 = jnp.where(row_index > k + 1, col_0[b], 0.0)
            below_1 = jnp.where(row_index > k + 1, col_1[b], 0.0)
            for j in range(k + 2, SUB):
                entry_0, entry_1 = fill(columns[j][b], k), fill(columns[j][b], k + 1)
                up_0 = d * entry_0 - h * entry_1
                up_1 = a * entry_1 - h * entry_0
                columns[j][b] = columns[j][b] - over_det * (below_0 * up_0 + below_1 * up_1)
                up_0, up_1 = over_det * up_0, over_det * up_1
                for i in range(b + 1, blocks):
                    columns[j][i] = columns[j][i] - (col_0[i] * up_0 + col_1[i] * up_1)
            row_0, row_1 = fill(work[b], k), fill(work[b], k + 1)
            up_0 = over_det * (d * row_0 - h * row_1)
            up_1 = over_det * (a * row_1 - h * row_0)
            for i in range(b + 1, blocks):
                work[i] = work[i] - (col_0[i] * up_0 + col_1[i] * up_1)
            second = jnp.where(row_index == k + 1, h * over_a, 0.0)
            work[b] = work[b] - (below_0 * up_0 + below_1 * up_1 + second * row_0)
            pivots = jnp.where(row_index == k, a, pivots)
            pivots = jnp.where(row_index == k + 1, det * over_a, pivots)
        rows.append(work[b] * lax.rsqrt(pivots))
    both = jnp.concatenate(rows, axis=0)
    keep = lax.broadcasted_iota(jnp.int32, (size, size), 1) >= lax.broadcasted_iota(
        jnp.int32, (size, size), 0
    )
    return jnp.where(keep, both[:, :size], 0.0), both[:, size:]


def shifted_factor(wide):
    whole_gram = gram_of(wide)
    squares = wide.astype(jnp.float32)
    squares = jnp.sum(squares * squares, axis=0, keepdims=True)
    trace = jnp.sum(squares, axis=1, keepdims=True)
    size = whole_gram.shape[0]
    diagonal = lax.broadcasted_iota(jnp.int32, (size, size), 0) == lax.broadcasted_iota(
        jnp.int32, (size, size), 1
    )
    scaled = whole_gram * (1.0 / trace)
    upper, inverse = eliminate(jnp.where(diagonal, scaled + shift_ratio, scaled))
    root = jnp.sqrt(trace)
    return upper * root, inverse * (1.0 / root)


def wide_of(at_ref, z_refs):
    chunks = [z_ref[at_ref[i]] for z_ref in z_refs for i in range(at_ref.shape[0])]
    return jnp.concatenate(chunks, axis=1)


def first_pass(at_ref, z_refs):
    wide = wide_of(at_ref, z_refs)
    upper, inverse_one = shifted_factor(wide)
    return small_times_wide(inverse_one, wide), upper


def back_product(at_ref, z_refs, a):
    first, unused = first_pass(at_ref, z_refs)
    rank = first.shape[0]
    terms = jnp.concatenate(terms_of(first), axis=0)
    tiles = []

    def tile(start):
        back = dot_nn(terms, a[:, start : start + TILE])
        tiles.append(back[:rank] + (back[rank : 2 * rank] + back[2 * rank :]))

    starts = range(0, a.shape[1], TILE)
    work = [functools.partial(tile, start) for start in starts]
    unused, inverse_two = eliminate(gram_of(first), work)
    return small_times_wide(inverse_two, jnp.concatenate(tiles, axis=1))


def store_parts(forth, at_ref, part_ref):
    chunks, unused, width = part_ref.shape
    for i in range(chunks):
        part_ref[at_ref[i]] = forth[:, width * i : width * (i + 1)]


def orth_kernel(at_ref, z_ref, other_ref, basis_ref, upper_ref):
    first, upper = first_pass(at_ref, (z_ref, other_ref))
    unused, inverse_two = eliminate(gram_of(first))
    basis_ref[...] = small_times_wide(inverse_two, first).astype(jnp.bfloat16)
    upper_ref[...] = upper


def power_kernel(at_ref, basis_ref, *refs):
    piece_refs, a_ref, part_ref = refs[:-2], refs[-2], refs[-1]
    start = 0
    for piece_ref in piece_refs:
        a_ref[start : start + piece_ref.shape[0], :] = piece_ref[...]
        start += piece_ref.shape[0]
    weights = dot_nn(basis_ref[...], a_ref[...]).astype(jnp.bfloat16)
    forth = dot_nt(weights, a_ref[: part_ref.shape[0] * part_ref.shape[2], :])
    store_parts(forth, at_ref, part_ref)


def turn_kernel(a_ref, turned_ref):
    turned_ref[...] = a_ref[: turned_ref.shape[1], :].T


def orth_power_kernel(at_ref, z_ref, other_ref, a_ref, turned_ref, part_ref):
    weights = back_product(at_ref, (z_ref, other_ref), a_ref[...]).astype(jnp.bfloat16)
    store_parts(dot_nn(weights, turned_ref[...]), at_ref, part_ref)


def last_kernel(at_ref, core_ref, z_ref, other_ref, a_ref, out_ref):
    cols = out_ref.shape[1]
    start = pl.multiple_of(core_ref[0] * cols, cols)
    out_ref[...] = back_product(at_ref, (z_ref, other_ref), a_ref[:, pl.ds(start, cols)])


def call(kernel, out_shapes, flops, scalars, *operands):
    moved = sum(x.size * x.dtype.itemsize for x in operands)
    return pl.pallas_call(
        kernel,
        out_shape=out_shapes,
        in_specs=[pl.BlockSpec(memory_space=pltpu.SMEM)] * len(scalars)
        + [pl.BlockSpec(memory_space=pltpu.VMEM)] * len(operands),
        out_specs=jax.tree.map(lambda _: pl.BlockSpec(memory_space=pltpu.VMEM), out_shapes),
        compiler_params=pltpu.CompilerParams(vmem_limit_bytes=20 * 1024 * 1024),
        cost_estimate=pl.CostEstimate(flops=flops, bytes_accessed=moved, transcendentals=0),
    )(*scalars, *operands)


def bits(size):
    return [1 << k for k in range(size.bit_length() - 1)]


def from_xor(value, axis, offset):
    size = math.prod(lax.axis_size(name) for name in axis)
    return lax.ppermute(value, axis, [(i, i ^ offset) for i in range(size)])


def square_devices():
    n_z, n_col = lax.axis_size("z"), lax.axis_size("col")
    sides = [(z, col) for z in range(2 if n_z > 2 else 1) for col in range(n_col)]
    return [(z * n_col + col, col * (2 if n_z > 2 else 1) + z) for z, col in sides[:0:-1]]


def sum_parts(total, dtype):
    offsets = square_devices()
    step = total.shape[0] // (len(offsets) + 1)
    others = [
        from_xor(total[step * place : step * (place + 1)].astype(dtype), ("z", "col"), offset)
        for offset, place in offsets
    ]
    total = functools.reduce(jnp.add, [x.astype(jnp.float32) for x in others], total[:step])
    for bit in far_bits():
        mine = total.astype(dtype)
        total = mine.astype(jnp.float32) + from_xor(mine, ("z",), bit).astype(jnp.float32)
    return total.astype(dtype)


def gather_parts(own):
    placed = {0: own}
    for offset, place in square_devices():
        placed[place] = from_xor(own, ("z", "col"), offset)
    own = jnp.concatenate([placed[place] for place in sorted(placed)])
    return own, from_xor(own, ("core",), 1)


def far_bits():
    return bits(lax.axis_size("z"))[1 if lax.axis_size("z") > 2 else 0 :]


def chunk_places(digits):
    n_z, n_col = lax.axis_size("z"), lax.axis_size("col")
    index = jnp.arange(n_z * n_col, dtype=jnp.int32)
    z_at, col_at = lax.axis_index("z"), lax.axis_index("col")
    column = index % n_col
    relative = {"z": index // n_col, "col": column ^ col_at}
    absolute = {"z": relative["z"] ^ z_at, "col": column}
    place = jnp.zeros_like(index)
    for axis, bit, is_relative in digits:
        place = place * 2 + ((relative if is_relative else absolute)[axis] // bit) % 2
    return place.astype(jnp.int32)


def per_device_transposed(sketch_base, states):
    n_z, n_core, n_col = lax.axis_size("z"), lax.axis_size("core"), lax.axis_size("col")
    n_row = n_z * n_core
    rows_local, width_local = states.shape
    rows_total, width_total = rows_local * n_row, width_local * n_col
    chunk = rows_local // n_col
    cols = width_local // n_z
    chunks = n_z * n_col
    z_at, col = lax.axis_index("z"), lax.axis_index("col")
    pieces = {}

    def block(offset, part=0, parts=1):
        rows = rows_local // parts
        start = (part * rows, (z_at ^ offset) * cols)
        return lax.dynamic_slice(states, start, (rows, cols))

    def move(blocks):
        for name, value in blocks.items():
            pieces[name] = from_xor(value, ("z",), name[0]) if name[0] else value

    def hold(value, names):
        value, moved = lax.optimization_barrier((value, [pieces[name] for name in names]))
        pieces.update(zip(names, moved))
        return value

    feature_index = col * width_local + jnp.arange(width_local, dtype=jnp.int32)
    omega = sketch_table(sketch_base[0], feature_index, RANK)
    z = lax.dot_general(
        omega, states, (((0,), (1,)), ((), ())), preferred_element_type=jnp.float32
    )
    z = z.reshape(RANK, n_col, chunk).transpose(1, 0, 2)
    z_bits = bits(n_z)[::-1]
    far = z_bits[0]
    move({(offset, 0): block(offset) for offset in [0, far, *range(1, far)]})
    first = list(pieces)
    late = {(o, part): block(o, part, 2) for o in range(far + 1, n_z) for part in range(2)}
    z = jnp.concatenate([z, from_xor(z, ("z",), far)])
    z, late = lax.optimization_barrier((z, late))
    move(late)
    for bit in bits(n_col):
        z = z + from_xor(z, ("col",), bit)
    z = hold(z, first)
    for bit in z_bits[1:]:
        z = jnp.concatenate([z, from_xor(z, ("z",), bit)])
    z = hold(z, [(offset, 0) for offset in range(far + 1, n_z)])
    z = z, from_xor(z, ("core",), 1)
    absolute_col = [("col", bit, False) for bit in bits(n_col)[::-1]]
    at_first = chunk_places([("z", bit, True) for bit in z_bits[::-1]] + absolute_col)
    digits = [("col", bit, True) for bit in bits(n_col)[::-1]]
    digits += [("z", 1, True)] if n_z > 2 else []
    at = chunk_places(digits + [("z", bit, False) for bit in far_bits()])
    late = list(late)
    others = {name: from_xor(pieces[name], ("core",), 1) for name in first}

    f32 = jnp.float32
    square = jax.ShapeDtypeStruct((RANK, RANK), f32)
    wide = jax.ShapeDtypeStruct((RANK, rows_total), jnp.bfloat16)
    slab = jax.ShapeDtypeStruct((rows_total, cols), states.dtype)
    parts = jax.ShapeDtypeStruct((chunks, RANK, chunk), f32)
    loadings = jax.ShapeDtypeStruct((RANK, cols // n_core), f32)
    orth_flops = 8 * 64 * 64 * rows_total * 6
    flops = orth_flops + 4 * 64 * rows_total * cols

    basis, upper = call(orth_kernel, (wide, square), orth_flops, (at_first,), *z)
    basis = hold(basis, late)
    others.update((name, from_xor(pieces[name], ("core",), 1)) for name in late)
    blocks = [half[name] for half in (pieces, others) for name in sorted(half)]
    factor = upper.T * (1.0 / math.sqrt(rows_total * width_total))
    a, total = call(power_kernel, (slab, parts), flops, (at,), basis, *blocks)
    turned = jax.ShapeDtypeStruct((cols, rows_total // n_core), states.dtype)
    turned = call(turn_kernel, turned, flops, (), a)
    share, turned = lax.optimization_barrier((sum_parts(total, f32), turned))
    z = gather_parts(share)
    for step in range(POWER - 1):
        total = call(orth_power_kernel, parts, flops, (at,), *z, a, turned)
        z = gather_parts(sum_parts(total, jnp.bfloat16))
    core = lax.axis_index("core")[None].astype(jnp.int32)
    return call(last_kernel, loadings, flops, (at, core), *z, a).T, factor


def local_gram(basis):
    return jnp.dot(basis.T, basis, precision=lax.Precision.HIGHEST)


def orthonormal_block(sketch):
    whole_gram = lax.psum(local_gram(sketch), "row")
    identity = jnp.eye(RANK, dtype=jnp.float32)
    lower = jnp.linalg.cholesky(whole_gram + shift_ratio * jnp.trace(whole_gram) * identity)
    first = jax.scipy.linalg.solve_triangular(lower, sketch.T, lower=True).T
    lower_two = jnp.linalg.cholesky(lax.psum(local_gram(first), "row"))
    return jax.scipy.linalg.solve_triangular(lower_two, first.T, lower=True).T, lower


def per_device_slabs(sketch_base, states):
    width_local = states.shape[1]
    rows_total = states.shape[0] * lax.axis_size("row")
    width_total = width_local * lax.axis_size("col")
    feature_index = lax.axis_index("col") * width_local + jnp.arange(width_local, dtype=jnp.int32)
    omega = sketch_table(sketch_base[0], feature_index, RANK)

    def row_basis(right):
        partial_sketch = jnp.dot(states, right, preferred_element_type=jnp.float32)
        basis_new, lower = orthonormal_block(lax.psum(partial_sketch, "col"))
        return basis_new.astype(jnp.bfloat16), lower

    def back(basis):
        return lax.dot_general(
            states, basis, (((0,), (0,)), ((), ())), preferred_element_type=jnp.float32
        )

    basis, first_lower = row_basis(omega)
    factor = first_lower * (1.0 / math.sqrt(rows_total * width_total))
    for step in range(POWER):
        basis, unused = row_basis(lax.psum(back(basis), "row").astype(jnp.bfloat16))
    return lax.psum_scatter(back(basis), "row", scatter_dimension=0, tiled=True), factor


def solution(mesh):
    n_grp, n_row, n_col = (mesh.shape[name] for name in ("grp", "row", "col"))
    fits = n_row >= 4 and n_row & (n_row - 1) == 0 and n_col & (n_col - 1) == 0

    def run(sketch_base, states):
        rows_local = states.shape[0] // (n_grp * n_row)
        width_local = states.shape[1] // n_col
        tiled = rows_local % (n_col * LANES) == 0 and width_local % (n_row * LANES) == 0
        if fits and tiled:
            split = mesh.devices.reshape(n_grp, n_row // 2, 2, n_col)
            inner = jax.sharding.Mesh(split, ("grp", "z", "core", "col"))
            row, step = ("z", "core"), per_device_transposed
        else:
            inner, row, step = mesh, ("row",), per_device_slabs
        return jax.shard_map(
            step,
            mesh=inner,
            in_specs=(P("grp"), P(("grp",) + row, "col")),
            out_specs=(P(("col",) + row, "grp"), P("grp", None)),
            check_vma=False,
        )(sketch_base, states)

    return run
```

```python
import functools
import math

import jax
import jax.numpy as jnp
from jax import lax
from jax.experimental import pallas as pl
from jax.experimental.pallas import tpu as pltpu
from jax.sharding import PartitionSpec as P

RANK = 64
POWER = 4
LANES = 128
SUB = 8
TILE = 256
ROW_TILE = 512


shift_ratio = 0.005


def scramble(value):
    value = value ^ jnp.right_shift(value, 16) & 65535
    value = value * 73244475
    value = value ^ jnp.right_shift(value, 16) & 65535
    value = value * 73244475
    value = value ^ jnp.right_shift(value, 16) & 65535
    return value


def sketch_table(base_value, feature_index, rank):
    counter = feature_index[:, None] * rank + jnp.arange(rank, dtype=jnp.int32)[None, :]
    offset = scramble(base_value)
    total = jnp.zeros(counter.shape, jnp.float32)
    for j in range(4):
        hashed = scramble(counter * 4 + j + offset)
        total = total + (hashed & 16777215).astype(jnp.float32) * (1.0 / 16777216.0)
    return ((total - 2.0) * 1.7320508).astype(jnp.bfloat16)


def terms_of(value):
    if value.dtype == jnp.bfloat16:
        return [value]
    high = value.astype(jnp.bfloat16)
    rest = value - high.astype(jnp.float32)
    middle = rest.astype(jnp.bfloat16)
    low = (rest - middle.astype(jnp.float32)).astype(jnp.bfloat16)
    return [high, middle, low]


def dot_nn(left, right):
    return lax.dot_general(
        left, right, (((1,), (0,)), ((), ())), preferred_element_type=jnp.float32
    )


def dot_nt(left, right):
    return lax.dot_general(
        left, right, (((1,), (1,)), ((), ())), preferred_element_type=jnp.float32
    )


def small_times_wide(small, right):
    left = terms_of(small)
    pairs = [(i, d - i) for d in (2, 1, 0) for i in range(d + 1)]
    pairs = [(i, j) for i, j in pairs if i < len(left) and j < len(right)]
    return dot_nn(
        jnp.concatenate([left[i] for i, unused in pairs], axis=1),
        jnp.concatenate([right[j] for unused, j in pairs], axis=0),
    )


def gram_of(terms):
    if len(terms) == 1:
        return dot_nt(terms[0], terms[0])
    stacked = jnp.concatenate(terms, axis=0)
    return fold_gram(dot_nt(stacked, stacked))


def fold_gram(both):
    rank = both.shape[0] // 3
    cross = both[rank : 2 * rank, :rank] + both[2 * rank :, :rank]
    return both[:rank, :rank] + ((cross + cross.T) + both[rank : 2 * rank, rank : 2 * rank])


def eliminate(matrix, beside=()):
    beside = list(beside)
    size = matrix.shape[0]
    blocks = size // SUB
    row_index = lax.broadcasted_iota(jnp.int32, (SUB, 2 * size), 0)
    square_row = lax.broadcasted_iota(jnp.int32, (SUB, size), 0)
    square_col = lax.broadcasted_iota(jnp.int32, (SUB, size), 1)
    work = []
    for i in range(blocks):
        unit = jnp.where(square_col == square_row + SUB * i, 1.0, 0.0).astype(jnp.float32)
        work.append(jnp.concatenate([matrix[SUB * i : SUB * (i + 1), :], unit], axis=1))

    def fill(register, k):
        return jnp.broadcast_to(register[k : k + 1, :], (SUB, 2 * size))

    rows = []
    for b in range(blocks):
        for unused in range(-(-len(beside) // (blocks - b))):
            beside.pop(0)()
        columns = [
            {
                i: jnp.broadcast_to(work[i][:, SUB * b + j : SUB * b + j + 1], (SUB, 2 * size))
                for i in range(b, blocks)
            }
            for j in range(SUB)
        ]
        pivots = jnp.ones((SUB, 2 * size), jnp.float32)
        for k in range(0, SUB, 2):
            col_0, col_1 = columns[k], columns[k + 1]
            a, h, d = fill(col_0[b], k), fill(col_1[b], k), fill(col_1[b], k + 1)
            det = a * d - h * h
            over_det, over_a = 1.0 / det, 1.0 / a
            below_0 = jnp.where(row_index > k + 1, col_0[b], 0.0)
            below_1 = jnp.where(row_index > k + 1, col_1[b], 0.0)
            for j in range(k + 2, SUB):
                entry_0, entry_1 = fill(columns[j][b], k), fill(columns[j][b], k + 1)
                up_0 = d * entry_0 - h * entry_1
                up_1 = a * entry_1 - h * entry_0
                columns[j][b] = columns[j][b] - over_det * (below_0 * up_0 + below_1 * up_1)
                up_0, up_1 = over_det * up_0, over_det * up_1
                for i in range(b + 1, blocks):
                    columns[j][i] = columns[j][i] - (col_0[i] * up_0 + col_1[i] * up_1)
            row_0, row_1 = fill(work[b], k), fill(work[b], k + 1)
            up_0 = over_det * (d * row_0 - h * row_1)
            up_1 = over_det * (a * row_1 - h * row_0)
            for i in range(b + 1, blocks):
                work[i] = work[i] - (col_0[i] * up_0 + col_1[i] * up_1)
            second = jnp.where(row_index == k + 1, h * over_a, 0.0)
            work[b] = work[b] - (below_0 * up_0 + below_1 * up_1 + second * row_0)
            pivots = jnp.where(row_index == k, a, pivots)
            pivots = jnp.where(row_index == k + 1, det * over_a, pivots)
        rows.append(work[b] * lax.rsqrt(pivots))
    both = jnp.concatenate(rows, axis=0)
    keep = lax.broadcasted_iota(jnp.int32, (size, size), 1) >= lax.broadcasted_iota(
        jnp.int32, (size, size), 0
    )
    return jnp.where(keep, both[:, :size], 0.0), both[:, size:]


def shifted_factor(wide, terms):
    whole_gram = gram_of(terms)
    squares = wide.astype(jnp.float32)
    squares = jnp.sum(squares * squares, axis=0, keepdims=True)
    trace = jnp.sum(squares, axis=1, keepdims=True)
    size = whole_gram.shape[0]
    diagonal = lax.broadcasted_iota(jnp.int32, (size, size), 0) == lax.broadcasted_iota(
        jnp.int32, (size, size), 1
    )
    scaled = whole_gram * (1.0 / trace)
    upper, inverse = eliminate(jnp.where(diagonal, scaled + shift_ratio, scaled))
    root = jnp.sqrt(trace)
    return upper * root, inverse * (1.0 / root)


def wide_of(at_ref, z_refs):
    chunks = [z_ref[at_ref[i]] for z_ref in z_refs for i in range(at_ref.shape[0])]
    return jnp.concatenate(chunks, axis=1)


def first_pass(at_ref, z_refs):
    wide = wide_of(at_ref, z_refs)
    terms = terms_of(wide)
    upper, inverse_one = shifted_factor(wide, terms)
    rows = ROW_TILE if len(terms) == 1 else wide.shape[1]
    tiles, both = [], 0.0
    for start in range(0, wide.shape[1], rows):
        part = small_times_wide(inverse_one, [term[:, start : start + rows] for term in terms])
        tiles.append(jnp.concatenate(terms_of(part), axis=0))
        both = both + dot_nt(tiles[-1], tiles[-1])
    return jnp.concatenate(tiles, axis=1), fold_gram(both), upper


def back_product(at_ref, z_refs, a):
    stacked, gram, unused = first_pass(at_ref, z_refs)
    rank = gram.shape[0]
    tiles = []

    def tile(start):
        back = dot_nn(stacked, a[:, start : start + TILE])
        tiles.append(back[:rank] + (back[rank : 2 * rank] + back[2 * rank :]))

    starts = range(0, a.shape[1], TILE)
    work = [functools.partial(tile, start) for start in starts]
    unused, inverse_two = eliminate(gram, work)
    return small_times_wide(inverse_two, terms_of(jnp.concatenate(tiles, axis=1)))


def store_parts(forth, at_ref, part_ref):
    chunks, unused, width = part_ref.shape
    for i in range(chunks):
        part_ref[at_ref[i]] = forth[:, width * i : width * (i + 1)]


def orth_kernel(at_ref, z_ref, other_ref, basis_ref, upper_ref):
    stacked, gram, upper = first_pass(at_ref, (z_ref, other_ref))
    unused, inverse_two = eliminate(gram)
    rank = gram.shape[0]
    terms = [stacked[rank * i : rank * (i + 1)] for i in range(3)]
    basis_ref[...] = small_times_wide(inverse_two, terms).astype(jnp.bfloat16)
    upper_ref[...] = upper


def power_kernel(at_ref, basis_ref, *refs):
    piece_refs, a_ref, part_ref = refs[:-2], refs[-2], refs[-1]
    start = 0
    for piece_ref in piece_refs:
        a_ref[start : start + piece_ref.shape[0], :] = piece_ref[...]
        start += piece_ref.shape[0]
    weights = dot_nn(basis_ref[...], a_ref[...]).astype(jnp.bfloat16)
    forth = dot_nt(weights, a_ref[: part_ref.shape[0] * part_ref.shape[2], :])
    store_parts(forth, at_ref, part_ref)


def turn_kernel(a_ref, turned_ref):
    turned_ref[...] = a_ref[: turned_ref.shape[1], :].T


def orth_power_kernel(at_ref, z_ref, other_ref, a_ref, turned_ref, part_ref):
    weights = back_product(at_ref, (z_ref, other_ref), a_ref[...]).astype(jnp.bfloat16)
    store_parts(dot_nn(weights, turned_ref[...]), at_ref, part_ref)


def last_kernel(at_ref, core_ref, z_ref, other_ref, a_ref, out_ref):
    cols = out_ref.shape[1]
    start = pl.multiple_of(core_ref[0] * cols, cols)
    out_ref[...] = back_product(at_ref, (z_ref, other_ref), a_ref[:, pl.ds(start, cols)])


def call(kernel, out_shapes, flops, scalars, *operands):
    moved = sum(x.size * x.dtype.itemsize for x in operands)
    return pl.pallas_call(
        kernel,
        out_shape=out_shapes,
        in_specs=[pl.BlockSpec(memory_space=pltpu.SMEM)] * len(scalars)
        + [pl.BlockSpec(memory_space=pltpu.VMEM)] * len(operands),
        out_specs=jax.tree.map(lambda _: pl.BlockSpec(memory_space=pltpu.VMEM), out_shapes),
        compiler_params=pltpu.CompilerParams(vmem_limit_bytes=20 * 1024 * 1024),
        cost_estimate=pl.CostEstimate(flops=flops, bytes_accessed=moved, transcendentals=0),
    )(*scalars, *operands)


def bits(size):
    return [1 << k for k in range(size.bit_length() - 1)]


def from_xor(value, axis, offset):
    size = math.prod(lax.axis_size(name) for name in axis)
    return lax.ppermute(value, axis, [(i, i ^ offset) for i in range(size)])


def square_devices():
    n_z, n_col = lax.axis_size("z"), lax.axis_size("col")
    sides = [(z, col) for z in range(2 if n_z > 2 else 1) for col in range(n_col)]
    return [(z * n_col + col, col * (2 if n_z > 2 else 1) + z) for z, col in sides[:0:-1]]


def sum_parts(total, dtype):
    offsets = square_devices()
    step = total.shape[0] // (len(offsets) + 1)
    others = [
        from_xor(total[step * place : step * (place + 1)].astype(dtype), ("z", "col"), offset)
        for offset, place in offsets
    ]
    total = functools.reduce(jnp.add, [x.astype(jnp.float32) for x in others], total[:step])
    for bit in far_bits():
        mine = total.astype(dtype)
        total = mine.astype(jnp.float32) + from_xor(mine, ("z",), bit).astype(jnp.float32)
    return total.astype(dtype)


def gather_parts(own):
    placed = {0: own}
    for offset, place in square_devices():
        placed[place] = from_xor(own, ("z", "col"), offset)
    own = jnp.concatenate([placed[place] for place in sorted(placed)])
    return own, from_xor(own, ("core",), 1)


def far_bits():
    return bits(lax.axis_size("z"))[1 if lax.axis_size("z") > 2 else 0 :]


def chunk_places(digits):
    n_z, n_col = lax.axis_size("z"), lax.axis_size("col")
    index = jnp.arange(n_z * n_col, dtype=jnp.int32)
    z_at, col_at = lax.axis_index("z"), lax.axis_index("col")
    column = index % n_col
    relative = {"z": index // n_col, "col": column ^ col_at}
    absolute = {"z": relative["z"] ^ z_at, "col": column}
    place = jnp.zeros_like(index)
    for axis, bit, is_relative in digits:
        place = place * 2 + ((relative if is_relative else absolute)[axis] // bit) % 2
    return place.astype(jnp.int32)


def per_device_transposed(sketch_base, states):
    n_z, n_core, n_col = lax.axis_size("z"), lax.axis_size("core"), lax.axis_size("col")
    n_row = n_z * n_core
    rows_local, width_local = states.shape
    rows_total, width_total = rows_local * n_row, width_local * n_col
    chunk = rows_local // n_col
    cols = width_local // n_z
    chunks = n_z * n_col
    z_at, col = lax.axis_index("z"), lax.axis_index("col")
    pieces = {}

    def block(offset, part=0, parts=1):
        rows = rows_local // parts
        start = (part * rows, (z_at ^ offset) * cols)
        return lax.dynamic_slice(states, start, (rows, cols))

    def move(blocks):
        for name, value in blocks.items():
            pieces[name] = from_xor(value, ("z",), name[0]) if name[0] else value

    def hold(value, names):
        value, moved = lax.optimization_barrier((value, [pieces[name] for name in names]))
        pieces.update(zip(names, moved))
        return value

    feature_index = col * width_local + jnp.arange(width_local, dtype=jnp.int32)
    omega = sketch_table(sketch_base[0], feature_index, RANK)
    z = lax.dot_general(
        omega, states, (((0,), (1,)), ((), ())), preferred_element_type=jnp.float32
    )
    z = z.reshape(RANK, n_col, chunk).transpose(1, 0, 2)
    z_bits = bits(n_z)[::-1]
    far = z_bits[0]
    move({(offset, 0): block(offset) for offset in [0, far, *range(1, far)]})
    first = list(pieces)
    late = {(o, part): block(o, part, 2) for o in range(far + 1, n_z) for part in range(2)}
    z = jnp.concatenate([z, from_xor(z, ("z",), far)])
    z, late = lax.optimization_barrier((z, late))
    move(late)
    for bit in bits(n_col):
        z = z + from_xor(z, ("col",), bit)
    z = hold(z, first)
    for bit in z_bits[1:]:
        z = jnp.concatenate([z, from_xor(z, ("z",), bit)])
    z = hold(z, [(offset, 0) for offset in range(far + 1, n_z)])
    z = z, from_xor(z, ("core",), 1)
    absolute_col = [("col", bit, False) for bit in bits(n_col)[::-1]]
    at_first = chunk_places([("z", bit, True) for bit in z_bits[::-1]] + absolute_col)
    digits = [("col", bit, True) for bit in bits(n_col)[::-1]]
    digits += [("z", 1, True)] if n_z > 2 else []
    at = chunk_places(digits + [("z", bit, False) for bit in far_bits()])
    late = list(late)
    others = {name: from_xor(pieces[name], ("core",), 1) for name in first}

    f32 = jnp.float32
    square = jax.ShapeDtypeStruct((RANK, RANK), f32)
    wide = jax.ShapeDtypeStruct((RANK, rows_total), jnp.bfloat16)
    slab = jax.ShapeDtypeStruct((rows_total, cols), states.dtype)
    parts = jax.ShapeDtypeStruct((chunks, RANK, chunk), f32)
    loadings = jax.ShapeDtypeStruct((RANK, cols // n_core), f32)
    orth_flops = 8 * 64 * 64 * rows_total * 6
    flops = orth_flops + 4 * 64 * rows_total * cols

    basis, upper = call(orth_kernel, (wide, square), orth_flops, (at_first,), *z)
    basis = hold(basis, late)
    others.update((name, from_xor(pieces[name], ("core",), 1)) for name in late)
    blocks = [half[name] for half in (pieces, others) for name in sorted(half)]
    factor = upper.T * (1.0 / math.sqrt(rows_total * width_total))
    a, total = call(power_kernel, (slab, parts), flops, (at,), basis, *blocks)
    turned = jax.ShapeDtypeStruct((cols, rows_total // n_core), states.dtype)
    turned = call(turn_kernel, turned, flops, (), a)
    share, turned = lax.optimization_barrier((sum_parts(total, f32), turned))
    z = gather_parts(share)
    for step in range(POWER - 1):
        total = call(orth_power_kernel, parts, flops, (at,), *z, a, turned)
        z = gather_parts(sum_parts(total, jnp.bfloat16))
    core = lax.axis_index("core")[None].astype(jnp.int32)
    return call(last_kernel, loadings, flops, (at, core), *z, a).T, factor


def local_gram(basis):
    return jnp.dot(basis.T, basis, precision=lax.Precision.HIGHEST)


def orthonormal_block(sketch):
    whole_gram = lax.psum(local_gram(sketch), "row")
    identity = jnp.eye(RANK, dtype=jnp.float32)
    lower = jnp.linalg.cholesky(whole_gram + shift_ratio * jnp.trace(whole_gram) * identity)
    first = jax.scipy.linalg.solve_triangular(lower, sketch.T, lower=True).T
    lower_two = jnp.linalg.cholesky(lax.psum(local_gram(first), "row"))
    return jax.scipy.linalg.solve_triangular(lower_two, first.T, lower=True).T, lower


def per_device_slabs(sketch_base, states):
    width_local = states.shape[1]
    rows_total = states.shape[0] * lax.axis_size("row")
    width_total = width_local * lax.axis_size("col")
    feature_index = lax.axis_index("col") * width_local + jnp.arange(width_local, dtype=jnp.int32)
    omega = sketch_table(sketch_base[0], feature_index, RANK)

    def row_basis(right):
        partial_sketch = jnp.dot(states, right, preferred_element_type=jnp.float32)
        basis_new, lower = orthonormal_block(lax.psum(partial_sketch, "col"))
        return basis_new.astype(jnp.bfloat16), lower

    def back(basis):
        return lax.dot_general(
            states, basis, (((0,), (0,)), ((), ())), preferred_element_type=jnp.float32
        )

    basis, first_lower = row_basis(omega)
    factor = first_lower * (1.0 / math.sqrt(rows_total * width_total))
    for step in range(POWER):
        basis, unused = row_basis(lax.psum(back(basis), "row").astype(jnp.bfloat16))
    return lax.psum_scatter(back(basis), "row", scatter_dimension=0, tiled=True), factor


def solution(mesh):
    n_grp, n_row, n_col = (mesh.shape[name] for name in ("grp", "row", "col"))
    fits = n_row >= 4 and n_row & (n_row - 1) == 0 and n_col & (n_col - 1) == 0

    def run(sketch_base, states):
        rows_local = states.shape[0] // (n_grp * n_row)
        width_local = states.shape[1] // n_col
        tiled = rows_local % (n_col * LANES) == 0 and width_local % (n_row * LANES) == 0
        if fits and tiled:
            split = mesh.devices.reshape(n_grp, n_row // 2, 2, n_col)
            inner = jax.sharding.Mesh(split, ("grp", "z", "core", "col"))
            row, step = ("z", "core"), per_device_transposed
        else:
            inner, row, step = mesh, ("row",), per_device_slabs
        return jax.shard_map(
            step,
            mesh=inner,
            in_specs=(P("grp"), P(("grp",) + row, "col")),
            out_specs=(P(("col",) + row, "grp"), P("grp", None)),
            check_vma=False,
        )(sketch_base, states)

    return run
```
